128 devices in a mesh: ctx: 8 (over z_lo, y), fsdp: 4 (over x), head: 4 (over z_hi, core).
Axes of the slice: x: 4, y: 4, z: 4 (z_hi: 2, z_lo: 2; z = z_hi * 2 + z_lo), core: 2. Of those that a mesh axis runs over, the one named last changes fastest.
Arguments:
- tokens: bfloat16 [4, 1024, 1024], P('fsdp', 'ctx'), may hold values from -6 to 6
- positions: int32 [4, 1024], P('fsdp'), may hold values from 0 to 1023, as said below
- attn_gain: float32 [1024], replicated, may hold values from 0.5 to 1.5
- ffn_gain: float32 [1024], replicated, may hold values from 0.5 to 1.5
- query_gain: float32 [64], replicated, may hold values from 0.5 to 1.5
- key_gain: float32 [64], replicated, may hold values from 0.5 to 1.5
- w_query: bfloat16 [1024, 1024], P(('ctx', 'fsdp'), 'head'), may hold values from -0.1875 to 0.1875
- w_key: bfloat16 [1024, 512], P(('ctx', 'fsdp'), 'head'), may hold values from -0.1875 to 0.1875
- w_value: bfloat16 [1024, 512], P(('ctx', 'fsdp'), 'head'), may hold values from -0.1875 to 0.1875
- w_out: bfloat16 [1024, 1024], P(('ctx', 'fsdp'), 'head'), may hold values from -1.5 to 1.5
- w_gate: bfloat16 [1024, 4608], P(('ctx', 'fsdp'), 'head'), may hold values from -0.1875 to 0.1875
- w_up: bfloat16 [1024, 4608], P(('ctx', 'fsdp'), 'head'), may hold values from -0.1875 to 0.1875
- w_down: bfloat16 [1024, 4608], P(('ctx', 'fsdp'), 'head'), may hold values from -0.09375 to 0.09375
- cotangent: bfloat16 [4, 1024, 1024], P('fsdp', 'ctx'), may hold values from -6 to 6
Outputs:
- block_out: bfloat16 [4, 1024, 1024], P('fsdp', 'ctx')
- tokens_grad: bfloat16 [4, 1024, 1024], P('fsdp', 'ctx')
- attn_gain_grad: float32 [1024], replicated
- ffn_gain_grad: float32 [1024], replicated
- query_gain_grad: float32 [64], replicated
- key_gain_grad: float32 [64], replicated
- w_query_grad: float32 [1024, 1024], P(('ctx', 'fsdp'), 'head')
- w_key_grad: float32 [1024, 512], P(('ctx', 'fsdp'), 'head')
- w_value_grad: float32 [1024, 512], P(('ctx', 'fsdp'), 'head')
- w_out_grad: float32 [1024, 1024], P(('ctx', 'fsdp'), 'head')
- w_gate_grad: float32 [1024, 4608], P(('ctx', 'fsdp'), 'head')
- w_up_grad: float32 [1024, 4608], P(('ctx', 'fsdp'), 'head')
- w_down_grad: float32 [1024, 4608], P(('ctx', 'fsdp'), 'head')
The draws below stay inside these ranges and needn't reach their ends.
Inputs may be any that keep to these rules, and one draw needn't show every extreme that they name: Each row of positions names every position of its sequence once; it is made of 16 aligned blocks of 64 consecutive rising positions, in an order drawn for each sequence.
All inputs are finite; a program needn't handle non-finite values.
Results may differ from the reference program's by a relative error of at most 0.03.
Values may be sent and summed in bfloat16 or wider, within the bound.
No kernel may reach another device: no remote copies, remote signals or barrier semaphores. Data moves between devices by JAX's collectives and lax.ppermute only.
A program may use at most 64 MiB of HBM per device.

```python
import math
from functools import partial
import jax
import jax.numpy as jnp
from jax import lax

D = 1024
HEADS = 16
KV_HEADS = 8
HEAD_DIM = 64
FF = 4608
LENGTH = 1024
SEQS = 4
BLOCKS = 16
BLOCK = 64


def draw_positions(key, part):
    key = jax.random.fold_in(key, 7)
    seq_keys = jax.random.split(key, SEQS)
    block_order = jax.vmap(lambda one_key: jax.random.permutation(one_key, BLOCKS))(seq_keys)
    offsets = jnp.arange(BLOCK).astype(jnp.int32)
    places = block_order.astype(jnp.int32)[:, :, None] * BLOCK + offsets[None, None, :]
    return places.reshape(SEQS, LENGTH).astype(jnp.int32)


def block_levels(own_key, shape, cuts, low, high):
    factor_of = 1.0
    for dim, parts in cuts:
        steps = jax.random.uniform(jax.random.fold_in(jax.random.fold_in(own_key, 6), dim), (parts,), jnp.float32, low / len(cuts), high / len(cuts))
        factor_of = factor_of * jnp.repeat(jnp.exp(steps), shape[dim] // parts).reshape((-1,) + (1,) * (len(shape) - 1 - dim))
    return factor_of


def centred(key, extent, deviation, bound, shards=(), kind=jnp.bfloat16):
    array = jax.random.normal(key, extent, jnp.float32) * deviation
    if len(shards) > 0:
        array = block_levels(key, extent, shards, -0.22, 0.18) * array
    return jnp.clip(array, min=-bound, max=bound).astype(kind)


def setup_inputs(seed: int = 0) -> dict:
    seeds = jax.random.split(jax.random.key(seed), 15)
    return {
        "tokens": centred(seeds[0], (SEQS, LENGTH, D), 1.0, 6.0, ((0, 4), (1, 8))),
        "positions": draw_positions(jax.random.fold_in(seeds[14], 71), 0),
        "attn_gain": jnp.clip(1.0 + 0.1 * jax.random.normal(seeds[2], (D,), jnp.float32), 0.5, 1.5),
        "ffn_gain": jnp.clip(1.0 + 0.1 * jax.random.normal(seeds[3], (D,), jnp.float32), 0.5, 1.5),
        "query_gain": jnp.clip(1.0 + 0.1 * jax.random.normal(seeds[4], (HEAD_DIM,), jnp.float32), 0.5, 1.5),
        "key_gain": jnp.clip(1.0 + 0.1 * jax.random.normal(seeds[5], (HEAD_DIM,), jnp.float32), 0.5, 1.5),
        "w_query": centred(seeds[6], (D, HEADS * HEAD_DIM), D ** -0.5, 0.1875, ((0, 32), (1, 4))),
        "w_key": centred(seeds[7], (D, KV_HEADS * HEAD_DIM), D ** -0.5, 0.1875, ((0, 32), (1, 4))),
        "w_value": centred(seeds[8], (D, KV_HEADS * HEAD_DIM), D ** -0.5, 0.1875, ((0, 32), (1, 4))),
        "w_out": centred(seeds[9], (D, HEADS * HEAD_DIM), (HEADS * HEAD_DIM * 16 // LENGTH) ** -0.5, 1.5, ((0, 32), (1, 4))),
        "w_gate": centred(seeds[10], (D, FF), D ** -0.5, 0.1875, ((0, 32), (1, 4))),
        "w_up": centred(seeds[11], (D, FF), D ** -0.5, 0.1875, ((0, 32), (1, 4))),
        "w_down": centred(seeds[12], (D, FF), FF ** -0.5, 0.09375, ((0, 32), (1, 4))),
        "cotangent": centred(seeds[13], (SEQS, LENGTH, D), 1.0, 6.0, ((0, 4), (1, 8))),
    }


EPSILON = 1e-05
ROPE_BASE = 1000000.0
PRECISE = lax.Precision.HIGHEST

@jax.custom_vjp
def low(v):
    return lax.optimization_barrier(v.astype(jnp.bfloat16)).astype(jnp.float32)

@jax.custom_vjp
def low_back(v):
    return v

def low_keep(v):
    return (low(v), None)

def low_pass(kept, grad):
    return (grad,)

def back_keep(v):
    return (v, None)

def back_low(kept, grad):
    return (low(grad),)
low.defvjp(low_keep, low_pass)
low_back.defvjp(back_keep, back_low)

def matmul(left, right):
    return jnp.dot(left, right, precision=PRECISE, preferred_element_type=jnp.float32)

def rms_scale(values):
    return lax.rsqrt(lax.optimization_barrier(jnp.mean(values * values, axis=-1, keepdims=True)) + EPSILON)

def rope_tables(places, head_dim):
    half_dim = head_dim // 2
    frequency = ROPE_BASE ** (-(jnp.arange(half_dim).astype(jnp.float32) * 2.0 / head_dim))
    angles = places.astype(jnp.float32)[..., None] * frequency
    return (jnp.cos(angles), jnp.sin(angles))

def rotate(values, cosine_table, sine_table):
    half_dim = values.shape[-1] // 2
    lower_half = values[..., :half_dim]
    upper_half = values[..., half_dim:]
    cosine_b = cosine_table[..., None, :]
    sine_b = sine_table[..., None, :]
    return jnp.concatenate([lower_half * cosine_b - upper_half * sine_b, upper_half * cosine_b + lower_half * sine_b], axis=-1)

def head_norm(values, gain):
    return values * rms_scale(values) * gain

def attend_block(q_block, place_block, key_rows, value_rows, key_places):
    row_count = q_block.shape[0]
    grouped = q_block.reshape(row_count, KV_HEADS, HEADS // KV_HEADS, HEAD_DIM)
    scores = low_back(jnp.einsum('tkgd,skd->kgts', grouped, key_rows, precision=PRECISE) * HEAD_DIM ** (-0.5))
    visible = key_places[None, :] <= place_block[:, None]
    weights = jnp.where(visible, jnp.exp(scores), 0.0)
    row_total = lax.optimization_barrier(jnp.sum(weights, axis=-1))
    inner_sum = low_back(jnp.einsum('kgts,skd->tkgd', low(weights), value_rows, precision=PRECISE))
    result = inner_sum / jnp.transpose(row_total, (2, 0, 1))[..., None]
    return result.reshape(row_count, HEADS * HEAD_DIM)

def attend_sequence(queries, key_rows, value_rows, places):
    block_rows = math.gcd(LENGTH, 512)
    q_blocks = queries.reshape(LENGTH // block_rows, block_rows, HEADS, HEAD_DIM)
    place_blocks = places.reshape(LENGTH // block_rows, block_rows)
    one_block = jax.checkpoint(lambda pair_in: attend_block(pair_in[0], pair_in[1], key_rows, value_rows, places))
    return lax.map(one_block, (q_blocks, place_blocks)).reshape(LENGTH, HEADS * HEAD_DIM)

def forward(positions, tokens, attn_gain, ffn_gain, query_gain, key_gain, w_query, w_key, w_value, w_out, w_gate, w_up, w_down):
    flat_rows = tokens.reshape(SEQS * LENGTH, D)
    x_hat = flat_rows * rms_scale(flat_rows)
    normed = low(x_hat * attn_gain)
    queries = low_back(matmul(normed, w_query))
    key_proj = low_back(matmul(normed, w_key))
    value_proj = low_back(matmul(normed, w_value))
    cosine_table, sine_table = rope_tables(positions, HEAD_DIM)
    q_heads = low(rotate(head_norm(queries.reshape(SEQS, LENGTH, HEADS, HEAD_DIM), query_gain), cosine_table, sine_table))
    k_heads = low(rotate(head_norm(key_proj.reshape(SEQS, LENGTH, KV_HEADS, HEAD_DIM), key_gain), cosine_table, sine_table))
    v_heads = low(value_proj.reshape(SEQS, LENGTH, KV_HEADS, HEAD_DIM))
    mixed_heads = lax.map(lambda packed: attend_sequence(packed[0], packed[1], packed[2], packed[3]), (q_heads, k_heads, v_heads, positions))
    attn_low = low(mixed_heads.reshape(SEQS * LENGTH, HEADS * HEAD_DIM))
    attn_out = low_back(matmul(attn_low, w_out.T))
    hidden = flat_rows + attn_out
    h_hat = hidden * rms_scale(hidden)
    h_normed = low(h_hat * ffn_gain)
    gate_proj = low_back(matmul(h_normed, w_gate))
    upward = low_back(matmul(h_normed, w_up))
    active = low(jax.nn.silu(gate_proj) * upward)
    branch = low_back(matmul(active, w_down.T))
    return (hidden + branch).reshape(SEQS, LENGTH, D)

def reference(tokens, positions, attn_gain, ffn_gain, query_gain, key_gain, w_query, w_key, w_value, w_out, w_gate, w_up, w_down, cotangent):
    result, pullback = jax.vjp(partial(forward, positions), tokens.astype(jnp.float32), attn_gain.astype(jnp.float32), ffn_gain.astype(jnp.float32), query_gain.astype(jnp.float32), key_gain.astype(jnp.float32), w_query.astype(jnp.float32), w_key.astype(jnp.float32), w_value.astype(jnp.float32), w_out.astype(jnp.float32), w_gate.astype(jnp.float32), w_up.astype(jnp.float32), w_down.astype(jnp.float32))
    grads = pullback(cotangent.astype(jnp.float32))
    return (result.astype(jnp.bfloat16), grads[0].astype(jnp.bfloat16), grads[1], grads[2], grads[3], grads[4], grads[5], grads[6], grads[7], grads[8], grads[9], grads[10], grads[11])
```

```python
import jax
import jax.numpy as jnp
from jax import lax
from jax.sharding import Mesh, PartitionSpec as P

HEAD_DIM = 64
EPSILON = 1e-05
ROPE_BASE = 1000000.0
AXES = ("zl", "y", "x", "zh", "c")
BF = jnp.bfloat16
F32 = jnp.float32


def rms_scale(values):
    return lax.rsqrt(jnp.mean(values * values, axis=-1, keepdims=True) + EPSILON)


def norm_grad(grad_norm, normal, scale_rows):
    return scale_rows * (grad_norm - normal * jnp.mean(grad_norm * normal, axis=-1, keepdims=True))


def rope_tables(places, head_dim):
    half_dim = head_dim // 2
    frequency = ROPE_BASE ** (-(jnp.arange(half_dim).astype(F32) * 2.0 / head_dim))
    angles = places.astype(F32)[..., None] * frequency
    return (jnp.cos(angles), jnp.sin(angles))


def rotate(values, cosine, sine):
    half = values.shape[-1] // 2
    low, high = values[..., :half], values[..., half:]
    cosine, sine = cosine[..., None, :], sine[..., None, :]
    return jnp.concatenate([low * cosine - high * sine, high * cosine + low * sine], axis=-1)


def rotate_back(values, cosine, sine):
    return rotate(values, cosine, -sine)


def dot(left, right):
    return jnp.dot(left, right, preferred_element_type=F32)


def left_product(left, right):
    return lax.dot_general(left, right, (((0,), (0,)), ((), ())), preferred_element_type=F32)


def right_product(left, right):
    return lax.dot_general(left, right, (((1,), (1,)), ((), ())), preferred_element_type=F32)


def swap(value, axes, size, mask):
    return lax.ppermute(value, axes, [(i, i ^ mask) for i in range(size)])


def fan(pieces, axes):
    return [swap(pieces[k], axes, 4, k) for k in (1, 2, 3)]


def spread(piece, axes):
    return jnp.stack([piece] + fan([piece] * 4, axes))


Z = ("zl", "zh")


def sum_scatter(partial):
    blocks = partial.reshape(4, 2, 32, partial.shape[-1])
    other = swap(blocks[:, 1].astype(BF), "c", 2, 1)
    pair = blocks[:, 0] + other.astype(F32)
    low = pair.astype(BF)
    total = pair[0]
    for got in fan([None] + [low[k] for k in (1, 2, 3)], Z):
        total = total + got.astype(F32)
    return total


def gather_rows(rows):
    column = spread(rows, Z)
    other = swap(column, "c", 2, 1)
    return jnp.stack([column, other], axis=1).reshape(256, rows.shape[-1])


def gather_head(rows, head):
    pair = jnp.stack([rows, swap(rows, "c", 2, 1)])
    quad = jnp.concatenate([pair, swap(pair, "zh", 2, 1)])
    return quad[head ^ jnp.arange(4)].reshape(128, rows.shape[-1])


def halves(parts, zl):
    low = jnp.concatenate([p[:, : p.shape[1] // 2] for p in parts], axis=1)
    high = jnp.concatenate([p[:, p.shape[1] // 2 :] for p in parts], axis=1)
    return jnp.where(zl == 0, low, high), jnp.where(zl == 0, high, low)


def in_order(own, other, zl, axis=0):
    return jnp.where(
        zl == 0, jnp.stack([own, other], axis=axis), jnp.stack([other, own], axis=axis)
    )


def local(
    tokens, positions, attn_gain, ffn_gain, query_gain, key_gain,
    w_query, w_key, w_value, w_out, w_gate, w_up, w_down, cotangent,
):
    zl, y, head = lax.axis_index("zl"), lax.axis_index("y"), lax.axis_index(("zh", "c"))
    scale = HEAD_DIM ** (-0.5)

    keep_a, send_a = halves([w_query, w_key, w_value, w_out], zl)
    keep_f, send_f = halves([w_gate, w_up, w_down], zl)
    got_a = swap(send_a, "zl", 2, 1)
    own_tokens = tokens[0].reshape(4, 32, 1024)[head ^ jnp.arange(4)].reshape(128, 1024)
    x_low = jnp.concatenate([own_tokens, swap(own_tokens, "zl", 2, 1)])
    got_f = swap(send_f, "zl", 2, 1)
    own_dy = cotangent[0].reshape(4, 32, 1024)[head ^ jnp.arange(4)].reshape(128, 1024)
    dy = jnp.concatenate([own_dy, swap(own_dy, "zl", 2, 1)])

    rows_f = in_order(keep_f, got_f, zl)
    full_f = lax.all_gather(rows_f, ("y", "x"), axis=0)
    full_f = jnp.transpose(full_f, (1, 0, 2, 3)).reshape(1024, -1)
    rows_a = in_order(keep_a, got_a, zl)
    full_a = lax.all_to_all(
        jnp.broadcast_to(rows_a[None], (16,) + rows_a.shape), ("y", "x"), 0, 0, tiled=True
    )
    full_a = jnp.transpose(full_a, (1, 0, 2, 3)).reshape(1024, -1)
    w_qkv, w_o = full_a[:, :256], full_a[:, 256:]
    gate_w, up_w, down_w = full_f[:, :576], full_f[:, 576:1152], full_f[:, 1152:]

    steps = jnp.array([dl * 16 + ky * 4 + d for ky in range(4) for dl in range(2) for d in range(4)])
    places = positions[0].reshape(32, 32)[steps ^ (zl * 16 + y * 4 + head)].reshape(1024)
    own_places = places[:256]

    x = x_low.astype(F32)
    x_scale = rms_scale(x)
    x_hat = x * x_scale
    normed = (x_hat * attn_gain).astype(BF)
    qkv = dot(normed, w_qkv)
    q = qkv[:, :128].reshape(256, 2, 64)
    k = qkv[:, 128:192].reshape(256, 1, 64)
    v = qkv[:, 192:].astype(BF)
    q_scale, k_scale = rms_scale(q), rms_scale(k)
    q_hat, k_hat = q * q_scale, k * k_scale
    cosine, sine = rope_tables(own_places, HEAD_DIM)
    qh = rotate(q_hat * query_gain, cosine, sine).astype(BF)
    kh = rotate(k_hat * key_gain, cosine, sine).astype(BF)
    kv = spread(jnp.concatenate([kh[:, 0], v], axis=1), "y").reshape(1024, 128)
    k_all, v_all = kv[:, :64], kv[:, 64:]
    visible = places[None, :] <= own_places[:, None]
    scores = jnp.einsum("tgd,sd->gts", qh, k_all, preferred_element_type=F32) * scale
    u = jnp.where(visible[None], jnp.exp(scores), 0.0)
    u_low = u.astype(BF)
    denom = jnp.sum(u, axis=-1).T[..., None]
    o = jnp.einsum("gts,sd->tgd", u_low, v_all, preferred_element_type=F32) / denom
    o_low = o.astype(BF).reshape(256, 128)

    own_x = x[:32]
    h = own_x + sum_scatter(right_product(o_low, w_o))
    h_scale = rms_scale(h)
    h_hat = h * h_scale
    hn = gather_rows((h_hat * ffn_gain).astype(BF))
    gate, up = dot(hn, gate_w), dot(hn, up_w)
    sig = jax.nn.sigmoid(gate)
    silu = gate * sig
    active = (silu * up).astype(BF)
    d_act = dot(dy, down_w)
    d_gate = (d_act * up * sig * (1.0 + gate * (1.0 - sig))).astype(BF)
    d_up = (d_act * silu).astype(BF)
    d_hn = right_product(d_gate, gate_w) + right_product(d_up, up_w)
    d_hn = sum_scatter(d_hn)

    branch = sum_scatter(right_product(active, down_w))
    block_out = gather_head((h + branch).astype(BF), head)[None]

    dw_f = jnp.concatenate(
        [left_product(hn, d_gate), left_product(hn, d_up), left_product(dy, active)], axis=1
    ).astype(BF)
    dw_f = jnp.transpose(dw_f.reshape(2, 16, 32, -1), (1, 0, 2, 3))
    dw_f = lax.psum_scatter(dw_f, ("y", "x"), scatter_dimension=0, tiled=True)[0]

    ffn_gain_part = jnp.sum(d_hn * h_hat, axis=0)
    dh = dy[:32].astype(F32) + norm_grad(d_hn * ffn_gain, h_hat, h_scale)
    d_attn = gather_rows(dh.astype(BF))
    d_o = dot(d_attn, w_o).reshape(256, 2, 64)
    d_inner = (d_o / denom).astype(BF)
    delta = (jnp.sum(d_o * o, axis=-1) / denom[..., 0]).T
    dp = jnp.einsum("tgd,sd->gts", d_inner, v_all, preferred_element_type=F32)
    ds = (u * (dp - delta[..., None])).astype(BF)
    d_kall = jnp.einsum("gts,tgd->sd", ds, qh, preferred_element_type=F32) * scale
    d_vall = jnp.einsum("gts,tgd->sd", u_low, d_inner, preferred_element_type=F32)
    d_kv = jnp.concatenate([d_kall, d_vall], axis=1).reshape(4, 256, 128)
    d_kv_low = d_kv.astype(BF)
    d_kv_sum = d_kv[0]
    for got in fan([d_kv_low[i] for i in range(4)], "y"):
        d_kv_sum = d_kv_sum + got.astype(F32)
    d_qh = jnp.einsum("gts,sd->tgd", ds, k_all, preferred_element_type=F32) * scale
    d_qn = rotate_back(d_qh, cosine, sine)
    d_kn = rotate_back(d_kv_sum[:, None, :64], cosine, sine)
    query_gain_part = jnp.sum(d_qn * q_hat, axis=(0, 1))
    key_gain_part = jnp.sum(d_kn * k_hat, axis=(0, 1))
    d_q = norm_grad(d_qn * query_gain, q_hat, q_scale).astype(BF).reshape(256, 128)
    d_k = norm_grad(d_kn * key_gain, k_hat, k_scale).astype(BF).reshape(256, 64)
    d_qkv = jnp.concatenate([d_q, d_k, d_kv_sum[:, 64:].astype(BF)], axis=1)
    d_xn_part = right_product(d_qkv, w_qkv)
    d_xn = sum_scatter(d_xn_part)

    dw_a = jnp.concatenate([left_product(normed, d_qkv), left_product(d_attn, o_low)], axis=1)
    dw_a = jnp.transpose(dw_a.astype(BF).reshape(2, 16, 32, -1), (1, 0, 2, 3))
    dw_a = lax.all_to_all(dw_a, ("y", "x"), 0, 0, tiled=True)
    dw_a = jnp.sum(dw_a.astype(F32), axis=0).astype(BF)

    def finish(total, widths):
        other = swap(jnp.where(zl == 0, total[1], total[0]), "zl", 2, 1)
        own = jnp.where(zl == 0, total[0], total[1])
        low, high = jnp.where(zl == 0, own, other), jnp.where(zl == 0, other, own)
        outs, at = [], 0
        for width in widths:
            pair = [low[:, at : at + width], high[:, at : at + width]]
            outs.append(jnp.concatenate(pair, axis=1).astype(F32))
            at += width
        return outs

    grad_wg, grad_wu, grad_wd = finish(dw_f, (576, 576, 576))
    grad_wq, grad_wk, grad_wv, grad_wo = finish(dw_a, (128, 64, 64, 128))

    own_hat = x_hat[:32]
    attn_gain_part = jnp.sum(d_xn * own_hat, axis=0)
    d_x = dh + norm_grad(d_xn * attn_gain, own_hat, x_scale[:32])
    tokens_grad = gather_head(d_x.astype(BF), head)[None]

    gains = jnp.concatenate([attn_gain_part, ffn_gain_part, query_gain_part, key_gain_part])
    gains = gains.reshape(17, 128)
    gains = gains + swap(gains, "c", 2, 1)
    for axes in (Z, "y", "x"):
        one, two, three = fan([gains] * 4, axes)
        gains = (gains + one) + (two + three)
    gains = gains.reshape(-1)
    return (
        block_out, tokens_grad, gains[:1024], gains[1024:2048], gains[2048:2112], gains[2112:],
        grad_wq, grad_wk, grad_wv, grad_wo, grad_wg, grad_wu, grad_wd,
    )


def solution(mesh):
    cube = Mesh(mesh.devices.reshape(2, 4, 4, 2, 2), AXES)
    rows = P("x", ("zl", "y"), None)
    weight = P(("zl", "y", "x"), ("zh", "c"))
    return jax.shard_map(
        local,
        mesh=cube,
        in_specs=(rows, P("x", None)) + (P(),) * 4 + (weight,) * 7 + (rows,),
        out_specs=(rows, rows) + (P(),) * 4 + (weight,) * 7,
        check_vma=False,
    )
```

```python
import functools

import jax
import jax.numpy as jnp
from jax import lax
from jax.experimental import pallas as pl
from jax.experimental.pallas import tpu as pltpu
from jax.sharding import Mesh, PartitionSpec as P

EPSILON = 1e-05
ROPE_BASE = 1000000.0
AXES = ("zl", "y", "x", "zh", "c")
Z = ("zl", "zh")
PLANE = ("zl", "y", "x")
BF = jnp.bfloat16
F32 = jnp.float32
SCALE = 64 ** (-0.5)
WHOLE = pl.BlockSpec(memory_space=pltpu.VMEM)


def call(body, outs, *operands):
    return pl.pallas_call(
        body,
        out_shape=[jax.ShapeDtypeStruct(shape, kind) for shape, kind in outs],
        in_specs=[WHOLE] * len(operands),
        out_specs=[WHOLE] * len(outs),
        compiler_params=pltpu.CompilerParams(vmem_limit_bytes=40 * 2**20),
    )(*operands)


def dot(left, right):
    return jnp.dot(left, right, preferred_element_type=F32)


def left_product(left, right):
    return lax.dot_general(left, right, (((0,), (0,)), ((), ())), preferred_element_type=F32)


def right_product(left, right):
    return lax.dot_general(left, right, (((1,), (1,)), ((), ())), preferred_element_type=F32)


def row_scale(values):
    return lax.rsqrt(jnp.mean(values * values, axis=-1, keepdims=True) + EPSILON)


def row_norm_grad(grad, normal, scale):
    return scale * (grad - normal * jnp.mean(grad * normal, axis=-1, keepdims=True))


def lanes(values):
    return lax.broadcasted_iota(jnp.int32, values.shape, 1)


def head_sum(values):
    low = lanes(values) < 64
    first = jnp.sum(jnp.where(low, values, 0.0), axis=-1, keepdims=True)
    second = jnp.sum(jnp.where(low, 0.0, values), axis=-1, keepdims=True)
    return jnp.where(low, first, second)


def head_scale(values):
    return lax.rsqrt(head_sum(values * values) * (1.0 / 64) + EPSILON)


def head_norm_grad(grad, normal, scale):
    return scale * (grad - normal * (head_sum(grad * normal) * (1.0 / 64)))


def other_half(values):
    low = (lanes(values) & 63) < 32
    return jnp.where(low, pltpu.roll(values, 96, 1), pltpu.roll(values, 32, 1))


def project(own, other, w, attn_gain, qk_gain, cosine, sine, normed, qh, kv, qkv):
    x = jnp.concatenate([own[...], other[...]]).astype(F32)
    low = (x * row_scale(x) * attn_gain[...]).astype(BF)
    normed[...] = low
    out = dot(low, w[:, :256])
    qkv[...] = out
    q, k = out[:, :128], out[:, 128:]
    cos, sin = cosine[...], sine[...]
    qn = q * head_scale(q) * qk_gain[0:1]
    qh[...] = (qn * cos + other_half(qn) * sin).astype(BF)
    kn = k * head_scale(k) * qk_gain[1:2]
    kr = kn * cos + other_half(kn) * sin
    kv[...] = jnp.where(lanes(k) < 64, kr, k).astype(BF)


def weights_of(q, k, visible):
    scores = right_product(q, k) * SCALE
    return jnp.where(visible, jnp.exp(scores), 0.0)


def attend(qh, kv0, kv1, kv2, kv3, own_places, places, w, send, keep, o_out, l_out):
    sums, totals = [0.0, 0.0], [0.0, 0.0]
    mine = own_places[...]
    for i, kv in enumerate((kv0, kv1, kv2, kv3)):
        visible = places[:, i * 256 : (i + 1) * 256] <= mine
        k, v = kv[:, :64], kv[:, 64:]
        for g in range(2):
            u = weights_of(qh[:, g * 64 : (g + 1) * 64], k, visible)
            totals[g] = totals[g] + jnp.sum(u, axis=-1, keepdims=True)
            sums[g] = sums[g] + dot(u.astype(BF), v)
    o = jnp.concatenate([sums[g] / totals[g] for g in range(2)], axis=1)
    o_out[...] = o
    l_out[...] = jnp.where(lanes(o) < 64, totals[0], totals[1])
    partial = right_product(o.astype(BF), w[:, 256:]).reshape(4, 2, 32, 1024)
    send[...] = partial[:, 1].astype(BF)
    keep[...] = partial[:, 0]


def pair_add(keep, got, own, one, two, three):
    own[...] = keep[0] + got[0].astype(F32)
    for k, out in ((1, one), (2, two), (3, three)):
        out[...] = (keep[k] + got[k].astype(F32)).astype(BF)


def total_of(own, one, two, three):
    return (own[...] + one[...].astype(F32)) + (two[...].astype(F32) + three[...].astype(F32))


def hidden(own, one, two, three, x, gain, h, hn):
    rows = x[:32].astype(F32) + total_of(own, one, two, three)
    h[...] = rows
    hn[...] = (rows * row_scale(rows) * gain[...]).astype(BF)


def feed_parts(gate, up, d_act):
    sig = jax.nn.sigmoid(gate)
    silu = gate * sig
    active = silu * up
    d_gate = d_act * up * sig * (1.0 + gate * (1.0 - sig))
    return active.astype(BF), d_gate, d_act * silu


def feed(p0, p1, p2, p3, p4, p5, p6, p7, dy_own, dy_other, w, send, keep, hn, act, dgu):
    rows = jnp.concatenate([p[...] for p in (p0, p1, p2, p3, p4, p5, p6, p7)])
    hn[...] = rows
    dy = jnp.concatenate([dy_own[...], dy_other[...]])
    def both(left, at, width):
        first, second = left[:, :512], left[:, 512:]
        return dot(first, w[:, 0, :, at : at + width].reshape(512, width)) + dot(
            second, w[:, 1, :, at : at + width].reshape(512, width)
        )
    gate, up, d_act = both(rows, 0, 512), both(rows, 512, 512), both(dy, 1024, 512)
    active, d_gate, d_up = feed_parts(gate, up, d_act)
    act[:, :512] = active
    d_gate, d_up = d_gate.astype(BF), d_up.astype(BF)
    dgu[:, :512] = d_gate
    dgu[:, 512:1024] = d_up
    tail, d_tail = both(rows, 1536, 128), both(dy, 1664, 128)
    low = lanes(tail) < 64
    gate = jnp.where(low, tail, 0.0)
    up = jnp.where(low, pltpu.roll(tail, 64, 1), 0.0)
    active, dg_tail, du_tail = feed_parts(gate, up, d_tail)
    act[:, 512:] = active
    dgu_tail = jnp.where(low, dg_tail, pltpu.roll(du_tail, 64, 1)).astype(BF)
    dgu[:, 1024:] = dgu_tail
    halves = []
    for z in range(2):
        part = right_product(d_gate, w[:, z, :, :512].reshape(512, 512))
        part = part + right_product(d_up, w[:, z, :, 512:1024].reshape(512, 512))
        part = part + right_product(dgu_tail, w[:, z, :, 1536:1664].reshape(512, 128))
        halves.append(part)
    partial = jnp.concatenate(halves, axis=1).reshape(4, 2, 32, 1024)
    send[...] = partial[:, 1].astype(BF)
    keep[...] = partial[:, 0]


def feed_weights(hn, dy_own, dy_other, act, dgu, w, send, keep, dw):
    dy = jnp.concatenate([dy_own[...], dy_other[...]])
    rows, active = hn[...], act[...]
    halves = []
    for z in range(2):
        part = right_product(active[:, :512], w[:, z, :, 1024:1536].reshape(512, 512))
        halves.append(part + right_product(active[:, 512:], w[:, z, :, 1664:].reshape(512, 128)))
    partial = jnp.concatenate(halves, axis=1).reshape(4, 2, 32, 1024)
    send[...] = partial[:, 1].astype(BF)
    keep[...] = partial[:, 0]
    for z in range(2):
        left, left_dy = rows[:, z * 512 : (z + 1) * 512], dy[:, z * 512 : (z + 1) * 512]
        def put(value, at, width):
            dw[:, z, :, at : at + width] = value.astype(BF).reshape(16, 32, width)
        put(left_product(left, dgu[:, :512]), 0, 512)
        put(left_product(left, dgu[:, 512:1024]), 512, 512)
        put(left_product(left_dy, active[:, :512]), 1024, 512)
        put(left_product(left, dgu[:, 1024:]), 1536, 128)
        put(left_product(left_dy, active[:, 512:]), 1664, 128)


def block_rows(own, one, two, three, h, out):
    out[...] = (h[...] + total_of(own, one, two, three)).astype(BF)


def hidden_grad(own, one, two, three, h, dy, gain, dh, low, gain_part):
    d_hn = total_of(own, one, two, three)
    rows = h[...]
    scale = row_scale(rows)
    hat = rows * scale
    gain_part[...] = jnp.sum(d_hn * hat, axis=0, keepdims=True)
    grad = dy[:32].astype(F32) + row_norm_grad(d_hn * gain[...], hat, scale)
    dh[...] = grad
    low[...] = grad.astype(BF)


def attend_grad(
    p0, p1, p2, p3, p4, p5, p6, p7, qh, kv0, kv1, kv2, kv3, own_places, places, w, o, l,
    d_attn, d_qh, d_kv0, d_kv1, d_kv2, d_kv3,
):
    rows = jnp.concatenate([p[...] for p in (p0, p1, p2, p3, p4, p5, p6, p7)])
    d_attn[...] = rows
    d_o = dot(rows, w[:, 256:])
    denom = l[...]
    d_inner = (d_o / denom).astype(BF)
    delta = head_sum(d_o * o[...]) / denom
    mine = own_places[...]
    d_q = [0.0, 0.0]
    for i, (kv, d_kv) in enumerate(((kv0, d_kv0), (kv1, d_kv1), (kv2, d_kv2), (kv3, d_kv3))):
        visible = places[:, i * 256 : (i + 1) * 256] <= mine
        k, v = kv[:, :64], kv[:, 64:]
        d_k, d_v = 0.0, 0.0
        for g in range(2):
            at = slice(g * 64, (g + 1) * 64)
            q, di = qh[:, at], d_inner[:, at]
            u = weights_of(q, k, visible)
            ds = (u * (right_product(di, v) - delta[:, g * 64 : g * 64 + 1])).astype(BF)
            d_q[g] = d_q[g] + dot(ds, k)
            d_k = d_k + left_product(ds, q)
            d_v = d_v + left_product(u.astype(BF), di)
        d_kv[...] = jnp.concatenate([d_k * SCALE, d_v], axis=1).astype(d_kv.dtype)
    d_qh[...] = jnp.concatenate(d_q, axis=1) * SCALE


def project_grad(
    d_qh, own, one, two, three, qkv, cosine, sine, qk_gain, w, x_own, x_other,
    d_qkv, send, keep, gain_part, head_part,
):
    d_kv = total_of(own, one, two, three)
    cos, sin = cosine[...], sine[...]
    q, k = qkv[:, :128], qkv[:, 128:]
    q_scale, k_scale = head_scale(q), head_scale(k)
    q_hat, k_hat = q * q_scale, k * k_scale
    d_q = d_qh[...]
    d_qn = d_q * cos - other_half(d_q) * sin
    d_kn = d_kv * cos - other_half(d_kv) * sin
    head_part[0:1] = jnp.sum(d_qn * q_hat, axis=0, keepdims=True)
    head_part[1:2] = jnp.sum(d_kn * k_hat, axis=0, keepdims=True)
    d_q = head_norm_grad(d_qn * qk_gain[0:1], q_hat, q_scale)
    d_k = head_norm_grad(d_kn * qk_gain[1:2], k_hat, k_scale)
    d_k = jnp.where(lanes(d_k) < 64, d_k, d_kv)
    low = jnp.concatenate([d_q, d_k], axis=1).astype(BF)
    d_qkv[...] = low
    partial = right_product(low, w[:, :256])
    x = jnp.concatenate([x_own[...], x_other[...]]).astype(F32)
    gain_part[...] = jnp.sum(partial * (x * row_scale(x)), axis=0, keepdims=True)
    partial = partial.reshape(4, 2, 32, 1024)
    send[...] = partial[:, 1].astype(BF)
    keep[...] = partial[:, 0]


def attend_weights(normed, d_qkv, dw):
    dw[...] = left_product(normed[...], d_qkv[...]).astype(BF)


def out_weights(d_attn, o, dw):
    dw[...] = left_product(d_attn[...], o[...].astype(BF)).astype(BF)


def token_rows(own, one, two, three, dh, x, gain, out):
    d_xn = total_of(own, one, two, three)
    rows = x[:32].astype(F32)
    scale = row_scale(rows)
    grad = row_norm_grad(d_xn * gain[...], rows * scale, scale)
    out[...] = (dh[...] + grad).astype(BF)


def finish_attend(parts, wq, wk, wv, wo):
    low = jnp.sum(parts[0].astype(F32), axis=0)
    high = jnp.sum(parts[1].astype(F32), axis=0)
    wq[...] = jnp.concatenate([low[:, :128], high[:, :128]], axis=1)
    wk[...] = jnp.concatenate([low[:, 128:192], high[:, 128:192]], axis=1)
    wv[...] = jnp.concatenate([low[:, 192:256], high[:, 192:256]], axis=1)
    wo[...] = jnp.concatenate([low[:, 256:], high[:, 256:]], axis=1)


def swap(value, axes, size, mask):
    return lax.ppermute(value, axes, [(i, i ^ mask) for i in range(size)])


def fan(pieces, axes):
    return [swap(pieces[k], axes, 4, k) for k in (1, 2, 3)]


def sum_scatter(send, keep):
    got = swap(send, "c", 2, 1)
    small = ((32, 1024), BF)
    own, one, two, three = call(pair_add, [((32, 1024), F32), small, small, small], keep, got)
    return [own] + fan([None, one, two, three], Z)


def gather_rows(rows):
    column = [rows] + fan([rows] * 4, Z)
    pieces = []
    for piece in column:
        pieces += [piece, swap(piece, "c", 2, 1)]
    return pieces


def place_rows(head, p0, p1, p2, p3, out):
    for k, piece in enumerate((p0, p1, p2, p3)):
        out[pl.ds((head[0] ^ k) * 32, 32)] = piece[...]


def gather_head(rows, head):
    other = swap(rows, "c", 2, 1)
    pieces = [rows, other, swap(rows, "zh", 2, 1), swap(other, "zh", 2, 1)]
    return pl.pallas_call(
        place_rows,
        out_shape=jax.ShapeDtypeStruct((128, 1024), BF),
        in_specs=[pl.BlockSpec(memory_space=pltpu.SMEM)] + [WHOLE] * 4,
        out_specs=WHOLE,
    )(head.reshape(1), *pieces)[None]


def column_half(parts, zl):
    return [
        jnp.where(zl == 0, p[:, : p.shape[1] // 2], p[:, p.shape[1] // 2 :]) for p in parts
    ]


def feed_columns(gate, up, down):
    zeros = jnp.zeros_like(gate[:, :64])
    parts = [gate[:, :512], up[:, :512], down[:, :512], gate[:, 512:], up[:, 512:], down[:, 512:]]
    return jnp.concatenate(parts + [zeros], axis=1)


def local(
    tokens, positions, attn_gain, ffn_gain, query_gain, key_gain,
    w_query, w_key, w_value, w_out, w_gate, w_up, w_down, cotangent,
):
    zl, y, head = lax.axis_index("zl"), lax.axis_index("y"), lax.axis_index(("zh", "c"))
    attn_gain_row, ffn_gain_row = attn_gain[None], ffn_gain[None]

    small = [w_query, w_key, w_value, w_out]
    lows = jnp.concatenate([p[:, : p.shape[1] // 2] for p in small], axis=1)
    highs = jnp.concatenate([p[:, p.shape[1] // 2 :] for p in small], axis=1)
    blocks = jnp.broadcast_to(jnp.stack([lows, highs])[:, None], (2, 16, 32, 384))
    w_a = lax.all_to_all(blocks.reshape(1024, 384), PLANE, 0, 0, tiled=True)

    feeds = [w_gate, w_up, w_down]
    keep_f = feed_columns(*column_half(feeds, zl))
    send_f = feed_columns(*column_half(feeds, 1 - zl))
    got_f = swap(send_f, "zl", 2, 1)
    rows_f = jnp.where(zl == 0, jnp.stack([keep_f, got_f]), jnp.stack([got_f, keep_f]))
    w_f = lax.all_gather(rows_f, ("y", "x"), axis=0)

    order = head ^ jnp.arange(4)
    x_own = tokens[0].reshape(4, 32, 1024)[order].reshape(128, 1024)
    x_other = swap(x_own, "zl", 2, 1)
    dy_own = cotangent[0].reshape(4, 32, 1024)[order].reshape(128, 1024)
    dy_other = swap(dy_own, "zl", 2, 1)

    steps = jnp.array([dl * 16 + ky * 4 + d for ky in range(4) for dl in range(2) for d in range(4)])
    places = positions[0].reshape(32, 32)[steps ^ (zl * 16 + y * 4 + head)].reshape(1024)
    own_places = places[:256]
    frequency = ROPE_BASE ** (-(jnp.arange(32).astype(F32) * 2.0 / 64))
    angles = own_places.astype(F32)[:, None] * frequency
    cosine, sine = jnp.cos(angles), jnp.sin(angles)
    cosine = jnp.concatenate([cosine] * 4, axis=1)
    sine = jnp.concatenate([-sine, sine] * 2, axis=1)
    own_places, places = own_places[:, None], places[None]
    qk_gain = jnp.stack([jnp.tile(query_gain, 2), jnp.tile(key_gain, 2)])

    halves = [((4, 32, 1024), BF), ((4, 32, 1024), F32)]
    flat = ((256, 128), BF)
    normed, qh, kv, qkv = call(
        project, [((256, 1024), BF), flat, flat, ((256, 256), F32)],
        x_own, x_other, w_a, attn_gain_row, qk_gain, cosine, sine,
    )
    kvs = [kv] + fan([kv] * 4, "y")
    send, keep, o, l = call(
        attend, halves + [((256, 128), F32)] * 2, qh, *kvs, own_places, places, w_a
    )
    h, hn = call(
        hidden, [((32, 1024), F32), ((32, 1024), BF)],
        *sum_scatter(send, keep), x_own, ffn_gain_row,
    )
    send, keep, hn_all, act, dgu = call(
        feed, halves + [((256, 1024), BF), ((256, 640), BF), ((256, 1152), BF)],
        *gather_rows(hn), dy_own, dy_other, w_f,
    )
    d_hn = sum_scatter(send, keep)
    send_b, keep_b, dw_f = call(
        feed_weights, halves + [((16, 2, 32, 1792), BF)], hn_all, dy_own, dy_other, act, dgu, w_f
    )
    (rows,) = call(block_rows, [((32, 1024), BF)], *sum_scatter(send_b, keep_b), h)
    block_out = gather_head(rows, head)
    dw_f = lax.psum_scatter(
        dw_f.reshape(1024, 1792), ("y", "x"), scatter_dimension=0, tiled=True
    ).reshape(2, 32, 1792)
    dh, d_low, ffn_gain_part = call(
        hidden_grad, [((32, 1024), F32), ((32, 1024), BF), ((1, 1024), F32)],
        *d_hn, h, dy_own, ffn_gain_row,
    )
    d_attn, d_qh, *d_kvs = call(
        attend_grad,
        [((256, 1024), BF), ((256, 128), F32), ((256, 128), F32), flat, flat, flat],
        *gather_rows(d_low), qh, *kvs, own_places, places, w_a, o, l,
    )
    d_qkv, send, keep, attn_gain_part, head_part = call(
        project_grad,
        [((256, 256), BF)] + halves + [((1, 1024), F32), ((2, 128), F32)],
        d_qh, d_kvs[0], *fan(d_kvs, "y"), qkv, cosine, sine, qk_gain, w_a, x_own, x_other,
    )
    d_xn = sum_scatter(send, keep)
    (dw_qkv,) = call(attend_weights, [((1024, 256), BF)], normed, d_qkv)
    (dw_o,) = call(out_weights, [((1024, 128), BF)], d_attn, o)
    dw_a = jnp.concatenate([dw_qkv, dw_o], axis=1)
    dw_a = lax.all_to_all(dw_a, PLANE, 0, 0, tiled=True)
    (rows,) = call(token_rows, [((32, 1024), BF)], *d_xn, dh, x_own, attn_gain_row)
    tokens_grad = gather_head(rows, head)
    grad_wq, grad_wk, grad_wv, grad_wo = call(
        finish_attend, [((32, n), F32) for n in (256, 128, 128, 256)],
        dw_a.reshape(2, 16, 32, 384),
    )

    def finish(total):
        other = swap(jnp.where(zl == 0, total[1], total[0]), "zl", 2, 1)
        own = jnp.where(zl == 0, total[0], total[1])
        low, high = jnp.where(zl == 0, own, other), jnp.where(zl == 0, other, own)
        outs = []
        for i in range(3):
            wide, tail = slice(i * 512, (i + 1) * 512), slice(1536 + i * 64, 1600 + i * 64)
            pieces = [low[:, wide], low[:, tail], high[:, wide], high[:, tail]]
            outs.append(jnp.concatenate(pieces, axis=1).astype(F32))
        return outs

    grad_wg, grad_wu, grad_wd = finish(dw_f)

    head_part = head_part[:, :64] + head_part[:, 64:] * jnp.array([[1.0], [0.0]], F32)
    gains = jnp.concatenate([attn_gain_part[0], ffn_gain_part[0], head_part.reshape(-1)])
    gains = gains.reshape(17, 128)
    gains = gains + swap(gains, "c", 2, 1)
    for axes in (Z, "y", "x"):
        one, two, three = fan([gains] * 4, axes)
        gains = (gains + one) + (two + three)
    gains = gains.reshape(-1)
    return (
        block_out, tokens_grad, gains[:1024], gains[1024:2048], gains[2048:2112], gains[2112:],
        grad_wq, grad_wk, grad_wv, grad_wo, grad_wg, grad_wu, grad_wd,
    )


def solution(mesh):
    cube = Mesh(mesh.devices.reshape(2, 4, 4, 2, 2), AXES)
    rows = P("x", ("zl", "y"), None)
    weight = P(("zl", "y", "x"), ("zh", "c"))
    return jax.shard_map(
        local,
        mesh=cube,
        in_specs=(rows, P("x", None)) + (P(),) * 4 + (weight,) * 7 + (rows,),
        out_specs=(rows, rows) + (P(),) * 4 + (weight,) * 7,
        check_vma=False,
    )
```

```python
import functools

import jax
import jax.numpy as jnp
from jax import lax
from jax.experimental import pallas as pl
from jax.experimental.pallas import tpu as pltpu
from jax.sharding import Mesh, PartitionSpec as P

EPSILON = 1e-05
ROPE_BASE = 1000000.0
AXES = ("zl", "y", "x", "zh", "c")
Z = ("zl", "zh")
PLANE = ("zl", "y", "x")
BF = jnp.bfloat16
F32 = jnp.float32
SCALE = 64 ** (-0.5)
WHOLE = pl.BlockSpec(memory_space=pltpu.VMEM)


def call(body, outs, *operands, room=12):
    return pl.pallas_call(
        body,
        out_shape=[jax.ShapeDtypeStruct(shape, kind) for shape, kind in outs],
        in_specs=[WHOLE] * len(operands),
        out_specs=[WHOLE] * len(outs),
        compiler_params=pltpu.CompilerParams(vmem_limit_bytes=room * 2**20),
    )(*operands)


def dot(left, right):
    return jnp.dot(left, right, preferred_element_type=F32)


def left_product(left, right):
    return lax.dot_general(left, right, (((0,), (0,)), ((), ())), preferred_element_type=F32)


def right_product(left, right):
    return lax.dot_general(left, right, (((1,), (1,)), ((), ())), preferred_element_type=F32)


def row_scale(values):
    return lax.rsqrt(jnp.mean(values * values, axis=-1, keepdims=True) + EPSILON)


def row_norm_grad(grad, normal, scale):
    return scale * (grad - normal * jnp.mean(grad * normal, axis=-1, keepdims=True))


def lanes(values):
    return lax.broadcasted_iota(jnp.int32, values.shape, 1)


def head_sum(values):
    low = lanes(values) < 64
    first = jnp.sum(jnp.where(low, values, 0.0), axis=-1, keepdims=True)
    second = jnp.sum(jnp.where(low, 0.0, values), axis=-1, keepdims=True)
    return jnp.where(low, first, second)


def head_scale(values):
    return lax.rsqrt(head_sum(values * values) * (1.0 / 64) + EPSILON)


def head_norm_grad(grad, normal, scale):
    return scale * (grad - normal * (head_sum(grad * normal) * (1.0 / 64)))


def other_half(values):
    low = (lanes(values) & 63) < 32
    return jnp.where(low, pltpu.roll(values, 96, 1), pltpu.roll(values, 32, 1))


def project(own, other, w, attn_gain, qk_gain, cosine, sine, normed, qh, kv, qkv):
    x = jnp.concatenate([own[...], other[...]]).astype(F32)
    low = (x * row_scale(x) * attn_gain[...]).astype(BF)
    normed[...] = low
    out = dot(low, w[:, :256])
    qkv[...] = out
    q, k = out[:, :128], out[:, 128:]
    cos, sin = cosine[...], sine[...]
    qn = q * head_scale(q) * qk_gain[0:1]
    qh[...] = (qn * cos + other_half(qn) * sin).astype(BF)
    kn = k * head_scale(k) * qk_gain[1:2]
    kr = kn * cos + other_half(kn) * sin
    kv[...] = jnp.where(lanes(k) < 64, kr, k).astype(BF)


def weights_of(q, k, visible):
    scores = right_product(q, k) * SCALE
    return jnp.where(visible, jnp.exp(scores), 0.0)


def attend(qh, kv0, kv1, kv2, kv3, own_places, places, w, send, keep, o_out, l_out):
    sums, totals = [0.0, 0.0], [0.0, 0.0]
    mine = own_places[...]
    for i, kv in enumerate((kv0, kv1, kv2, kv3)):
        visible = places[:, i * 256 : (i + 1) * 256] <= mine
        k, v = kv[:, :64], kv[:, 64:]
        for g in range(2):
            u = weights_of(qh[:, g * 64 : (g + 1) * 64], k, visible)
            totals[g] = totals[g] + jnp.sum(u, axis=-1, keepdims=True)
            sums[g] = sums[g] + dot(u.astype(BF), v)
    o = jnp.concatenate([sums[g] / totals[g] for g in range(2)], axis=1)
    o_out[...] = o
    l_out[...] = jnp.where(lanes(o) < 64, totals[0], totals[1])
    partial = right_product(o.astype(BF), w[:, 256:]).reshape(4, 2, 32, 1024)
    send[...] = partial[:, 1].astype(BF)
    keep[...] = partial[:, 0]


def pair_add(keep, got, own, one, two, three):
    own[...] = keep[0] + got[0].astype(F32)
    for k, out in ((1, one), (2, two), (3, three)):
        out[...] = (keep[k] + got[k].astype(F32)).astype(BF)


def total_of(own, one, two, three):
    return (own[...] + one[...].astype(F32)) + (two[...].astype(F32) + three[...].astype(F32))


def hidden(own, one, two, three, x, gain, h, hn):
    rows = x[:32].astype(F32) + total_of(own, one, two, three)
    h[...] = rows
    hn[...] = (rows * row_scale(rows) * gain[...]).astype(BF)


def feed_parts(gate, up, d_act):
    sig = jax.nn.sigmoid(gate)
    silu = gate * sig
    active = silu * up
    d_gate = d_act * up * sig * (1.0 + gate * (1.0 - sig))
    return active.astype(BF), d_gate, d_act * silu


def feed(p0, p1, p2, p3, p4, p5, p6, p7, dy_own, dy_other, w, send, keep, hn, act, dgu):
    rows = jnp.concatenate([p[...] for p in (p0, p1, p2, p3, p4, p5, p6, p7)])
    hn[...] = rows
    dy = jnp.concatenate([dy_own[...], dy_other[...]])
    def both(left, at, width):
        first, second = left[:, :512], left[:, 512:]
        return dot(first, w[:, 0, :, at : at + width].reshape(512, width)) + dot(
            second, w[:, 1, :, at : at + width].reshape(512, width)
        )
    gate, up, d_act = both(rows, 0, 512), both(rows, 512, 512), both(dy, 1024, 512)
    active, d_gate, d_up = feed_parts(gate, up, d_act)
    act[:, :512] = active
    d_gate, d_up = d_gate.astype(BF), d_up.astype(BF)
    dgu[:, :512] = d_gate
    dgu[:, 512:1024] = d_up
    tail, d_tail = both(rows, 1536, 128), both(dy, 1664, 128)
    low = lanes(tail) < 64
    gate = jnp.where(low, tail, 0.0)
    up = jnp.where(low, pltpu.roll(tail, 64, 1), 0.0)
    active, dg_tail, du_tail = feed_parts(gate, up, d_tail)
    act[:, 512:] = active
    dgu_tail = jnp.where(low, dg_tail, pltpu.roll(du_tail, 64, 1)).astype(BF)
    dgu[:, 1024:] = dgu_tail
    halves = []
    for z in range(2):
        part = right_product(d_gate, w[:, z, :, :512].reshape(512, 512))
        part = part + right_product(d_up, w[:, z, :, 512:1024].reshape(512, 512))
        part = part + right_product(dgu_tail, w[:, z, :, 1536:1664].reshape(512, 128))
        halves.append(part)
    partial = jnp.concatenate(halves, axis=1).reshape(4, 2, 32, 1024)
    send[...] = partial[:, 1].astype(BF)
    keep[...] = partial[:, 0]


def feed_weights(hn, dy_own, dy_other, act, dgu, w, send, keep, dw):
    dy = jnp.concatenate([dy_own[...], dy_other[...]])
    rows, active = hn[...], act[...]
    halves = []
    for z in range(2):
        part = right_product(active[:, :512], w[:, z, :, 1024:1536].reshape(512, 512))
        halves.append(part + right_product(active[:, 512:], w[:, z, :, 1664:].reshape(512, 128)))
    partial = jnp.concatenate(halves, axis=1).reshape(4, 2, 32, 1024)
    send[...] = partial[:, 1].astype(BF)
    keep[...] = partial[:, 0]
    for z in range(2):
        left, left_dy = rows[:, z * 512 : (z + 1) * 512], dy[:, z * 512 : (z + 1) * 512]
        def put(value, at, width):
            blocks = value.astype(BF).reshape(4, 4, 32, width)
            for y in range(4):
                dw[:, z, y, :, at : at + width] = blocks[y]
        put(left_product(left, dgu[:, :512]), 0, 512)
        put(left_product(left, dgu[:, 512:1024]), 512, 512)
        put(left_product(left_dy, active[:, :512]), 1024, 512)
        put(left_product(left, dgu[:, 1024:]), 1536, 128)
        put(left_product(left_dy, active[:, 512:]), 1664, 128)


def block_rows(own, one, two, three, h, out):
    out[...] = (h[...] + total_of(own, one, two, three)).astype(BF)


def hidden_grad(own, one, two, three, h, dy, gain, dh, low, gain_part):
    d_hn = total_of(own, one, two, three)
    rows = h[...]
    scale = row_scale(rows)
    hat = rows * scale
    gain_part[...] = jnp.sum(d_hn * hat, axis=0, keepdims=True)
    grad = dy[:32].astype(F32) + row_norm_grad(d_hn * gain[...], hat, scale)
    dh[...] = grad
    low[...] = grad.astype(BF)


def attend_grad(
    p0, p1, p2, p3, p4, p5, p6, p7, qh, kv0, kv1, kv2, kv3, own_places, places, w, o, l,
    d_attn, d_qh, d_kv0, d_kv1, d_kv2, d_kv3,
):
    rows = jnp.concatenate([p[...] for p in (p0, p1, p2, p3, p4, p5, p6, p7)])
    d_attn[...] = rows
    d_o = dot(rows, w[:, 256:])
    denom = l[...]
    d_inner = (d_o / denom).astype(BF)
    delta = head_sum(d_o * o[...]) / denom
    mine = own_places[...]
    d_q = [0.0, 0.0]
    for i, (kv, d_kv) in enumerate(((kv0, d_kv0), (kv1, d_kv1), (kv2, d_kv2), (kv3, d_kv3))):
        visible = places[:, i * 256 : (i + 1) * 256] <= mine
        k, v = kv[:, :64], kv[:, 64:]
        d_k, d_v = 0.0, 0.0
        for g in range(2):
            at = slice(g * 64, (g + 1) * 64)
            q, di = qh[:, at], d_inner[:, at]
            u = weights_of(q, k, visible)
            ds = (u * (right_product(di, v) - delta[:, g * 64 : g * 64 + 1])).astype(BF)
            d_q[g] = d_q[g] + dot(ds, k)
            d_k = d_k + left_product(ds, q)
            d_v = d_v + left_product(u.astype(BF), di)
        d_kv[...] = jnp.concatenate([d_k * SCALE, d_v], axis=1).astype(d_kv.dtype)
    d_qh[...] = jnp.concatenate(d_q, axis=1) * SCALE


def project_grad(
    d_qh, own, one, two, three, qkv, cosine, sine, qk_gain, w, x_own, x_other,
    d_qkv, send, keep, gain_part, head_part,
):
    d_kv = total_of(own, one, two, three)
    cos, sin = cosine[...], sine[...]
    q, k = qkv[:, :128], qkv[:, 128:]
    q_scale, k_scale = head_scale(q), head_scale(k)
    q_hat, k_hat = q * q_scale, k * k_scale
    d_q = d_qh[...]
    d_qn = d_q * cos - other_half(d_q) * sin
    d_kn = d_kv * cos - other_half(d_kv) * sin
    head_part[0:1] = jnp.sum(d_qn * q_hat, axis=0, keepdims=True)
    head_part[1:2] = jnp.sum(d_kn * k_hat, axis=0, keepdims=True)
    d_q = head_norm_grad(d_qn * qk_gain[0:1], q_hat, q_scale)
    d_k = head_norm_grad(d_kn * qk_gain[1:2], k_hat, k_scale)
    d_k = jnp.where(lanes(d_k) < 64, d_k, d_kv)
    low = jnp.concatenate([d_q, d_k], axis=1).astype(BF)
    d_qkv[...] = low
    partial = right_product(low, w[:, :256])
    x = jnp.concatenate([x_own[...], x_other[...]]).astype(F32)
    gain_part[...] = jnp.sum(partial * (x * row_scale(x)), axis=0, keepdims=True)
    partial = partial.reshape(4, 2, 32, 1024)
    send[...] = partial[:, 1].astype(BF)
    keep[...] = partial[:, 0]


def attend_weights(normed, d_qkv, d_attn, o, attn_part, ffn_part, head_part, dw):
    first = left_product(normed[...], d_qkv[...]).astype(BF)
    second = left_product(d_attn[...], o[...].astype(BF)).astype(BF)
    dw[:, :32, :256] = first.reshape(32, 32, 256)
    dw[:, :32, 256:] = second.reshape(32, 32, 128)
    def fold(part):
        rows = [part[:, i * 128 : (i + 1) * 128] for i in range(8)]
        return jnp.concatenate(rows + [jnp.zeros((8, 128), F32)])
    heads = jnp.concatenate([head_part[...], jnp.zeros((14, 128), F32)])
    gains = jnp.concatenate([fold(attn_part), fold(ffn_part), heads], axis=1).astype(BF)
    dw[:, 32:, :] = jnp.broadcast_to(gains[None], (32, 16, 384))


def token_rows(own, one, two, three, dh, x, gain, out):
    d_xn = total_of(own, one, two, three)
    rows = x[:32].astype(F32)
    scale = row_scale(rows)
    grad = row_norm_grad(d_xn * gain[...], rows * scale, scale)
    out[...] = (dh[...] + grad).astype(BF)


def finish_attend(parts, wq, wk, wv, wo, gains):
    sums = [jnp.sum(parts[z].astype(F32), axis=0) for z in range(2)]
    gains[...] = sums[0][32:] + sums[1][32:]
    low, high = sums[0][:32], sums[1][:32]
    wq[...] = jnp.concatenate([low[:, :128], high[:, :128]], axis=1)
    wk[...] = jnp.concatenate([low[:, 128:192], high[:, 128:192]], axis=1)
    wv[...] = jnp.concatenate([low[:, 192:256], high[:, 192:256]], axis=1)
    wo[...] = jnp.concatenate([low[:, 256:], high[:, 256:]], axis=1)


def finish_feed(parts, wg, wu, wd):
    low = jnp.sum(parts[0].astype(F32), axis=0)
    high = jnp.sum(parts[1].astype(F32), axis=0)
    for i, out in enumerate((wg, wu, wd)):
        wide, tail = slice(i * 512, (i + 1) * 512), slice(1536 + i * 64, 1600 + i * 64)
        out[...] = jnp.concatenate(
            [low[:, wide], low[:, tail], high[:, wide], high[:, tail]], axis=1
        )


def finish_gains(one, two, attn, ffn, query, key):
    total = one[...] + two[...]
    attn[...] = total[:8, :128]
    ffn[...] = total[:8, 128:256]
    query[...] = total[0:1, 256:320] + total[0:1, 320:384]
    key[...] = total[1:2, 256:320]


def add_gains(one, two, out):
    out[...] = one[...] + two[...]


def swap(value, axes, size, mask):
    return lax.ppermute(value, axes, [(i, i ^ mask) for i in range(size)])


def fan(pieces, axes):
    return [swap(pieces[k], axes, 4, k) for k in (1, 2, 3)]


def sum_pair(send, keep):
    got = swap(send, "c", 2, 1)
    small = ((32, 1024), BF)
    return list(call(pair_add, [((32, 1024), F32), small, small, small], keep, got))


def sum_scatter(send, keep):
    own, *rest = sum_pair(send, keep)
    return [own] + fan([None] + rest, Z)


def gather_rows(rows):
    column = [rows] + fan([rows] * 4, Z)
    pieces = []
    for piece in column:
        pieces += [piece, swap(piece, "c", 2, 1)]
    return pieces


def place_rows(head, p0, p1, p2, p3, out):
    for k, piece in enumerate((p0, p1, p2, p3)):
        out[pl.ds((head[0] ^ k) * 32, 32)] = piece[...]


def gather_head(rows, head):
    other = swap(rows, "c", 2, 1)
    pieces = [rows, other, swap(rows, "zh", 2, 1), swap(other, "zh", 2, 1)]
    return pl.pallas_call(
        place_rows,
        out_shape=jax.ShapeDtypeStruct((128, 1024), BF),
        in_specs=[pl.BlockSpec(memory_space=pltpu.SMEM)] + [WHOLE] * 4,
        out_specs=WHOLE,
    )(head.reshape(1), *pieces)[None]


def column_half(parts, zl):
    return [
        jnp.where(zl == 0, p[:, : p.shape[1] // 2], p[:, p.shape[1] // 2 :]) for p in parts
    ]


def feed_columns(gate, up, down):
    zeros = jnp.zeros_like(gate[:, :64])
    parts = [gate[:, :512], up[:, :512], down[:, :512], gate[:, 512:], up[:, 512:], down[:, 512:]]
    return jnp.concatenate(parts + [zeros], axis=1)


def after(values, *first):
    out = lax.optimization_barrier(tuple(values) + tuple(first))
    return list(out[: len(values)])


def local(
    tokens, positions, attn_gain, ffn_gain, query_gain, key_gain,
    w_query, w_key, w_value, w_out, w_gate, w_up, w_down, cotangent,
):
    zl, y, head = lax.axis_index("zl"), lax.axis_index("y"), lax.axis_index(("zh", "c"))
    attn_gain_row, ffn_gain_row = attn_gain[None], ffn_gain[None]

    feeds = [w_gate, w_up, w_down]
    send_f = feed_columns(*column_half(feeds, 1 - zl))
    got_f = swap(send_f, "zl", 2, 1)

    small = [w_query, w_key, w_value, w_out]
    small = after(small, send_f)
    lows = jnp.concatenate([p[:, : p.shape[1] // 2] for p in small], axis=1)
    highs = jnp.concatenate([p[:, p.shape[1] // 2 :] for p in small], axis=1)
    blocks = jnp.broadcast_to(jnp.stack([lows, highs])[:, None], (2, 16, 32, 384))
    blocks = blocks.reshape(1024, 384)
    w_a = lax.all_to_all(blocks, PLANE, 0, 0, tiled=True)

    order = head ^ jnp.arange(4)
    (late_tokens,) = after([tokens], blocks)
    x_own = late_tokens[0].reshape(4, 32, 1024)[order].reshape(128, 1024)
    x_other = swap(x_own, "zl", 2, 1)

    keep_f = feed_columns(*column_half(after(feeds, blocks), zl))
    rows_f = jnp.where(zl == 0, jnp.stack([keep_f, got_f]), jnp.stack([got_f, keep_f]))
    w_f = lax.all_gather(rows_f, ("y", "x"), axis=0)

    (late_positions,) = after([positions], blocks)
    steps = jnp.array([dl * 16 + ky * 4 + d for ky in range(4) for dl in range(2) for d in range(4)])
    places = late_positions[0].reshape(32, 32)[steps ^ (zl * 16 + y * 4 + head)].reshape(1024)
    own_places = places[:256]
    frequency = ROPE_BASE ** (-(jnp.arange(32).astype(F32) * 2.0 / 64))
    angles = own_places.astype(F32)[:, None] * frequency
    cosine, sine = jnp.cos(angles), jnp.sin(angles)
    cosine = jnp.concatenate([cosine] * 4, axis=1)
    sine = jnp.concatenate([-sine, sine] * 2, axis=1)
    own_places, places = own_places[:, None], places[None]
    qk_gain = jnp.stack([jnp.tile(query_gain, 2), jnp.tile(key_gain, 2)])

    halves = [((4, 32, 1024), BF), ((4, 32, 1024), F32)]
    flat = ((256, 128), BF)
    normed, qh, kv, qkv = call(
        project, [((256, 1024), BF), flat, flat, ((256, 256), F32)],
        x_own, x_other, w_a, attn_gain_row, qk_gain, cosine, sine,
    )
    kvs = [kv] + fan([kv] * 4, "y")
    (late_dy,) = after([cotangent], kv)
    dy_own = late_dy[0].reshape(4, 32, 1024)[order].reshape(128, 1024)
    dy_other = swap(dy_own, "zl", 2, 1)
    send, keep, o, l = call(
        attend, halves + [((256, 128), F32)] * 2, qh, *kvs, own_places, places, w_a
    )
    h, hn = call(
        hidden, [((32, 1024), F32), ((32, 1024), BF)],
        *sum_scatter(send, keep), x_own, ffn_gain_row,
    )
    send, keep, hn_all, act, dgu = call(
        feed, halves + [((256, 1024), BF), ((256, 640), BF), ((256, 1152), BF)],
        *gather_rows(hn), dy_own, dy_other, w_f, room=20,
    )
    pair = sum_pair(send, keep)
    act, dgu = after([act, dgu], *pair)
    d_hn = [pair[0]] + fan([None] + pair[1:], Z)
    send_b, keep_b, dw_f = call(
        feed_weights, halves + [((4, 2, 4, 32, 1792), BF)],
        hn_all, dy_own, dy_other, act, dgu, w_f, room=20,
    )
    dw_f = lax.psum_scatter(
        dw_f.reshape(1024, 1792), "x", scatter_dimension=0, tiled=True
    )
    dh, d_low, ffn_gain_part = call(
        hidden_grad, [((32, 1024), F32), ((32, 1024), BF), ((1, 1024), F32)],
        *d_hn, h, dy_own, ffn_gain_row,
    )
    d_attn, d_qh, *d_kvs = call(
        attend_grad,
        [((256, 1024), BF), ((256, 128), F32), ((256, 128), F32), flat, flat, flat],
        *gather_rows(d_low), qh, *kvs, own_places, places, w_a, o, l,
    )
    d_qkv, send, keep, attn_gain_part, head_part = call(
        project_grad,
        [((256, 256), BF)] + halves + [((1, 1024), F32), ((2, 128), F32)],
        d_qh, d_kvs[0], *fan(d_kvs, "y"), qkv, cosine, sine, qk_gain, w_a, x_own, x_other,
    )
    (dw_a,) = call(
        attend_weights, [((32, 48, 384), BF)],
        normed, d_qkv, d_attn, o, attn_gain_part, ffn_gain_part, head_part,
    )
    (keep,) = after([keep], dw_a)
    d_xn = sum_scatter(send, keep)
    (send_b,) = after([send_b], d_xn[0])
    (rows,) = call(block_rows, [((32, 1024), BF)], *sum_scatter(send_b, keep_b), h)
    dw_a = lax.all_to_all(dw_a, PLANE, 0, 0, tiled=True)
    block_out = gather_head(rows, head)
    (rows,) = call(token_rows, [((32, 1024), BF)], *d_xn, dh, x_own, attn_gain_row)
    tokens_grad = gather_head(rows, head)
    dw_f = lax.all_to_all(dw_f, ("zl", "y"), 0, 0, tiled=True)
    grad_wq, grad_wk, grad_wv, grad_wo, gains = call(
        finish_attend, [((32, n), F32) for n in (256, 128, 128, 256)] + [((16, 384), F32)],
        dw_a.reshape(2, 16, 48, 384),
    )
    (gains,) = call(add_gains, [((16, 384), F32)], gains, swap(gains, "c", 2, 1))
    attn_sum, ffn_sum, query_sum, key_sum = call(
        finish_gains, [((8, 128), F32)] * 2 + [((1, 64), F32)] * 2,
        gains, swap(gains, "zh", 2, 1),
    )
    grad_wg, grad_wu, grad_wd = call(
        finish_feed, [((32, 1152), F32)] * 3, dw_f.reshape(2, 4, 32, 1792)
    )
    return (
        block_out, tokens_grad, attn_sum.reshape(1024), ffn_sum.reshape(1024),
        query_sum.reshape(64), key_sum.reshape(64),
        grad_wq, grad_wk, grad_wv, grad_wo, grad_wg, grad_wu, grad_wd,
    )


def solution(mesh):
    cube = Mesh(mesh.devices.reshape(2, 4, 4, 2, 2), AXES)
    rows = P("x", ("zl", "y"), None)
    weight = P(("zl", "y", "x"), ("zh", "c"))
    return jax.shard_map(
        local,
        mesh=cube,
        in_specs=(rows, P("x", None)) + (P(),) * 4 + (weight,) * 7 + (rows,),
        out_specs=(rows, rows) + (P(),) * 4 + (weight,) * 7,
        check_vma=False,
    )
```

```python
import functools

import jax
import jax.numpy as jnp
from jax import lax
from jax.experimental import pallas as pl
from jax.experimental.pallas import tpu as pltpu
from jax.sharding import Mesh, PartitionSpec as P

EPSILON = 1e-05
ROPE_BASE = 1000000.0
AXES = ("zl", "y", "x", "zh", "c")
Z = ("zl", "zh")
PLANE = ("zl", "y", "x")
BF = jnp.bfloat16
F32 = jnp.float32
SCALE = 64 ** (-0.5)
WHOLE = pl.BlockSpec(memory_space=pltpu.VMEM)


class Far:
    def __init__(self, value, kind=None):
        self.value, self.kind = value, kind


def call(body, outs, *operands, room=16):
    spec = lambda item: pl.BlockSpec() if isinstance(item, Far) else WHOLE
    bare = lambda item: item.value if isinstance(item, Far) else item
    return list(
        pl.pallas_call(
            body,
            out_shape=[jax.ShapeDtypeStruct(*bare(out)) for out in outs],
            in_specs=[spec(item) for item in operands],
            out_specs=[spec(out) for out in outs],
            compiler_params=pltpu.CompilerParams(vmem_limit_bytes=room * 2**20),
        )(*[bare(item) for item in operands])
    )


def dot(left, right):
    return jnp.dot(left, right, preferred_element_type=F32)


def left_product(left, right):
    return lax.dot_general(left, right, (((0,), (0,)), ((), ())), preferred_element_type=F32)


def right_product(left, right):
    return lax.dot_general(left, right, (((1,), (1,)), ((), ())), preferred_element_type=F32)


def row_scale(values):
    return lax.rsqrt(jnp.mean(values * values, axis=-1, keepdims=True) + EPSILON)


def row_norm_grad(grad, normal, scale):
    return scale * (grad - normal * jnp.mean(grad * normal, axis=-1, keepdims=True))


def lanes(values):
    return lax.broadcasted_iota(jnp.int32, values.shape, 1)


def head_sum(values):
    low = lanes(values) < 64
    first = jnp.sum(jnp.where(low, values, 0.0), axis=-1, keepdims=True)
    second = jnp.sum(jnp.where(low, 0.0, values), axis=-1, keepdims=True)
    return jnp.where(low, first, second)


def head_scale(values):
    return lax.rsqrt(head_sum(values * values) * (1.0 / 64) + EPSILON)


def head_norm_grad(grad, normal, scale):
    return scale * (grad - normal * (head_sum(grad * normal) * (1.0 / 64)))


def other_half(values):
    low = (lanes(values) & 63) < 32
    return jnp.where(low, pltpu.roll(values, 96, 1), pltpu.roll(values, 32, 1))


def project(own, other, w, attn_gain, qk_gain, cosine, sine, normed, qh, kv, qkv):
    x = jnp.concatenate([own[...], other[...]]).astype(F32)
    low = (x * row_scale(x) * attn_gain[...]).astype(BF)
    normed[...] = low
    out = dot(low, w[:, :256])
    qkv[...] = out
    q, k = out[:, :128], out[:, 128:]
    cos, sin = cosine[...], sine[...]
    qn = q * head_scale(q) * qk_gain[0:1]
    qh[...] = (qn * cos + other_half(qn) * sin).astype(BF)
    kn = k * head_scale(k) * qk_gain[1:2]
    kr = kn * cos + other_half(kn) * sin
    kv[...] = jnp.where(lanes(k) < 64, kr, k).astype(BF)


def weights_of(q, k, visible):
    scores = right_product(q, k) * SCALE
    return jnp.where(visible, jnp.exp(scores), 0.0)


def attend(qh, kv0, kv1, kv2, kv3, own_places, places, w, send, keep, o_out, l_out):
    sums, totals = [0.0, 0.0], [0.0, 0.0]
    mine = own_places[...]
    for i, kv in enumerate((kv0, kv1, kv2, kv3)):
        visible = places[:, i * 256 : (i + 1) * 256] <= mine
        k, v = kv[:, :64], kv[:, 64:]
        for g in range(2):
            u = weights_of(qh[:, g * 64 : (g + 1) * 64], k, visible)
            totals[g] = totals[g] + jnp.sum(u, axis=-1, keepdims=True)
            sums[g] = sums[g] + dot(u.astype(BF), v)
    o = jnp.concatenate([sums[g] / totals[g] for g in range(2)], axis=1)
    o_out[...] = o
    l_out[...] = jnp.where(lanes(o) < 64, totals[0], totals[1])
    partial = right_product(o.astype(BF), w[:, 256:]).reshape(4, 2, 32, 1024)
    send[...] = partial[:, 1].astype(BF)
    keep[...] = partial[:, 0]


def pair_add(keep, got, own, one, two, three):
    own[...] = keep[0] + got[0].astype(F32)
    for k, out in ((1, one), (2, two), (3, three)):
        out[...] = (keep[k] + got[k].astype(F32)).astype(BF)


def total_of(own, one, two, three):
    return (own[...] + one[...].astype(F32)) + (two[...].astype(F32) + three[...].astype(F32))


def hidden(own, one, two, three, x, gain, h, hn):
    rows = x[:32].astype(F32) + total_of(own, one, two, three)
    h[...] = rows
    hn[...] = (rows * row_scale(rows) * gain[...]).astype(BF)


def feed_parts(gate, up, d_act):
    sig = jax.nn.sigmoid(gate)
    silu = gate * sig
    active = silu * up
    d_gate = d_act * up * sig * (1.0 + gate * (1.0 - sig))
    return active.astype(BF), d_gate, d_act * silu


def feed(
    p0, p1, p2, p3, p4, p5, p6, p7, dy_own, dy_other, w,
    send, keep, hn, act, dgu,
):
    rows = jnp.concatenate([p[...] for p in (p0, p1, p2, p3, p4, p5, p6, p7)])
    hn[...] = rows
    dy = jnp.concatenate([dy_own[...], dy_other[...]])
    def both(left, at, width):
        first, second = left[:, :512], left[:, 512:]
        return dot(first, w[:, 0, :, at : at + width].reshape(512, width)) + dot(
            second, w[:, 1, :, at : at + width].reshape(512, width)
        )
    gate, up, d_act = both(rows, 0, 512), both(rows, 512, 512), both(dy, 1024, 512)
    active, d_gate, d_up = feed_parts(gate, up, d_act)
    act[:, :512] = active
    d_gate, d_up = d_gate.astype(BF), d_up.astype(BF)
    dgu[:, :512] = d_gate
    dgu[:, 512:1024] = d_up
    tail, d_tail = both(rows, 1536, 128), both(dy, 1664, 128)
    low = lanes(tail) < 64
    gate = jnp.where(low, tail, 0.0)
    up = jnp.where(low, pltpu.roll(tail, 64, 1), 0.0)
    active, dg_tail, du_tail = feed_parts(gate, up, d_tail)
    act[:, 512:] = active
    dgu_tail = jnp.where(low, dg_tail, pltpu.roll(du_tail, 64, 1)).astype(BF)
    dgu[:, 1024:] = dgu_tail
    halves = []
    for z in range(2):
        part = right_product(d_gate, w[:, z, :, :512].reshape(512, 512))
        part = part + right_product(d_up, w[:, z, :, 512:1024].reshape(512, 512))
        part = part + right_product(dgu_tail, w[:, z, :, 1536:1664].reshape(512, 128))
        halves.append(part)
    partial = jnp.concatenate(halves, axis=1).reshape(4, 2, 32, 1024)
    send[:, :32] = partial[:, 1].astype(BF)
    keep[:, :32] = partial[:, 0]
    low_act = act[...]
    halves = []
    for z in range(2):
        part = right_product(low_act[:, :512], w[:, z, :, 1024:1536].reshape(512, 512))
        halves.append(part + right_product(low_act[:, 512:], w[:, z, :, 1664:].reshape(512, 128)))
    partial = jnp.concatenate(halves, axis=1).reshape(4, 2, 32, 1024)
    send[:, 32:] = partial[:, 1].astype(BF)
    keep[:, 32:] = partial[:, 0]


def feed_weights(hn, dy_own, dy_other, act, dgu, dw):
    dy = jnp.concatenate([dy_own[...], dy_other[...]])
    rows, active = hn[...], act[...]
    for z in range(2):
        left, left_dy = rows[:, z * 512 : (z + 1) * 512], dy[:, z * 512 : (z + 1) * 512]
        def put(value, at, width):
            blocks = value.astype(BF).reshape(4, 4, 32, width)
            for y in range(4):
                dw[:, z, y, :, at : at + width] = blocks[y]
        put(left_product(left, dgu[:, :512]), 0, 512)
        put(left_product(left, dgu[:, 512:1024]), 512, 512)
        put(left_product(left_dy, active[:, :512]), 1024, 512)
        put(left_product(left, dgu[:, 1024:]), 1536, 128)
        put(left_product(left_dy, active[:, 512:]), 1664, 128)


def hidden_grad(own, one, two, three, h, dy, gain, dh, low, gain_part, block):
    total = total_of(own, one, two, three)
    d_hn, branch = total[:32], total[32:]
    rows = h[...]
    block[...] = (rows + branch).astype(BF)
    scale = row_scale(rows)
    hat = rows * scale
    gain_part[...] = jnp.sum(d_hn * hat, axis=0, keepdims=True)
    grad = dy[:32].astype(F32) + row_norm_grad(d_hn * gain[...], hat, scale)
    dh[...] = grad
    low[...] = grad.astype(BF)


def attend_grad(
    p0, p1, p2, p3, p4, p5, p6, p7, qh, kv0, kv1, kv2, kv3, own_places, places, w, o, l,
    d_attn, d_qh, d_kv0, d_kv1, d_kv2, d_kv3,
):
    rows = jnp.concatenate([p[...] for p in (p0, p1, p2, p3, p4, p5, p6, p7)])
    d_attn[...] = rows
    d_o = dot(rows, w[:, 256:])
    denom = l[...]
    d_inner = (d_o / denom).astype(BF)
    delta = head_sum(d_o * o[...]) / denom
    mine = own_places[...]
    d_q = [0.0, 0.0]
    for i, (kv, d_kv) in enumerate(((kv0, d_kv0), (kv1, d_kv1), (kv2, d_kv2), (kv3, d_kv3))):
        visible = places[:, i * 256 : (i + 1) * 256] <= mine
        k, v = kv[:, :64], kv[:, 64:]
        d_k, d_v = 0.0, 0.0
        for g in range(2):
            at = slice(g * 64, (g + 1) * 64)
            q, di = qh[:, at], d_inner[:, at]
            u = weights_of(q, k, visible)
            ds = (u * (right_product(di, v) - delta[:, g * 64 : g * 64 + 1])).astype(BF)
            d_q[g] = d_q[g] + dot(ds, k)
            d_k = d_k + left_product(ds, q)
            d_v = d_v + left_product(u.astype(BF), di)
        d_kv[...] = jnp.concatenate([d_k * SCALE, d_v], axis=1).astype(d_kv.dtype)
    d_qh[...] = jnp.concatenate(d_q, axis=1) * SCALE


def project_grad(
    d_qh, own, one, two, three, qkv, cosine, sine, qk_gain, w, x_own, x_other, ffn_part,
    d_qkv, send, keep, gains,
):
    d_kv = total_of(own, one, two, three)
    cos, sin = cosine[...], sine[...]
    q, k = qkv[:, :128], qkv[:, 128:]
    q_scale, k_scale = head_scale(q), head_scale(k)
    q_hat, k_hat = q * q_scale, k * k_scale
    d_q = d_qh[...]
    d_qn = d_q * cos - other_half(d_q) * sin
    d_kn = d_kv * cos - other_half(d_kv) * sin
    heads = jnp.concatenate(
        [jnp.sum(d_qn * q_hat, axis=0, keepdims=True), jnp.sum(d_kn * k_hat, axis=0, keepdims=True)]
    )
    d_q = head_norm_grad(d_qn * qk_gain[0:1], q_hat, q_scale)
    d_k = head_norm_grad(d_kn * qk_gain[1:2], k_hat, k_scale)
    d_k = jnp.where(lanes(d_k) < 64, d_k, d_kv)
    low = jnp.concatenate([d_q, d_k], axis=1).astype(BF)
    d_qkv[...] = low
    partial = right_product(low, w[:, :256])
    x = jnp.concatenate([x_own[...], x_other[...]]).astype(F32)
    attn_part = jnp.sum(partial * (x * row_scale(x)), axis=0, keepdims=True)
    def fold(part):
        rows = [part[:, i * 128 : (i + 1) * 128] for i in range(8)]
        return jnp.concatenate(rows + [jnp.zeros((8, 128), F32)])
    heads = jnp.concatenate([heads, jnp.zeros((14, 128), F32)])
    gains[...] = jnp.concatenate([fold(attn_part), fold(ffn_part), heads], axis=1).astype(BF)
    partial = partial.reshape(4, 2, 32, 1024)
    send[...] = partial[:, 1].astype(BF)
    keep[...] = partial[:, 0]


def attend_weights(normed, d_qkv, d_attn, o, gains, dw):
    first = left_product(normed[...], d_qkv[...]).astype(BF).reshape(8, 4, 32, 256)
    second = left_product(d_attn[...], o[...].astype(BF)).astype(BF).reshape(8, 4, 32, 128)
    for i in range(8):
        dw[:, i * 32 : (i + 1) * 32, :256] = first[i]
        dw[:, i * 32 : (i + 1) * 32, 256:] = second[i]
    dw[:, 256:] = jnp.broadcast_to(gains[...][None], (4, 16, 384))


def share_gains(dw, out):
    out[:, :32] = dw[:256].reshape(8, 32, 384)
    out[:, 32:] = jnp.broadcast_to(dw[256:][None], (8, 16, 384))


def token_rows(own, one, two, three, dh, x, gain, block, out):
    d_xn = total_of(own, one, two, three)
    rows = x[:32].astype(F32)
    scale = row_scale(rows)
    grad = row_norm_grad(d_xn * gain[...], rows * scale, scale)
    out[:32] = (dh[...] + grad).astype(BF)
    out[32:] = block[...]


def finish_attend(parts, wq, wk, wv, wo, gains):
    sums = [jnp.sum(parts[z].astype(F32), axis=0) for z in range(2)]
    gains[...] = sums[0][32:] + sums[1][32:]
    low, high = sums[0][:32], sums[1][:32]
    wq[...] = jnp.concatenate([low[:, :128], high[:, :128]], axis=1)
    wk[...] = jnp.concatenate([low[:, 128:192], high[:, 128:192]], axis=1)
    wv[...] = jnp.concatenate([low[:, 192:256], high[:, 192:256]], axis=1)
    wo[...] = jnp.concatenate([low[:, 256:], high[:, 256:]], axis=1)


def finish_feed(parts, wg, wu, wd):
    low = jnp.sum(parts[0].astype(F32), axis=0)
    high = jnp.sum(parts[1].astype(F32), axis=0)
    for i, out in enumerate((wg, wu, wd)):
        wide, tail = slice(i * 512, (i + 1) * 512), slice(1536 + i * 64, 1600 + i * 64)
        out[...] = jnp.concatenate(
            [low[:, wide], low[:, tail], high[:, wide], high[:, tail]], axis=1
        )


def add_two(own, one, out):
    out[...] = own[...] + one[...]


def finish_gains(one, two, attn, ffn, query, key):
    total = one[...] + two[...]
    attn[...] = total[:8, :128]
    ffn[...] = total[:8, 128:256]
    query[...] = total[0:1, 256:320] + total[0:1, 320:384]
    key[...] = total[1:2, 256:320]


def prepare(zl, wq, wk, wv, wo, wg, wu, wd, blocks, send_f, keep_f):
    for z in range(2):
        at = 0
        for w in (wq, wk, wv, wo):
            width = w.shape[1] // 2
            part = w[:, z * width : (z + 1) * width]
            blocks[z, :, :, at : at + width] = jnp.broadcast_to(part[None], (16, 32, width))
            at += width
    pad = jnp.zeros((32, 64), BF)
    sides = []
    for z in range(2):
        parts = [w[:, z * 576 : (z + 1) * 576] for w in (wg, wu, wd)]
        sides.append(
            jnp.concatenate([p[:, :512] for p in parts] + [p[:, 512:] for p in parts] + [pad], axis=1)
        )
    first = zl[0] == 0
    keep_f[...] = jnp.where(first, sides[0], sides[1])
    send_f[...] = jnp.where(first, sides[1], sides[0])


def order_rows(zl, own, got, out):
    out[zl[0]] = own[...]
    out[1 - zl[0]] = got[...]


def swap(value, axes, size, mask):
    return lax.ppermute(value, axes, [(i, i ^ mask) for i in range(size)])


def fan(pieces, axes):
    return [swap(pieces[k], axes, 4, k) for k in (1, 2, 3)]


def sum_pair(send, keep):
    got = swap(send, "c", 2, 1)
    shape = send.shape[1:]
    return call(pair_add, [(shape, F32)] + [(shape, BF)] * 3, keep, got)


def sum_scatter(send, keep):
    own, *rest = sum_pair(send, keep)
    return [own] + fan([None] + rest, Z)


def gather_rows(rows):
    column = [rows] + fan([rows] * 4, Z)
    pieces = []
    for piece in column:
        pieces += [piece, swap(piece, "c", 2, 1)]
    return pieces


def place_rows(head, p0, p1, p2, p3, tokens_grad, block_out):
    for k, piece in enumerate((p0, p1, p2, p3)):
        at = pl.ds((head[0] ^ k) * 32, 32)
        tokens_grad[at] = piece[:32]
        block_out[at] = piece[32:]


def gather_head(rows, head):
    other = swap(rows, "c", 2, 1)
    pieces = [rows, other, swap(rows, "zh", 2, 1), swap(other, "zh", 2, 1)]
    return pl.pallas_call(
        place_rows,
        out_shape=[jax.ShapeDtypeStruct((128, 1024), BF)] * 2,
        in_specs=[pl.BlockSpec(memory_space=pltpu.SMEM)] + [WHOLE] * 4,
        out_specs=[pl.BlockSpec()] * 2,
    )(head.reshape(1), *pieces)


def after(values, *first):
    out = lax.optimization_barrier(tuple(values) + tuple(first))
    return list(out[: len(values)])


def local(
    tokens, positions, attn_gain, ffn_gain, query_gain, key_gain,
    w_query, w_key, w_value, w_out, w_gate, w_up, w_down, cotangent,
):
    zl, y, head = lax.axis_index("zl"), lax.axis_index("y"), lax.axis_index(("zh", "c"))
    attn_gain_row, ffn_gain_row = attn_gain[None], ffn_gain[None]

    scalar = pl.BlockSpec(memory_space=pltpu.SMEM)
    zl_ref = zl.reshape(1)
    blocks, send_f, keep_f = pl.pallas_call(
        prepare,
        out_shape=[
            jax.ShapeDtypeStruct(shape, BF)
            for shape in ((2, 16, 32, 384), (32, 1792), (32, 1792))
        ],
        in_specs=[scalar] + [pl.BlockSpec()] * 7,
        out_specs=[WHOLE] * 3,
    )(zl_ref, w_query, w_key, w_value, w_out, w_gate, w_up, w_down)
    got_f = swap(send_f, "zl", 2, 1)
    w_a = lax.all_to_all(blocks.reshape(1024, 384), PLANE, 0, 0, tiled=True)
    rows_f = pl.pallas_call(
        order_rows,
        out_shape=jax.ShapeDtypeStruct((2, 32, 1792), BF),
        in_specs=[scalar] + [WHOLE] * 2,
        out_specs=pl.BlockSpec(),
    )(zl_ref, keep_f, got_f)
    w_f = lax.all_gather(rows_f, ("y", "x"), axis=0)

    order = head ^ jnp.arange(4)
    (late_tokens,) = after([tokens], blocks)
    x_own = late_tokens[0].reshape(4, 32, 1024)[order].reshape(128, 1024)
    x_other = swap(x_own, "zl", 2, 1)

    (late_dy,) = after([cotangent], x_own)
    dy_own = late_dy[0].reshape(4, 32, 1024)[order].reshape(128, 1024)
    dy_other = swap(dy_own, "zl", 2, 1)

    (late_positions,) = after([positions], blocks)
    steps = jnp.array([dl * 16 + ky * 4 + d for ky in range(4) for dl in range(2) for d in range(4)])
    places = late_positions[0].reshape(32, 32)[steps ^ (zl * 16 + y * 4 + head)].reshape(1024)
    own_places = places[:256]
    frequency = ROPE_BASE ** (-(jnp.arange(32).astype(F32) * 2.0 / 64))
    angles = own_places.astype(F32)[:, None] * frequency
    cosine, sine = jnp.cos(angles), jnp.sin(angles)
    cosine = jnp.concatenate([cosine] * 4, axis=1)
    sine = jnp.concatenate([-sine, sine] * 2, axis=1)
    own_places, places = own_places[:, None], places[None]
    qk_gain = jnp.stack([jnp.tile(query_gain, 2), jnp.tile(key_gain, 2)])

    halves = [((4, 32, 1024), BF), ((4, 32, 1024), F32)]
    flat, wide_flat = ((256, 128), BF), ((256, 128), F32)
    rows_low, rows_high = ((32, 1024), BF), ((32, 1024), F32)
    normed, qh, kv, qkv = call(
        project, [Far(((256, 1024), BF)), flat, flat, Far(((256, 256), F32))],
        x_own, x_other, Far(w_a), attn_gain_row, qk_gain, cosine, sine,
    )
    kvs = [kv] + fan([kv] * 4, "y")
    send, keep, o, l = call(
        attend, halves + [Far(wide_flat)] * 2, qh, *kvs, own_places, places, Far(w_a)
    )
    h, hn = call(
        hidden, [Far(rows_high), rows_low], *sum_scatter(send, keep), x_own, ffn_gain_row
    )
    send, keep, hn_all, act, dgu = call(
        feed,
        [((4, 64, 1024), BF), ((4, 64, 1024), F32)]
        + [((256, 1024), BF), ((256, 640), BF), ((256, 1152), BF)],
        *gather_rows(hn), dy_own, dy_other, Far(w_f), room=24,
    )
    pair = sum_pair(send, keep)
    act, dgu = after([act, dgu], *pair)
    d_hn = [pair[0]] + fan([None] + pair[1:], Z)
    (dw_f,) = call(
        feed_weights, [Far(((4, 2, 4, 32, 1792), BF))], hn_all, dy_own, dy_other, act, dgu, room=24
    )
    dw_f = lax.psum_scatter(dw_f.reshape(1024, 1792), "x", scatter_dimension=0, tiled=True)
    dh, d_low, ffn_part, block = call(
        hidden_grad, [Far(rows_high), rows_low, Far(((1, 1024), F32)), Far(rows_low)],
        *d_hn, Far(h), dy_own, ffn_gain_row,
    )
    d_attn, d_qh, *d_kvs = call(
        attend_grad, [Far(((256, 1024), BF)), wide_flat, wide_flat, flat, flat, flat],
        *gather_rows(d_low), Far(qh), *[Far(t) for t in kvs], own_places, places, Far(w_a), Far(o), Far(l),
    )
    d_qkv, send, keep, gains = call(
        project_grad, [((256, 256), BF)] + halves + [((16, 384), BF)],
        d_qh, d_kvs[0], *fan(d_kvs, "y"), Far(qkv), cosine, sine, qk_gain, Far(w_a),
        Far(x_own), Far(x_other), Far(ffn_part),
    )
    (dw_a,) = call(
        attend_weights, [Far(((4, 272, 384), BF))], Far(normed), d_qkv, Far(d_attn), Far(o), gains
    )
    (keep,) = after([keep], dw_a)
    dw_a = lax.psum_scatter(dw_a.reshape(1088, 384), "x", scatter_dimension=0, tiled=True)
    d_xn = sum_scatter(send, keep)
    (rows,) = call(
        token_rows, [((64, 1024), BF)], *d_xn, Far(dh), x_own, attn_gain_row, Far(block)
    )
    tokens_grad, block_out = gather_head(rows, head)
    tokens_grad, block_out = tokens_grad[None], block_out[None]

    (dw_f,) = after([dw_f], rows)
    dw_f = lax.all_to_all(dw_f, ("zl", "y"), 0, 0, tiled=True)
    grad_wg, grad_wu, grad_wd = call(
        finish_feed, [Far(((32, 1152), F32))] * 3, dw_f.reshape(2, 4, 32, 1792)
    )
    (dw_a,) = after([dw_a], grad_wg)
    (dw_a,) = call(share_gains, [((8, 48, 384), BF)], dw_a)
    dw_a = lax.all_to_all(dw_a, ("zl", "y"), 0, 0, tiled=True)
    grad_wq, grad_wk, grad_wv, grad_wo, gains = call(
        finish_attend,
        [Far(((32, n), F32)) for n in (256, 128, 128, 256)] + [((16, 384), F32)],
        dw_a.reshape(2, 4, 48, 384),
    )
    (gains,) = call(add_two, [((16, 384), F32)], gains, swap(gains, "c", 2, 1))
    attn_sum, ffn_sum, query_sum, key_sum = call(
        finish_gains, [((8, 128), F32)] * 2 + [((1, 64), F32)] * 2,
        gains, swap(gains, "zh", 2, 1),
    )
    return (
        block_out, tokens_grad, attn_sum.reshape(1024), ffn_sum.reshape(1024),
        query_sum.reshape(64), key_sum.reshape(64),
        grad_wq, grad_wk, grad_wv, grad_wo, grad_wg, grad_wu, grad_wd,
    )


def solution(mesh):
    cube = Mesh(mesh.devices.reshape(2, 4, 4, 2, 2), AXES)
    rows = P("x", ("zl", "y"), None)
    weight = P(("zl", "y", "x"), ("zh", "c"))
    return jax.shard_map(
        local,
        mesh=cube,
        in_specs=(rows, P("x", None)) + (P(),) * 4 + (weight,) * 7 + (rows,),
        out_specs=(rows, rows) + (P(),) * 4 + (weight,) * 7,
        check_vma=False,
    )
```

```python
import functools

import jax
import jax.numpy as jnp
from jax import lax
from jax.experimental import pallas as pl
from jax.experimental.pallas import tpu as pltpu
from jax.sharding import Mesh, PartitionSpec as P

EPSILON = 1e-05
ROPE_BASE = 1000000.0
AXES = ("zl", "y", "x", "zh", "c")
Z = ("zl", "zh")
PLANE = ("zl", "y", "x")
BF = jnp.bfloat16
F32 = jnp.float32
SCALE = 64 ** (-0.5)
GROUPS = ((0, 0, 1, 3), (0, 1, 3, 1), (1, 0, 1, 3), (1, 1, 3, 1))
WHOLE = pl.BlockSpec(memory_space=pltpu.VMEM)


class Far:
    def __init__(self, value, kind=None):
        self.value, self.kind = value, kind


def call(body, outs, *operands, room=16, scalars=(), scratch=()):
    spec = lambda item: pl.BlockSpec() if isinstance(item, Far) else WHOLE
    bare = lambda item: item.value if isinstance(item, Far) else item
    scalar = pl.BlockSpec(memory_space=pltpu.SMEM)
    return list(
        pl.pallas_call(
            body,
            out_shape=[jax.ShapeDtypeStruct(*bare(out)) for out in outs],
            in_specs=[scalar] * len(scalars) + [spec(item) for item in operands],
            out_specs=[spec(out) for out in outs],
            scratch_shapes=list(scratch),
            compiler_params=pltpu.CompilerParams(vmem_limit_bytes=room * 2**20),
        )(*scalars, *[bare(item) for item in operands])
    )


def dot(left, right):
    return jnp.dot(left, right, preferred_element_type=F32)


def left_product(left, right):
    return lax.dot_general(left, right, (((0,), (0,)), ((), ())), preferred_element_type=F32)


def right_product(left, right):
    return lax.dot_general(left, right, (((1,), (1,)), ((), ())), preferred_element_type=F32)


def row_scale(values):
    return lax.rsqrt(jnp.mean(values * values, axis=-1, keepdims=True) + EPSILON)


def row_norm_grad(grad, normal, scale):
    return scale * (grad - normal * jnp.mean(grad * normal, axis=-1, keepdims=True))


def lanes(values):
    return lax.broadcasted_iota(jnp.int32, values.shape, 1)


def head_sum(values):
    low = lanes(values) < 64
    first = jnp.sum(jnp.where(low, values, 0.0), axis=-1, keepdims=True)
    second = jnp.sum(jnp.where(low, 0.0, values), axis=-1, keepdims=True)
    return jnp.where(low, first, second)


def head_scale(values):
    return lax.rsqrt(head_sum(values * values) * (1.0 / 64) + EPSILON)


def head_norm_grad(grad, normal, scale):
    return scale * (grad - normal * (head_sum(grad * normal) * (1.0 / 64)))


def other_half(values):
    low = (lanes(values) & 63) < 32
    return jnp.where(low, pltpu.roll(values, 96, 1), pltpu.roll(values, 32, 1))


def project(own, other, w, attn_gain, qk_gain, cosine, sine, normed, qh, kv, qkv):
    x = jnp.concatenate([own[...], other[...]]).astype(F32)
    low = (x * row_scale(x) * attn_gain[...]).astype(BF)
    normed[...] = low
    out = dot(low, w[:, :256])
    qkv[...] = out
    q, k = out[:, :128], out[:, 128:]
    cos, sin = cosine[...], sine[...]
    qn = q * head_scale(q) * qk_gain[0:1]
    qh[...] = (qn * cos + other_half(qn) * sin).astype(BF)
    kn = k * head_scale(k) * qk_gain[1:2]
    kr = kn * cos + other_half(kn) * sin
    kv[...] = jnp.where(lanes(k) < 64, kr, k).astype(BF)


def weights_of(q, k, visible):
    scores = right_product(q, k) * SCALE
    return jnp.where(visible, jnp.exp(scores), 0.0)


def attend(qh, kv0, kv1, kv2, kv3, own_places, places, w, send, keep, o_out, l_out):
    sums, totals = [0.0, 0.0], [0.0, 0.0]
    mine = own_places[...]
    for i, kv in enumerate((kv0, kv1, kv2, kv3)):
        visible = places[:, i * 256 : (i + 1) * 256] <= mine
        k, v = kv[:, :64], kv[:, 64:]
        for g in range(2):
            u = weights_of(qh[:, g * 64 : (g + 1) * 64], k, visible)
            totals[g] = totals[g] + jnp.sum(u, axis=-1, keepdims=True)
            sums[g] = sums[g] + dot(u.astype(BF), v)
    o = jnp.concatenate([sums[g] / totals[g] for g in range(2)], axis=1)
    o_out[...] = o
    l_out[...] = jnp.where(lanes(o) < 64, totals[0], totals[1])
    partial = right_product(o.astype(BF), w[:, 256:]).reshape(4, 2, 32, 1024)
    send[...] = partial[:, 1].astype(BF)
    keep[...] = partial[:, 0]


def pair_add(keep, got, own, one, two, three):
    own[...] = keep[0] + got[0].astype(F32)
    for k, out in ((1, one), (2, two), (3, three)):
        out[...] = (keep[k] + got[k].astype(F32)).astype(BF)


def total_of(own, one, two, three):
    return (own[...] + one[...].astype(F32)) + (two[...].astype(F32) + three[...].astype(F32))


def hidden(own, one, two, three, x, gain, h, hn):
    rows = x[:32].astype(F32) + total_of(own, one, two, three)
    h[...] = rows
    hn[...] = (rows * row_scale(rows) * gain[...]).astype(BF)


def feed_parts(gate, up, d_act):
    sig = jax.nn.sigmoid(gate)
    silu = gate * sig
    active = silu * up
    d_gate = d_act * up * sig * (1.0 + gate * (1.0 - sig))
    return active.astype(BF), d_gate, d_act * silu


def feed(
    p0, p1, p2, p3, p4, p5, p6, p7, dy_own, dy_other, w,
    send, keep, hn, act, dgu,
):
    rows = jnp.concatenate([p[...] for p in (p0, p1, p2, p3, p4, p5, p6, p7)])
    hn[...] = rows
    dy = jnp.concatenate([dy_own[...], dy_other[...]])
    def both(left, at, width):
        first, second = left[:, :512], left[:, 512:]
        return dot(first, w[0, :, :, at : at + width].reshape(512, width)) + dot(
            second, w[1, :, :, at : at + width].reshape(512, width)
        )
    gate, up, d_act = both(rows, 0, 512), both(rows, 512, 512), both(dy, 1024, 512)
    active, d_gate, d_up = feed_parts(gate, up, d_act)
    act[:, :512] = active
    d_gate, d_up = d_gate.astype(BF), d_up.astype(BF)
    dgu[:, :512] = d_gate
    dgu[:, 512:1024] = d_up
    tail, d_tail = both(rows, 1536, 128), both(dy, 1664, 128)
    low = lanes(tail) < 64
    gate = jnp.where(low, tail, 0.0)
    up = jnp.where(low, pltpu.roll(tail, 64, 1), 0.0)
    active, dg_tail, du_tail = feed_parts(gate, up, d_tail)
    act[:, 512:] = active
    dgu_tail = jnp.where(low, dg_tail, pltpu.roll(du_tail, 64, 1)).astype(BF)
    dgu[:, 1024:] = dgu_tail
    halves = []
    for z in range(2):
        part = right_product(d_gate, w[z, :, :, :512].reshape(512, 512))
        part = part + right_product(d_up, w[z, :, :, 512:1024].reshape(512, 512))
        part = part + right_product(dgu_tail, w[z, :, :, 1536:1664].reshape(512, 128))
        halves.append(part)
    partial = jnp.concatenate(halves, axis=1).reshape(4, 2, 32, 1024)
    send[:, :32] = partial[:, 1].astype(BF)
    keep[:, :32] = partial[:, 0]
    low_act = act[...]
    halves = []
    for z in range(2):
        part = right_product(low_act[:, :512], w[z, :, :, 1024:1536].reshape(512, 512))
        halves.append(part + right_product(low_act[:, 512:], w[z, :, :, 1664:].reshape(512, 128)))
    partial = jnp.concatenate(halves, axis=1).reshape(4, 2, 32, 1024)
    send[:, 32:] = partial[:, 1].astype(BF)
    keep[:, 32:] = partial[:, 0]


def feed_weights(place, hn, dy_own, dy_other, act, dgu, *outs):
    dw = outs[8]
    dy = jnp.concatenate([dy_own[...], dy_other[...]])
    rows, active = hn[...], act[...]
    for z in range(2):
        left, left_dy = rows[:, z * 512 : (z + 1) * 512], dy[:, z * 512 : (z + 1) * 512]
        def put(value, at, width):
            dw[z, :, :, at : at + width] = value.astype(BF).reshape(16, 32, width)
        put(left_product(left, dgu[:, :512]), 0, 512)
        put(left_product(left, dgu[:, 512:1024]), 512, 512)
        put(left_product(left_dy, active[:, :512]), 1024, 512)
        put(left_product(left, dgu[:, 1024:]), 1536, 128)
        put(left_product(left_dy, active[:, 512:]), 1664, 128)
    for group, (side, z, first, second) in enumerate(GROUPS):
        for i, (sent, kept) in enumerate(((first, 0), (2, second))):
            for other in range(4):
                for out, near in ((outs[group], sent), (outs[4 + group], kept)):
                    dy_, dx_ = (other, near) if side == 0 else (near, other)
                    at = (place[0] ^ dy_) * 4 + (place[1] ^ dx_)
                    out[i, other] = dw[z, at, :, side * 896 : (side + 1) * 896]


def add_first(*refs):
    keeps, gots, sends, owns = refs[:4], refs[4:8], refs[8:12], refs[12:]
    for keep, got, send, own in zip(keeps, gots, sends, owns):
        own[...] = keep[0].astype(F32) + got[0].astype(F32)
        send[...] = (keep[1].astype(F32) + got[1].astype(F32)).astype(BF)


def add_second(*refs):
    owns, gots, outs = refs[:4], refs[4:8], refs[8:]
    for group, (side, z, _, _) in enumerate(GROUPS):
        total = owns[group][...] + gots[group][...].astype(F32)
        outs[side * 4][z] = total[0]
        for k in range(1, 4):
            outs[side * 4 + k][z] = total[k].astype(BF)


def add_third(zl, *refs):
    ins, own, send = refs[:8], refs[8], refs[9]
    for side in range(2):
        mine, one, two, three = ins[side * 4 : side * 4 + 4]
        at = slice(side * 896, (side + 1) * 896)
        def total(z):
            first = mine[z] + one[z].astype(F32)
            return first + (two[z].astype(F32) + three[z].astype(F32))
        own[:, at] = total(zl[0])
        send[:, at] = total(1 - zl[0]).astype(BF)


def hidden_grad(own, one, two, three, h, dy, gain, dh, low, gain_part, block):
    total = total_of(own, one, two, three)
    d_hn, branch = total[:32], total[32:]
    rows = h[...]
    block[...] = (rows + branch).astype(BF)
    scale = row_scale(rows)
    hat = rows * scale
    gain_part[...] = jnp.sum(d_hn * hat, axis=0, keepdims=True)
    grad = dy[:32].astype(F32) + row_norm_grad(d_hn * gain[...], hat, scale)
    dh[...] = grad
    low[...] = grad.astype(BF)


def attend_grad(
    p0, p1, p2, p3, p4, p5, p6, p7, qh, kv0, kv1, kv2, kv3, own_places, places, w, o, l,
    d_attn, d_qh, d_kv0, d_kv1, d_kv2, d_kv3,
):
    rows = jnp.concatenate([p[...] for p in (p0, p1, p2, p3, p4, p5, p6, p7)])
    d_attn[...] = rows
    d_o = dot(rows, w[:, 256:])
    denom = l[...]
    d_inner = (d_o / denom).astype(BF)
    delta = head_sum(d_o * o[...]) / denom
    mine = own_places[...]
    d_q = [0.0, 0.0]
    for i, (kv, d_kv) in enumerate(((kv0, d_kv0), (kv1, d_kv1), (kv2, d_kv2), (kv3, d_kv3))):
        visible = places[:, i * 256 : (i + 1) * 256] <= mine
        k, v = kv[:, :64], kv[:, 64:]
        d_k, d_v = 0.0, 0.0
        for g in range(2):
            at = slice(g * 64, (g + 1) * 64)
            q, di = qh[:, at], d_inner[:, at]
            u = weights_of(q, k, visible)
            ds = (u * (right_product(di, v) - delta[:, g * 64 : g * 64 + 1])).astype(BF)
            d_q[g] = d_q[g] + dot(ds, k)
            d_k = d_k + left_product(ds, q)
            d_v = d_v + left_product(u.astype(BF), di)
        d_kv[...] = jnp.concatenate([d_k * SCALE, d_v], axis=1).astype(d_kv.dtype)
    d_qh[...] = jnp.concatenate(d_q, axis=1) * SCALE


def project_grad(
    d_qh, own, one, two, three, qkv, cosine, sine, qk_gain, w, x_own, x_other, ffn_part,
    d_qkv, send, keep, gains,
):
    d_kv = total_of(own, one, two, three)
    cos, sin = cosine[...], sine[...]
    q, k = qkv[:, :128], qkv[:, 128:]
    q_scale, k_scale = head_scale(q), head_scale(k)
    q_hat, k_hat = q * q_scale, k * k_scale
    d_q = d_qh[...]
    d_qn = d_q * cos - other_half(d_q) * sin
    d_kn = d_kv * cos - other_half(d_kv) * sin
    heads = jnp.concatenate(
        [jnp.sum(d_qn * q_hat, axis=0, keepdims=True), jnp.sum(d_kn * k_hat, axis=0, keepdims=True)]
    )
    d_q = head_norm_grad(d_qn * qk_gain[0:1], q_hat, q_scale)
    d_k = head_norm_grad(d_kn * qk_gain[1:2], k_hat, k_scale)
    d_k = jnp.where(lanes(d_k) < 64, d_k, d_kv)
    low = jnp.concatenate([d_q, d_k], axis=1).astype(BF)
    d_qkv[...] = low
    partial = right_product(low, w[:, :256])
    x = jnp.concatenate([x_own[...], x_other[...]]).astype(F32)
    attn_part = jnp.sum(partial * (x * row_scale(x)), axis=0, keepdims=True)
    def fold(part):
        rows = [part[:, i * 128 : (i + 1) * 128] for i in range(8)]
        return jnp.concatenate(rows + [jnp.zeros((8, 128), F32)])
    heads = jnp.concatenate([heads, jnp.zeros((14, 128), F32)])
    gains[...] = jnp.concatenate([fold(attn_part), fold(ffn_part), heads], axis=1).astype(BF)
    partial = partial.reshape(4, 2, 32, 1024)
    send[...] = partial[:, 1].astype(BF)
    keep[...] = partial[:, 0]


def attend_weights(normed, d_qkv, d_attn, o, gains, dw):
    first = left_product(normed[...], d_qkv[...]).astype(BF)
    second = left_product(d_attn[...], o[...].astype(BF)).astype(BF)
    dw[:, :32, :256] = first.reshape(32, 32, 256)
    dw[:, :32, 256:] = second.reshape(32, 32, 128)
    dw[:, 32:] = jnp.broadcast_to(gains[...][None], (32, 16, 384))


def token_rows(own, one, two, three, dh, x, gain, block, out):
    d_xn = total_of(own, one, two, three)
    rows = x[:32].astype(F32)
    scale = row_scale(rows)
    grad = row_norm_grad(d_xn * gain[...], rows * scale, scale)
    out[:32] = (dh[...] + grad).astype(BF)
    out[32:] = block[...]


def finish_attend(parts, wq, wk, wv, wo, gains):
    sums = [jnp.sum(parts[z].astype(F32), axis=0) for z in range(2)]
    gains[...] = sums[0][32:] + sums[1][32:]
    low, high = sums[0][:32], sums[1][:32]
    wq[...] = jnp.concatenate([low[:, :128], high[:, :128]], axis=1)
    wk[...] = jnp.concatenate([low[:, 128:192], high[:, 128:192]], axis=1)
    wv[...] = jnp.concatenate([low[:, 192:256], high[:, 192:256]], axis=1)
    wo[...] = jnp.concatenate([low[:, 256:], high[:, 256:]], axis=1)


def finish_feed(zl, own, got, wg, wu, wd):
    mine, its = own[...], got[...].astype(F32)
    first = zl[0] == 0
    low, high = jnp.where(first, mine, its), jnp.where(first, its, mine)
    for i, out in enumerate((wg, wu, wd)):
        wide, tail = slice(i * 512, (i + 1) * 512), slice(1536 + i * 64, 1600 + i * 64)
        out[...] = jnp.concatenate(
            [low[:, wide], low[:, tail], high[:, wide], high[:, tail]], axis=1
        )


def add_two(own, one, out):
    out[...] = own[...] + one[...]


def finish_gains(one, two, attn, ffn, query, key):
    total = one[...] + two[...]
    attn[...] = total[:8, :128]
    ffn[...] = total[:8, 128:256]
    query[...] = total[0:1, 256:320] + total[0:1, 320:384]
    key[...] = total[1:2, 256:320]


def prepare(zl, head, wq, wk, wv, wo, wg, wu, wd, tokens, blocks, send_f, keep_f, x_own):
    for z in range(2):
        at = 0
        for w in (wq, wk, wv, wo):
            width = w.shape[1] // 2
            part = w[:, z * width : (z + 1) * width]
            blocks[z, :, :, at : at + width] = jnp.broadcast_to(part[None], (16, 32, width))
            at += width
    pad = jnp.zeros((32, 64), BF)
    sides = []
    for z in range(2):
        parts = [w[:, z * 576 : (z + 1) * 576] for w in (wg, wu, wd)]
        sides.append(
            jnp.concatenate([p[:, :512] for p in parts] + [p[:, 512:] for p in parts] + [pad], axis=1)
        )
    first = zl[0] == 0
    keep_f[...] = jnp.where(first, sides[0], sides[1])
    send_f[...] = jnp.where(first, sides[1], sides[0])
    relative_rows(head, tokens, x_own)


def relative_rows(head, rows, out):
    for k in range(4):
        out[k * 32 : (k + 1) * 32] = rows[0, pl.ds((head[0] ^ k) * 32, 32)]


def order_rows(zl, own, got, *outs):
    for side, out in enumerate(outs):
        at = slice(side * 896, (side + 1) * 896)
        out[zl[0]] = own[:, at]
        out[1 - zl[0]] = got[:, at]


def join_first(*refs):
    for group, (side, z, _, _) in enumerate(GROUPS):
        for k in range(4):
            refs[8 + group][k] = refs[side * 4 + k][z]


def join_second(*refs):
    for own, got, out in zip(refs[:4], refs[4:8], refs[8:]):
        out[0] = own[...]
        out[1] = got[...]


def assemble(place, *refs):
    out = refs[8]
    for group, (side, z, first, second) in enumerate(GROUPS):
        held, got = refs[group], refs[4 + group]
        for i, (near, far) in enumerate(((0, second), (first, 2))):
            for other in range(4):
                for blocks, step in ((held, near), (got, far)):
                    dy_, dx_ = (other, step) if side == 0 else (step, other)
                    at = (place[0] ^ dy_) * 4 + (place[1] ^ dx_)
                    out[z, at, :, side * 896 : (side + 1) * 896] = blocks[i, other]


def swap(value, axes, size, mask):
    return lax.ppermute(value, axes, [(i, i ^ mask) for i in range(size)])


def fan(pieces, axes):
    return [swap(pieces[k], axes, 4, k) for k in (1, 2, 3)]


def sum_pair(send, keep):
    got = swap(send, "c", 2, 1)
    shape = send.shape[1:]
    return call(pair_add, [(shape, F32)] + [(shape, BF)] * 3, keep, got)


def sum_scatter(send, keep):
    own, *rest = sum_pair(send, keep)
    return [own] + fan([None] + rest, Z)


def gather_rows(rows):
    column = [rows] + fan([rows] * 4, Z)
    pieces = []
    for piece in column:
        pieces += [piece, swap(piece, "c", 2, 1)]
    return pieces


def place_rows(head, p0, p1, p2, p3, tokens_grad, block_out):
    for k, piece in enumerate((p0, p1, p2, p3)):
        at = pl.ds((head[0] ^ k) * 32, 32)
        tokens_grad[at] = piece[:32]
        block_out[at] = piece[32:]


def gather_head(rows, head):
    other = swap(rows, "c", 2, 1)
    pieces = [rows, other, swap(rows, "zh", 2, 1), swap(other, "zh", 2, 1)]
    return pl.pallas_call(
        place_rows,
        out_shape=[jax.ShapeDtypeStruct((128, 1024), BF)] * 2,
        in_specs=[pl.BlockSpec(memory_space=pltpu.SMEM)] + [WHOLE] * 4,
        out_specs=[pl.BlockSpec()] * 2,
    )(head.reshape(1), *pieces)


def after(values, *first):
    out = lax.optimization_barrier(tuple(values) + tuple(first))
    return list(out[: len(values)])


def local(
    tokens, positions, attn_gain, ffn_gain, query_gain, key_gain,
    w_query, w_key, w_value, w_out, w_gate, w_up, w_down, cotangent,
):
    zl, y, head = lax.axis_index("zl"), lax.axis_index("y"), lax.axis_index(("zh", "c"))
    attn_gain_row, ffn_gain_row = attn_gain[None], ffn_gain[None]

    zl_ref, head_ref = zl.reshape(1), head.reshape(1)
    place = jnp.stack([y, lax.axis_index("x")])
    side, group = ((2, 32, 896), BF), ((4, 32, 896), BF)
    pairs = ((2, 4, 32, 896), BF)

    def partner(values, turn):
        axes = ("x", "y")
        return [
            swap(value, axes[g[0]], 4, g[2 + turn]) for value, g in zip(values, GROUPS)
        ]

    blocks, send_f, keep_f, x_own = call(
        prepare,
        [((2, 16, 32, 384), BF), ((32, 1792), BF), ((32, 1792), BF), ((128, 1024), BF)],
        *[Far(w) for w in (w_query, w_key, w_value, w_out, w_gate, w_up, w_down, tokens)],
        scalars=(zl_ref, head_ref),
    )
    got_f = swap(send_f, "zl", 2, 1)
    x_other = swap(x_own, "zl", 2, 1)
    w_a = lax.all_to_all(blocks.reshape(1024, 384), PLANE, 0, 0, tiled=True)
    (late_dy,) = after([cotangent], x_own)
    (dy_own,) = call(relative_rows, [((128, 1024), BF)], Far(late_dy), scalars=(head_ref,))
    dy_other = swap(dy_own, "zl", 2, 1)

    sides = call(order_rows, [side, side], keep_f, got_f, scalars=(zl_ref,))
    pieces = [sides[0], *fan([sides[0]] * 4, "y"), sides[1], *fan([sides[1]] * 4, "x")]
    held = call(join_first, [group] * 4, *pieces)

    (late_positions,) = after([positions], blocks)
    steps = jnp.array([dl * 16 + ky * 4 + d for ky in range(4) for dl in range(2) for d in range(4)])
    places = late_positions[0].reshape(32, 32)[steps ^ (zl * 16 + y * 4 + head)].reshape(1024)
    own_places = places[:256]
    frequency = ROPE_BASE ** (-(jnp.arange(32).astype(F32) * 2.0 / 64))
    angles = own_places.astype(F32)[:, None] * frequency
    cosine, sine = jnp.cos(angles), jnp.sin(angles)
    cosine = jnp.concatenate([cosine] * 4, axis=1)
    sine = jnp.concatenate([-sine, sine] * 2, axis=1)
    own_places, places = own_places[:, None], places[None]
    qk_gain = jnp.stack([jnp.tile(query_gain, 2), jnp.tile(key_gain, 2)])

    halves = [((4, 32, 1024), BF), ((4, 32, 1024), F32)]
    flat, wide_flat = ((256, 128), BF), ((256, 128), F32)
    rows_low, rows_high = ((32, 1024), BF), ((32, 1024), F32)
    normed, qh, kv, qkv = call(
        project, [Far(((256, 1024), BF)), flat, flat, Far(((256, 256), F32))],
        x_own, x_other, Far(w_a), attn_gain_row, qk_gain, cosine, sine,
    )
    kvs = [kv] + fan([kv] * 4, "y")
    held = after(held, kv)
    held = call(join_second, [pairs] * 4, *held, *partner(held, 0))
    send, keep, o, l = call(
        attend, halves + [Far(wide_flat)] * 2, qh, *kvs, own_places, places, Far(w_a)
    )
    held = after(held, send)
    w_f = call(
        assemble, [((2, 16, 32, 1792), BF)], *held, *partner(held, 1), scalars=(place,)
    )[0]
    h, hn = call(
        hidden, [Far(rows_high), rows_low], *sum_scatter(send, keep), x_own, ffn_gain_row
    )
    send, keep, hn_all, act, dgu = call(
        feed,
        [((4, 64, 1024), BF), ((4, 64, 1024), F32)]
        + [((256, 1024), BF), ((256, 640), BF), ((256, 1152), BF)],
        *gather_rows(hn), dy_own, dy_other, w_f, room=24,
    )
    pair = sum_pair(send, keep)
    act, dgu = after([act, dgu], *pair)
    d_hn = [pair[0]] + fan([None] + pair[1:], Z)
    groups = call(
        feed_weights, [pairs] * 8, hn_all, dy_own, dy_other, act, dgu, room=24,
        scalars=(place,), scratch=[pltpu.VMEM((2, 16, 32, 1792), BF)],
    )
    sums = call(
        add_first, [group] * 4 + [((4, 32, 896), F32)] * 4, *groups[4:], *partner(groups[:4], 0)
    )
    dh, d_low, ffn_part, block = call(
        hidden_grad, [Far(rows_high), rows_low, Far(((1, 1024), F32)), Far(rows_low)],
        *d_hn, Far(h), dy_own, ffn_gain_row,
    )
    pieces_low = gather_rows(d_low)
    pieces_low = after(pieces_low, sums[4])
    d_attn, d_qh, *d_kvs = call(
        attend_grad, [Far(((256, 1024), BF)), wide_flat, wide_flat, flat, flat, flat],
        *pieces_low, Far(qh), *[Far(t) for t in kvs], own_places, places, Far(w_a), Far(o), Far(l),
    )
    sums = call(
        add_second, [((2, 32, 896), F32), side, side, side] * 2, *sums[4:], *partner(sums[:4], 1)
    )
    (d_qh,) = after([d_qh], sums[0])
    d_qkv, send, keep, gains = call(
        project_grad, [((256, 256), BF)] + halves + [((16, 384), BF)],
        d_qh, d_kvs[0], *fan(d_kvs, "y"), Far(qkv), cosine, sine, qk_gain, Far(w_a),
        Far(x_own), Far(x_other), Far(ffn_part),
    )
    (dw_a,) = call(
        attend_weights, [((32, 48, 384), BF)], Far(normed), d_qkv, Far(d_attn), Far(o), gains
    )
    d_xn = sum_scatter(send, keep)
    last = [sums[0], *fan(sums[:4], "y"), sums[4], *fan(sums[4:], "x")]
    own_f, send_f = call(
        add_third, [((32, 1792), F32), ((32, 1792), BF)], *last, scalars=(zl_ref,)
    )
    grad_wg, grad_wu, grad_wd = call(
        finish_feed, [Far(((32, 1152), F32))] * 3, own_f, swap(send_f, "zl", 2, 1),
        scalars=(zl_ref,),
    )
    (rows,) = call(
        token_rows, [((64, 1024), BF)], *d_xn, Far(dh), x_own, attn_gain_row, Far(block)
    )
    tokens_grad, block_out = gather_head(rows, head)
    tokens_grad, block_out = tokens_grad[None], block_out[None]

    (dw_a,) = after([dw_a], d_xn[0])
    dw_a = lax.all_to_all(dw_a, PLANE, 0, 0, tiled=True)
    grad_wq, grad_wk, grad_wv, grad_wo, gains = call(
        finish_attend,
        [Far(((32, n), F32)) for n in (256, 128, 128, 256)] + [((16, 384), F32)],
        dw_a.reshape(2, 16, 48, 384),
    )
    (gains,) = call(add_two, [((16, 384), F32)], gains, swap(gains, "c", 2, 1))
    attn_sum, ffn_sum, query_sum, key_sum = call(
        finish_gains, [((8, 128), F32)] * 2 + [((1, 64), F32)] * 2,
        gains, swap(gains, "zh", 2, 1),
    )
    return (
        block_out, tokens_grad, attn_sum.reshape(1024), ffn_sum.reshape(1024),
        query_sum.reshape(64), key_sum.reshape(64),
        grad_wq, grad_wk, grad_wv, grad_wo, grad_wg, grad_wu, grad_wd,
    )


def solution(mesh):
    cube = Mesh(mesh.devices.reshape(2, 4, 4, 2, 2), AXES)
    rows = P("x", ("zl", "y"), None)
    weight = P(("zl", "y", "x"), ("zh", "c"))
    return jax.shard_map(
        local,
        mesh=cube,
        in_specs=(rows, P("x", None)) + (P(),) * 4 + (weight,) * 7 + (rows,),
        out_specs=(rows, rows) + (P(),) * 4 + (weight,) * 7,
        check_vma=False,
    )
```

```python
import functools

import jax
import jax.numpy as jnp
from jax import lax
from jax.experimental import pallas as pl
from jax.experimental.pallas import tpu as pltpu
from jax.sharding import Mesh, PartitionSpec as P

EPSILON = 1e-05
ROPE_BASE = 1000000.0
AXES = ("zl", "y", "x", "zh", "c")
Z = ("zl", "zh")
PLANE = ("zl", "y", "x")
BF = jnp.bfloat16
F32 = jnp.float32
SCALE = 64 ** (-0.5)
WHOLE = pl.BlockSpec(memory_space=pltpu.VMEM)


class Far:
    def __init__(self, value):
        self.value = value


class Held:
    def __init__(self, value):
        self.value = value


def spec(item):
    if isinstance(item, Held):
        return pl.BlockSpec(memory_space=pltpu.HBM)
    return pl.BlockSpec() if isinstance(item, Far) else WHOLE


def bare(item):
    return item.value if isinstance(item, (Far, Held)) else item


def call(body, outs, *operands, room=16, scalars=(), scratch=()):
    scalar = pl.BlockSpec(memory_space=pltpu.SMEM)
    return list(
        pl.pallas_call(
            body,
            out_shape=[jax.ShapeDtypeStruct(*bare(out)) for out in outs],
            in_specs=[scalar] * len(scalars) + [spec(item) for item in operands],
            out_specs=[spec(out) for out in outs],
            scratch_shapes=list(scratch),
            compiler_params=pltpu.CompilerParams(vmem_limit_bytes=room * 2**20),
        )(*scalars, *[bare(item) for item in operands])
    )


def dot(left, right):
    return jnp.dot(left, right, preferred_element_type=F32)


def left_product(left, right):
    return lax.dot_general(left, right, (((0,), (0,)), ((), ())), preferred_element_type=F32)


def right_product(left, right):
    return lax.dot_general(left, right, (((1,), (1,)), ((), ())), preferred_element_type=F32)


def row_scale(values):
    return lax.rsqrt(jnp.mean(values * values, axis=-1, keepdims=True) + EPSILON)


def row_norm_grad(grad, normal, scale):
    return scale * (grad - normal * jnp.mean(grad * normal, axis=-1, keepdims=True))


def lanes(values):
    return lax.broadcasted_iota(jnp.int32, values.shape, 1)


def head_sum(values):
    low = lanes(values) < 64
    first = jnp.sum(jnp.where(low, values, 0.0), axis=-1, keepdims=True)
    second = jnp.sum(jnp.where(low, 0.0, values), axis=-1, keepdims=True)
    return jnp.where(low, first, second)


def head_scale(values):
    return lax.rsqrt(head_sum(values * values) * (1.0 / 64) + EPSILON)


def head_norm_grad(grad, normal, scale):
    return scale * (grad - normal * (head_sum(grad * normal) * (1.0 / 64)))


def other_half(values):
    low = (lanes(values) & 63) < 32
    return jnp.where(low, pltpu.roll(values, 96, 1), pltpu.roll(values, 32, 1))


def project(own, other, w, attn_gain, qk_gain, cosine, sine, qh, kv, qkv):
    x = jnp.concatenate([own[...], other[...]]).astype(F32)
    low = (x * row_scale(x) * attn_gain[...]).astype(BF)
    out = dot(low, w[:, :256])
    qkv[...] = out
    q, k = out[:, :128], out[:, 128:]
    cos, sin = cosine[...], sine[...]
    qn = q * head_scale(q) * qk_gain[0:1]
    qh[...] = (qn * cos + other_half(qn) * sin).astype(BF)
    kn = k * head_scale(k) * qk_gain[1:2]
    kr = kn * cos + other_half(kn) * sin
    kv[...] = jnp.where(lanes(k) < 64, kr, k).astype(BF)


def weights_of(q, k, visible):
    scores = right_product(q, k) * SCALE
    return jnp.where(visible, jnp.exp(scores), 0.0)


def attend(qh, kv0, kv1, kv2, kv3, own_places, places, w, send, keep, o_out, l_out):
    sums, totals = [0.0, 0.0], [0.0, 0.0]
    mine = own_places[...]
    for i, kv in enumerate((kv0, kv1, kv2, kv3)):
        visible = places[:, i * 256 : (i + 1) * 256] <= mine
        k, v = kv[:, :64], kv[:, 64:]
        for g in range(2):
            u = weights_of(qh[:, g * 64 : (g + 1) * 64], k, visible)
            totals[g] = totals[g] + jnp.sum(u, axis=-1, keepdims=True)
            sums[g] = sums[g] + dot(u.astype(BF), v)
    o = jnp.concatenate([sums[g] / totals[g] for g in range(2)], axis=1)
    o_out[...] = o
    l_out[...] = jnp.where(lanes(o) < 64, totals[0], totals[1])
    partial = right_product(o.astype(BF), w[:, 256:]).reshape(4, 2, 32, 1024)
    send[...] = partial[:, 1].astype(BF)
    keep[...] = partial[:, 0]


def pair_add(keep, got, own, one, two, three):
    own[...] = keep[0] + got[0].astype(F32)
    for k, out in ((1, one), (2, two), (3, three)):
        out[...] = (keep[k] + got[k].astype(F32)).astype(BF)


def total_of(own, one, two, three):
    return (own[...] + one[...].astype(F32)) + (two[...].astype(F32) + three[...].astype(F32))


def hidden(own, one, two, three, x, gain, h, hn):
    rows = x[:32].astype(F32) + total_of(own, one, two, three)
    h[...] = rows
    hn[...] = (rows * row_scale(rows) * gain[...]).astype(BF)


def feed_parts(gate, up, d_act):
    sig = jax.nn.sigmoid(gate)
    silu = gate * sig
    active = silu * up
    d_gate = d_act * up * sig * (1.0 + gate * (1.0 - sig))
    return active.astype(BF), d_gate, d_act * silu


def feed(
    p0, p1, p2, p3, p4, p5, p6, p7, dy_own, dy_other, w_far,
    send, keep, hn, act, dgu, w, arrived,
):
    copies = []
    for i, (at, width) in enumerate(((0, 1024), (1024, 768))):
        part = (slice(None), slice(None), slice(None), pl.ds(at, width))
        copies.append(pltpu.make_async_copy(w_far.at[part], w.at[part], arrived.at[i]))
        copies[i].start()
    rows = jnp.concatenate([p[...] for p in (p0, p1, p2, p3, p4, p5, p6, p7)])
    hn[...] = rows
    dy = jnp.concatenate([dy_own[...], dy_other[...]])
    def both(left, at, width):
        first, second = left[:, :512], left[:, 512:]
        return dot(first, w[:, 0, :, at : at + width].reshape(512, width)) + dot(
            second, w[:, 1, :, at : at + width].reshape(512, width)
        )
    copies[0].wait()
    gate, up = both(rows, 0, 512), both(rows, 512, 512)
    copies[1].wait()
    d_act = both(dy, 1024, 512)
    active, d_gate, d_up = feed_parts(gate, up, d_act)
    act[:, :512] = active
    d_gate, d_up = d_gate.astype(BF), d_up.astype(BF)
    dgu[:, :512] = d_gate
    dgu[:, 512:1024] = d_up
    tail, d_tail = both(rows, 1536, 128), both(dy, 1664, 128)
    low = lanes(tail) < 64
    gate = jnp.where(low, tail, 0.0)
    up = jnp.where(low, pltpu.roll(tail, 64, 1), 0.0)
    active, dg_tail, du_tail = feed_parts(gate, up, d_tail)
    act[:, 512:] = active
    dgu_tail = jnp.where(low, dg_tail, pltpu.roll(du_tail, 64, 1)).astype(BF)
    dgu[:, 1024:] = dgu_tail
    halves = []
    for z in range(2):
        part = right_product(d_gate, w[:, z, :, :512].reshape(512, 512))
        part = part + right_product(d_up, w[:, z, :, 512:1024].reshape(512, 512))
        part = part + right_product(dgu_tail, w[:, z, :, 1536:1664].reshape(512, 128))
        halves.append(part)
    partial = jnp.concatenate(halves, axis=1).reshape(4, 2, 32, 1024)
    send[:, :32] = partial[:, 1].astype(BF)
    keep[:, :32] = partial[:, 0]
    low_act = act[...]
    halves = []
    for z in range(2):
        part = right_product(low_act[:, :512], w[:, z, :, 1024:1536].reshape(512, 512))
        halves.append(part + right_product(low_act[:, 512:], w[:, z, :, 1664:].reshape(512, 128)))
    partial = jnp.concatenate(halves, axis=1).reshape(4, 2, 32, 1024)
    send[:, 32:] = partial[:, 1].astype(BF)
    keep[:, 32:] = partial[:, 0]


def feed_weights(hn, dy_own, dy_other, act, dgu, out, dw, sent):
    dy = jnp.concatenate([dy_own[...], dy_other[...]])
    rows, active = hn[...], act[...]
    copies = []
    def put(left, right, at, width):
        for z in range(2):
            value = left_product(left[:, z * 512 : (z + 1) * 512], right)
            blocks = value.astype(BF).reshape(4, 4, 32, width)
            for y in range(4):
                dw[:, y, z, :, at : at + width] = blocks[y]
    def leave(at, width):
        part = (slice(None), slice(None), slice(None), slice(None), pl.ds(at, width))
        copies.append(pltpu.make_async_copy(dw.at[part], out.at[part], sent.at[len(copies)]))
        copies[-1].start()
    put(rows, dgu[:, :512], 0, 512)
    leave(0, 512)
    put(rows, dgu[:, 512:1024], 512, 512)
    leave(512, 512)
    put(dy, active[:, :512], 1024, 512)
    leave(1024, 512)
    put(rows, dgu[:, 1024:], 1536, 128)
    put(dy, active[:, 512:], 1664, 128)
    leave(1536, 256)
    for copy in copies:
        copy.wait()


def hidden_grad(own, one, two, three, h, dy, gain, dh, low, gain_part, block):
    total = total_of(own, one, two, three)
    d_hn, branch = total[:32], total[32:]
    rows = h[...]
    block[...] = (rows + branch).astype(BF)
    scale = row_scale(rows)
    hat = rows * scale
    gain_part[...] = jnp.sum(d_hn * hat, axis=0, keepdims=True)
    grad = dy[:32].astype(F32) + row_norm_grad(d_hn * gain[...], hat, scale)
    dh[...] = grad
    low[...] = grad.astype(BF)


def attend_grad(
    p0, p1, p2, p3, p4, p5, p6, p7, qh, kv0, kv1, kv2, kv3, own_places, places, w, o, l,
    d_attn, d_qh, d_kv0, d_kv1, d_kv2, d_kv3,
):
    rows = jnp.concatenate([p[...] for p in (p0, p1, p2, p3, p4, p5, p6, p7)])
    d_attn[...] = rows
    d_o = dot(rows, w[:, 256:])
    denom = l[...]
    d_inner = (d_o / denom).astype(BF)
    delta = head_sum(d_o * o[...]) / denom
    mine = own_places[...]
    d_q = [0.0, 0.0]
    for i, (kv, d_kv) in enumerate(((kv0, d_kv0), (kv1, d_kv1), (kv2, d_kv2), (kv3, d_kv3))):
        visible = places[:, i * 256 : (i + 1) * 256] <= mine
        k, v = kv[:, :64], kv[:, 64:]
        d_k, d_v = 0.0, 0.0
        for g in range(2):
            at = slice(g * 64, (g + 1) * 64)
            q, di = qh[:, at], d_inner[:, at]
            u = weights_of(q, k, visible)
            ds = (u * (right_product(di, v) - delta[:, g * 64 : g * 64 + 1])).astype(BF)
            d_q[g] = d_q[g] + dot(ds, k)
            d_k = d_k + left_product(ds, q)
            d_v = d_v + left_product(u.astype(BF), di)
        d_kv[...] = jnp.concatenate([d_k * SCALE, d_v], axis=1).astype(d_kv.dtype)
    d_qh[...] = jnp.concatenate(d_q, axis=1) * SCALE


def project_grad(
    d_qh, own, one, two, three, qkv, cosine, sine, qk_gain, w, x_own, x_other, ffn_part,
    d_qkv, send, keep, gains,
):
    d_kv = total_of(own, one, two, three)
    cos, sin = cosine[...], sine[...]
    q, k = qkv[:, :128], qkv[:, 128:]
    q_scale, k_scale = head_scale(q), head_scale(k)
    q_hat, k_hat = q * q_scale, k * k_scale
    d_q = d_qh[...]
    d_qn = d_q * cos - other_half(d_q) * sin
    d_kn = d_kv * cos - other_half(d_kv) * sin
    heads = jnp.concatenate(
        [jnp.sum(d_qn * q_hat, axis=0, keepdims=True), jnp.sum(d_kn * k_hat, axis=0, keepdims=True)]
    )
    d_q = head_norm_grad(d_qn * qk_gain[0:1], q_hat, q_scale)
    d_k = head_norm_grad(d_kn * qk_gain[1:2], k_hat, k_scale)
    d_k = jnp.where(lanes(d_k) < 64, d_k, d_kv)
    low = jnp.concatenate([d_q, d_k], axis=1).astype(BF)
    d_qkv[...] = low
    partial = right_product(low, w[:, :256])
    x = jnp.concatenate([x_own[...], x_other[...]]).astype(F32)
    attn_part = jnp.sum(partial * (x * row_scale(x)), axis=0, keepdims=True)
    def fold(part):
        rows = [part[:, i * 128 : (i + 1) * 128] for i in range(8)]
        return jnp.concatenate(rows + [jnp.zeros((8, 128), F32)])
    heads = jnp.concatenate([heads, jnp.zeros((14, 128), F32)])
    gains[...] = jnp.concatenate([fold(attn_part), fold(ffn_part), heads], axis=1).astype(BF)
    partial = partial.reshape(4, 2, 32, 1024)
    send[...] = partial[:, 1].astype(BF)
    keep[...] = partial[:, 0]


def attend_weights(x_own, x_other, attn_gain, d_qkv, d_attn, o, gains, dw):
    x = jnp.concatenate([x_own[...], x_other[...]]).astype(F32)
    normed = (x * row_scale(x) * attn_gain[...]).astype(BF)
    first = left_product(normed, d_qkv[...]).astype(BF)
    second = left_product(d_attn[...], o[...].astype(BF)).astype(BF)
    dw[:, :32, :256] = first.reshape(32, 32, 256)
    dw[:, :32, 256:] = second.reshape(32, 32, 128)
    dw[:, 32:] = jnp.broadcast_to(gains[...][None], (32, 16, 384))


def token_rows(own, one, two, three, dh, x, gain, block, out):
    d_xn = total_of(own, one, two, three)
    rows = x[:32].astype(F32)
    scale = row_scale(rows)
    grad = row_norm_grad(d_xn * gain[...], rows * scale, scale)
    out[:32] = (dh[...] + grad).astype(BF)
    out[32:] = block[...]


def finish_attend(parts, wq, wk, wv, wo, gains):
    sums = [jnp.sum(parts[z].astype(F32), axis=0) for z in range(2)]
    gains[...] = sums[0][32:] + sums[1][32:]
    low, high = sums[0][:32], sums[1][:32]
    wq[...] = jnp.concatenate([low[:, :128], high[:, :128]], axis=1)
    wk[...] = jnp.concatenate([low[:, 128:192], high[:, 128:192]], axis=1)
    wv[...] = jnp.concatenate([low[:, 192:256], high[:, 192:256]], axis=1)
    wo[...] = jnp.concatenate([low[:, 256:], high[:, 256:]], axis=1)


def split_feed(zl, parts, own, send):
    own[...] = parts[pl.ds(zl[0] * 32, 32)]
    send[...] = parts[pl.ds((1 - zl[0]) * 32, 32)]


def finish_feed(zl, own, got, wg, wu, wd):
    mine, its = own[...].astype(F32), got[...].astype(F32)
    first = zl[0] == 0
    low, high = jnp.where(first, mine, its), jnp.where(first, its, mine)
    for i, out in enumerate((wg, wu, wd)):
        wide, tail = slice(i * 512, (i + 1) * 512), slice(1536 + i * 64, 1600 + i * 64)
        out[...] = jnp.concatenate(
            [low[:, wide], low[:, tail], high[:, wide], high[:, tail]], axis=1
        )


def add_two(own, one, out):
    out[...] = own[...] + one[...]


def finish_gains(one, two, attn, ffn, query, key):
    total = one[...] + two[...]
    attn[...] = total[:8, :128]
    ffn[...] = total[:8, 128:256]
    query[...] = total[0:1, 256:320] + total[0:1, 320:384]
    key[...] = total[1:2, 256:320]


def prepare(zl, head, wq, wk, wv, wo, wg, wu, wd, tokens, blocks, send_f, keep_f, x_own):
    for z in range(2):
        at = 0
        for w in (wq, wk, wv, wo):
            width = w.shape[1] // 2
            part = w[:, z * width : (z + 1) * width]
            blocks[z, :, :, at : at + width] = jnp.broadcast_to(part[None], (16, 32, width))
            at += width
    pad = jnp.zeros((32, 64), BF)
    sides = []
    for z in range(2):
        parts = [w[:, z * 576 : (z + 1) * 576] for w in (wg, wu, wd)]
        sides.append(
            jnp.concatenate([p[:, :512] for p in parts] + [p[:, 512:] for p in parts] + [pad], axis=1)
        )
    first = zl[0] == 0
    keep_f[...] = jnp.where(first, sides[0], sides[1])
    send_f[...] = jnp.where(first, sides[1], sides[0])
    relative_rows(head, tokens, x_own)


def relative_rows(head, rows, out):
    for k in range(4):
        out[k * 32 : (k + 1) * 32] = rows[0, pl.ds((head[0] ^ k) * 32, 32)]


def order_rows(zl, own, got, out):
    out[zl[0]] = own[...]
    out[1 - zl[0]] = got[...]


def swap(value, axes, size, mask):
    return lax.ppermute(value, axes, [(i, i ^ mask) for i in range(size)])


def fan(pieces, axes):
    return [swap(pieces[k], axes, 4, k) for k in (1, 2, 3)]


def sum_pair(send, keep):
    got = swap(send, "c", 2, 1)
    shape = send.shape[1:]
    return call(pair_add, [(shape, F32)] + [(shape, BF)] * 3, keep, got)


def sum_scatter(send, keep):
    own, *rest = sum_pair(send, keep)
    return [own] + fan([None] + rest, Z)


def gather_rows(rows):
    column = [rows] + fan([rows] * 4, Z)
    pieces = []
    for piece in column:
        pieces += [piece, swap(piece, "c", 2, 1)]
    return pieces


def place_rows(head, p0, p1, p2, p3, tokens_grad, block_out):
    for k, piece in enumerate((p0, p1, p2, p3)):
        at = pl.ds((head[0] ^ k) * 32, 32)
        tokens_grad[at] = piece[:32]
        block_out[at] = piece[32:]


def gather_head(rows, head):
    other = swap(rows, "c", 2, 1)
    pieces = [rows, other, swap(rows, "zh", 2, 1), swap(other, "zh", 2, 1)]
    return pl.pallas_call(
        place_rows,
        out_shape=[jax.ShapeDtypeStruct((128, 1024), BF)] * 2,
        in_specs=[pl.BlockSpec(memory_space=pltpu.SMEM)] + [WHOLE] * 4,
        out_specs=[pl.BlockSpec()] * 2,
    )(head.reshape(1), *pieces)


def after(values, *first):
    out = lax.optimization_barrier(tuple(values) + tuple(first))
    return list(out[: len(values)])


def local(
    tokens, positions, attn_gain, ffn_gain, query_gain, key_gain,
    w_query, w_key, w_value, w_out, w_gate, w_up, w_down, cotangent,
):
    zl, y, head = lax.axis_index("zl"), lax.axis_index("y"), lax.axis_index(("zh", "c"))
    attn_gain_row, ffn_gain_row = attn_gain[None], ffn_gain[None]

    zl_ref, head_ref = zl.reshape(1), head.reshape(1)
    blocks, send_f, keep_f, x_own = call(
        prepare,
        [((2, 16, 32, 384), BF), ((32, 1792), BF), ((32, 1792), BF), ((128, 1024), BF)],
        *[Far(w) for w in (w_query, w_key, w_value, w_out, w_gate, w_up, w_down, tokens)],
        scalars=(zl_ref, head_ref),
    )
    got_f = swap(send_f, "zl", 2, 1)
    x_other = swap(x_own, "zl", 2, 1)
    w_a = lax.all_to_all(blocks.reshape(1024, 384), PLANE, 0, 0, tiled=True)
    (rows_f,) = call(order_rows, [Far(((2, 32, 1792), BF))], keep_f, got_f, scalars=(zl_ref,))
    w_f = lax.all_gather(rows_f, ("y", "x"), axis=0)

    (late_dy,) = after([cotangent], x_own)
    (dy_own,) = call(relative_rows, [((128, 1024), BF)], Far(late_dy), scalars=(head_ref,))
    dy_other = swap(dy_own, "zl", 2, 1)
    (x_late,) = after([x_own], dy_other)

    (late_positions,) = after([positions], blocks)
    steps = jnp.array([dl * 16 + ky * 4 + d for ky in range(4) for dl in range(2) for d in range(4)])
    places = late_positions[0].reshape(32, 32)[steps ^ (zl * 16 + y * 4 + head)].reshape(1024)
    own_places = places[:256]
    frequency = ROPE_BASE ** (-(jnp.arange(32).astype(F32) * 2.0 / 64))
    angles = own_places.astype(F32)[:, None] * frequency
    cosine, sine = jnp.cos(angles), jnp.sin(angles)
    cosine = jnp.concatenate([cosine] * 4, axis=1)
    sine = jnp.concatenate([-sine, sine] * 2, axis=1)
    own_places, places = own_places[:, None], places[None]
    qk_gain = jnp.stack([jnp.tile(query_gain, 2), jnp.tile(key_gain, 2)])

    halves = [((4, 32, 1024), BF), ((4, 32, 1024), F32)]
    flat, wide_flat = ((256, 128), BF), ((256, 128), F32)
    rows_low, rows_high = ((32, 1024), BF), ((32, 1024), F32)
    qh, kv, qkv = call(
        project, [flat, flat, Far(((256, 256), F32))],
        x_late, x_other, Far(w_a), attn_gain_row, qk_gain, cosine, sine,
    )
    kvs = [kv] + fan([kv] * 4, "y")
    send, keep, o, l = call(
        attend, halves + [Far(wide_flat)] * 2, qh, *kvs, own_places, places, Far(w_a)
    )
    h, hn = call(
        hidden, [Far(rows_high), rows_low], *sum_scatter(send, keep), x_own, ffn_gain_row
    )
    send, keep, hn_all, act, dgu = call(
        feed,
        [((4, 64, 1024), BF), ((4, 64, 1024), F32)]
        + [((256, 1024), BF), ((256, 640), BF), ((256, 1152), BF)],
        *gather_rows(hn), dy_own, dy_other, Held(w_f), room=24,
        scratch=[pltpu.VMEM((16, 2, 32, 1792), BF), pltpu.SemaphoreType.DMA((2,))],
    )
    pair = sum_pair(send, keep)
    act, dgu = after([act, dgu], *pair)
    d_hn = [pair[0]] + fan([None] + pair[1:], Z)
    (dw_f,) = call(
        feed_weights, [Held(((4, 4, 2, 32, 1792), BF))], hn_all, dy_own, dy_other, act, dgu, room=24,
        scratch=[pltpu.VMEM((4, 4, 2, 32, 1792), BF), pltpu.SemaphoreType.DMA((4,))],
    )
    dw_f = lax.psum_scatter(dw_f.reshape(1024, 1792), "x", scatter_dimension=0, tiled=True)
    dh, d_low, ffn_part, block = call(
        hidden_grad, [Far(rows_high), rows_low, Far(((1, 1024), F32)), Far(rows_low)],
        *d_hn, Far(h), dy_own, ffn_gain_row,
    )
    d_attn, d_qh, *d_kvs = call(
        attend_grad, [Far(((256, 1024), BF)), wide_flat, wide_flat, flat, flat, flat],
        *gather_rows(d_low), Far(qh), *[Far(t) for t in kvs], own_places, places, Far(w_a), Far(o), Far(l),
    )
    d_qkv, send, keep, gains = call(
        project_grad, [((256, 256), BF)] + halves + [((16, 384), BF)],
        d_qh, d_kvs[0], *fan(d_kvs, "y"), Far(qkv), cosine, sine, qk_gain, Far(w_a),
        Far(x_own), Far(x_other), Far(ffn_part),
    )
    (dw_a,) = call(
        attend_weights, [((32, 48, 384), BF)],
        Far(x_own), Far(x_other), attn_gain_row, d_qkv, Far(d_attn), Far(o), gains,
    )
    own, *rest = sum_pair(send, keep)
    dw_a, dw_f = after([dw_a, dw_f], own)
    dw_half = dw_f
    dw_f = lax.psum_scatter(dw_f, "y", scatter_dimension=0, tiled=True)
    dw_a = lax.all_to_all(dw_a, PLANE, 0, 0, tiled=True)
    d_xn = after([own] + fan([None] + rest, Z), dw_half)
    (rows,) = call(
        token_rows, [((64, 1024), BF)], *d_xn, Far(dh), x_own, attn_gain_row, Far(block)
    )
    tokens_grad, block_out = gather_head(rows, head)
    tokens_grad, block_out = tokens_grad[None], block_out[None]

    (dw_a,) = after([dw_a], rows)
    grad_wq, grad_wk, grad_wv, grad_wo, gains = call(
        finish_attend,
        [Far(((32, n), F32)) for n in (256, 128, 128, 256)] + [((16, 384), F32)],
        dw_a.reshape(2, 16, 48, 384),
    )
    (dw_f,) = after([dw_f], gains)
    (gains,) = call(add_two, [((16, 384), F32)], gains, swap(gains, "c", 2, 1))
    attn_sum, ffn_sum, query_sum, key_sum = call(
        finish_gains, [((8, 128), F32)] * 2 + [((1, 64), F32)] * 2,
        gains, swap(gains, "zh", 2, 1),
    )
    own_f, send_f = call(
        split_feed, [((32, 1792), BF)] * 2, Far(dw_f), scalars=(zl_ref,)
    )
    grad_wg, grad_wu, grad_wd = call(
        finish_feed, [Far(((32, 1152), F32))] * 3, own_f, swap(send_f, "zl", 2, 1),
        scalars=(zl_ref,),
    )
    return (
        block_out, tokens_grad, attn_sum.reshape(1024), ffn_sum.reshape(1024),
        query_sum.reshape(64), key_sum.reshape(64),
        grad_wq, grad_wk, grad_wv, grad_wo, grad_wg, grad_wu, grad_wd,
    )


def solution(mesh):
    cube = Mesh(mesh.devices.reshape(2, 4, 4, 2, 2), AXES)
    rows = P("x", ("zl", "y"), None)
    weight = P(("zl", "y", "x"), ("zh", "c"))
    return jax.shard_map(
        local,
        mesh=cube,
        in_specs=(rows, P("x", None)) + (P(),) * 4 + (weight,) * 7 + (rows,),
        out_specs=(rows, rows) + (P(),) * 4 + (weight,) * 7,
        check_vma=False,
    )
```

```python
import functools

import jax
import jax.numpy as jnp
from jax import lax
from jax.experimental import pallas as pl
from jax.experimental.pallas import tpu as pltpu
from jax.sharding import Mesh, PartitionSpec as P

EPSILON = 1e-05
ROPE_BASE = 1000000.0
AXES = ("zl", "y", "x", "zh", "c")
Z = ("zl", "zh")
PLANE = ("zl", "y", "x")
BF = jnp.bfloat16
F32 = jnp.float32
SCALE = 64 ** (-0.5)
WHOLE = pl.BlockSpec(memory_space=pltpu.VMEM)


class Far:
    def __init__(self, value):
        self.value = value


def spec(item):
    return pl.BlockSpec() if isinstance(item, Far) else WHOLE


def bare(item):
    return item.value if isinstance(item, Far) else item


def call(body, outs, *operands, room=8, scalars=(), scratch=()):
    scalar = pl.BlockSpec(memory_space=pltpu.SMEM)
    return list(
        pl.pallas_call(
            body,
            out_shape=[jax.ShapeDtypeStruct(*bare(out)) for out in outs],
            in_specs=[scalar] * len(scalars) + [spec(item) for item in operands],
            out_specs=[spec(out) for out in outs],
            scratch_shapes=list(scratch),
            compiler_params=pltpu.CompilerParams(vmem_limit_bytes=room * 2**20 if room else None),
        )(*scalars, *[bare(item) for item in operands])
    )


def dot(left, right):
    return jnp.dot(left, right, preferred_element_type=F32)


def left_product(left, right):
    return lax.dot_general(left, right, (((0,), (0,)), ((), ())), preferred_element_type=F32)


def right_product(left, right):
    return lax.dot_general(left, right, (((1,), (1,)), ((), ())), preferred_element_type=F32)


def row_scale(values):
    return lax.rsqrt(jnp.mean(values * values, axis=-1, keepdims=True) + EPSILON)


def row_norm_grad(grad, normal, scale):
    return scale * (grad - normal * jnp.mean(grad * normal, axis=-1, keepdims=True))


def lanes(values):
    return lax.broadcasted_iota(jnp.int32, values.shape, 1)


def head_sum(values):
    low = lanes(values) < 64
    first = jnp.sum(jnp.where(low, values, 0.0), axis=-1, keepdims=True)
    second = jnp.sum(jnp.where(low, 0.0, values), axis=-1, keepdims=True)
    return jnp.where(low, first, second)


def head_scale(values):
    return lax.rsqrt(head_sum(values * values) * (1.0 / 64) + EPSILON)


def head_norm_grad(grad, normal, scale):
    return scale * (grad - normal * (head_sum(grad * normal) * (1.0 / 64)))


def other_half(values):
    low = (lanes(values) & 63) < 32
    return jnp.where(low, pltpu.roll(values, 96, 1), pltpu.roll(values, 32, 1))


def project(own, other, w, attn_gain, qk_gain, cosine, sine, qh, kv, qkv):
    x = jnp.concatenate([own[...], other[...]]).astype(F32)
    low = (x * row_scale(x) * attn_gain[...]).astype(BF)
    out = dot(low, w[:, :256])
    qkv[...] = out
    q, k = out[:, :128], out[:, 128:]
    cos, sin = cosine[...], sine[...]
    qn = q * head_scale(q) * qk_gain[0:1]
    qh[...] = (qn * cos + other_half(qn) * sin).astype(BF)
    kn = k * head_scale(k) * qk_gain[1:2]
    kr = kn * cos + other_half(kn) * sin
    kv[...] = jnp.where(lanes(k) < 64, kr, k).astype(BF)


def weights_of(q, k, visible):
    scores = right_product(q, k) * SCALE
    return jnp.where(visible, jnp.exp(scores), 0.0)


def attend(qh, kv0, kv1, kv2, kv3, own_places, places, w, send, keep, o_out, l_out):
    sums, totals = [0.0, 0.0], [0.0, 0.0]
    mine = own_places[...]
    for i, kv in enumerate((kv0, kv1, kv2, kv3)):
        visible = places[:, i * 256 : (i + 1) * 256] <= mine
        k, v = kv[:, :64], kv[:, 64:]
        for g in range(2):
            u = weights_of(qh[:, g * 64 : (g + 1) * 64], k, visible)
            totals[g] = totals[g] + jnp.sum(u, axis=-1, keepdims=True)
            sums[g] = sums[g] + dot(u.astype(BF), v)
    o = jnp.concatenate([sums[g] / totals[g] for g in range(2)], axis=1)
    o_out[...] = o
    l_out[...] = jnp.where(lanes(o) < 64, totals[0], totals[1])
    partial = right_product(o.astype(BF), w[:, 256:]).reshape(4, 2, 32, 1024)
    send[...] = partial[:, 1].astype(BF)
    keep[...] = partial[:, 0]


def pair_add(keep, got, own, one, two, three):
    own[...] = keep[0] + got[0].astype(F32)
    for k, out in ((1, one), (2, two), (3, three)):
        out[...] = (keep[k] + got[k].astype(F32)).astype(BF)


def total_of(own, one, two, three):
    return (own[...] + one[...].astype(F32)) + (two[...].astype(F32) + three[...].astype(F32))


def hidden(own, one, two, three, x, gain, h, hn):
    rows = x[:32].astype(F32) + total_of(own, one, two, three)
    h[...] = rows
    hn[...] = (rows * row_scale(rows) * gain[...]).astype(BF)


def feed_parts(gate, up, d_act):
    sig = jax.nn.sigmoid(gate)
    silu = gate * sig
    active = silu * up
    d_gate = d_act * up * sig * (1.0 + gate * (1.0 - sig))
    return active.astype(BF), d_gate, d_act * silu


def feed(
    p0, p1, p2, p3, p4, p5, p6, p7, dy_own, dy_other, w,
    send, keep, hn, act, dgu,
):
    rows = jnp.concatenate([p[...] for p in (p0, p1, p2, p3, p4, p5, p6, p7)])
    hn[...] = rows
    dy = jnp.concatenate([dy_own[...], dy_other[...]])
    def both(left, at, width):
        first, second = left[:, :512], left[:, 512:]
        return dot(first, w[:, 0, :, at : at + width].reshape(512, width)) + dot(
            second, w[:, 1, :, at : at + width].reshape(512, width)
        )
    gate, up, d_act = both(rows, 0, 512), both(rows, 512, 512), both(dy, 1024, 512)
    active, d_gate, d_up = feed_parts(gate, up, d_act)
    act[:, :512] = active
    d_gate, d_up = d_gate.astype(BF), d_up.astype(BF)
    dgu[:, :512] = d_gate
    dgu[:, 512:1024] = d_up
    tail, d_tail = both(rows, 1536, 128), both(dy, 1664, 128)
    low = lanes(tail) < 64
    gate = jnp.where(low, tail, 0.0)
    up = jnp.where(low, pltpu.roll(tail, 64, 1), 0.0)
    active, dg_tail, du_tail = feed_parts(gate, up, d_tail)
    act[:, 512:] = active
    dgu_tail = jnp.where(low, dg_tail, pltpu.roll(du_tail, 64, 1)).astype(BF)
    dgu[:, 1024:] = dgu_tail
    halves = []
    for z in range(2):
        part = right_product(d_gate, w[:, z, :, :512].reshape(512, 512))
        part = part + right_product(d_up, w[:, z, :, 512:1024].reshape(512, 512))
        part = part + right_product(dgu_tail, w[:, z, :, 1536:1664].reshape(512, 128))
        halves.append(part)
    partial = jnp.concatenate(halves, axis=1).reshape(4, 2, 32, 1024)
    send[:, :32] = partial[:, 1].astype(BF)
    keep[:, :32] = partial[:, 0]
    low_act = act[...]
    halves = []
    for z in range(2):
        part = right_product(low_act[:, :512], w[:, z, :, 1024:1536].reshape(512, 512))
        halves.append(part + right_product(low_act[:, 512:], w[:, z, :, 1664:].reshape(512, 128)))
    partial = jnp.concatenate(halves, axis=1).reshape(4, 2, 32, 1024)
    send[:, 32:] = partial[:, 1].astype(BF)
    keep[:, 32:] = partial[:, 0]


def feed_weights(hn, dy_own, dy_other, act, dgu, dw):
    dy = jnp.concatenate([dy_own[...], dy_other[...]])
    rows, active = hn[...], act[...]
    def put(left, right, at, width):
        for z in range(2):
            value = left_product(left[:, z * 512 : (z + 1) * 512], right)
            blocks = value.astype(BF).reshape(4, 4, 32, width)
            for y in range(4):
                dw[:, z, y, :, at : at + width] = blocks[y]
    put(rows, dgu[:, :512], 0, 512)
    put(rows, dgu[:, 512:1024], 512, 512)
    put(dy, active[:, :512], 1024, 512)
    put(rows, dgu[:, 1024:], 1536, 128)
    put(dy, active[:, 512:], 1664, 128)


def hidden_grad(own, one, two, three, h, dy, gain, dh, low, gain_part, block):
    total = total_of(own, one, two, three)
    d_hn, branch = total[:32], total[32:]
    rows = h[...]
    block[...] = (rows + branch).astype(BF)
    scale = row_scale(rows)
    hat = rows * scale
    gain_part[...] = jnp.sum(d_hn * hat, axis=0, keepdims=True)
    grad = dy[:32].astype(F32) + row_norm_grad(d_hn * gain[...], hat, scale)
    dh[...] = grad
    low[...] = grad.astype(BF)


def attend_grad(
    p0, p1, p2, p3, p4, p5, p6, p7, qh, kv0, kv1, kv2, kv3, own_places, places, w, o, l,
    d_attn, d_qh, d_kv0, d_kv1, d_kv2, d_kv3,
):
    rows = jnp.concatenate([p[...] for p in (p0, p1, p2, p3, p4, p5, p6, p7)])
    d_attn[...] = rows
    d_o = dot(rows, w[:, 256:])
    denom = l[...]
    d_inner = (d_o / denom).astype(BF)
    delta = head_sum(d_o * o[...]) / denom
    mine = own_places[...]
    d_q = [0.0, 0.0]
    for i, (kv, d_kv) in enumerate(((kv0, d_kv0), (kv1, d_kv1), (kv2, d_kv2), (kv3, d_kv3))):
        visible = places[:, i * 256 : (i + 1) * 256] <= mine
        k, v = kv[:, :64], kv[:, 64:]
        d_k, d_v = 0.0, 0.0
        for g in range(2):
            at = slice(g * 64, (g + 1) * 64)
            q, di = qh[:, at], d_inner[:, at]
            u = weights_of(q, k, visible)
            ds = (u * (right_product(di, v) - delta[:, g * 64 : g * 64 + 1])).astype(BF)
            d_q[g] = d_q[g] + dot(ds, k)
            d_k = d_k + left_product(ds, q)
            d_v = d_v + left_product(u.astype(BF), di)
        d_kv[...] = jnp.concatenate([d_k * SCALE, d_v], axis=1).astype(d_kv.dtype)
    d_qh[...] = jnp.concatenate(d_q, axis=1) * SCALE


def project_grad(
    d_qh, own, one, two, three, qkv, cosine, sine, qk_gain, w, x_own, x_other, ffn_part,
    d_qkv, send, keep, gains,
):
    d_kv = total_of(own, one, two, three)
    cos, sin = cosine[...], sine[...]
    q, k = qkv[:, :128], qkv[:, 128:]
    q_scale, k_scale = head_scale(q), head_scale(k)
    q_hat, k_hat = q * q_scale, k * k_scale
    d_q = d_qh[...]
    d_qn = d_q * cos - other_half(d_q) * sin
    d_kn = d_kv * cos - other_half(d_kv) * sin
    heads = jnp.concatenate(
        [jnp.sum(d_qn * q_hat, axis=0, keepdims=True), jnp.sum(d_kn * k_hat, axis=0, keepdims=True)]
    )
    d_q = head_norm_grad(d_qn * qk_gain[0:1], q_hat, q_scale)
    d_k = head_norm_grad(d_kn * qk_gain[1:2], k_hat, k_scale)
    d_k = jnp.where(lanes(d_k) < 64, d_k, d_kv)
    low = jnp.concatenate([d_q, d_k], axis=1).astype(BF)
    d_qkv[...] = low
    partial = right_product(low, w[:, :256])
    x = jnp.concatenate([x_own[...], x_other[...]]).astype(F32)
    attn_part = jnp.sum(partial * (x * row_scale(x)), axis=0, keepdims=True)
    def fold(part):
        rows = [part[:, i * 128 : (i + 1) * 128] for i in range(8)]
        return jnp.concatenate(rows + [jnp.zeros((8, 128), F32)])
    heads = jnp.concatenate([heads, jnp.zeros((14, 128), F32)])
    gains[...] = jnp.concatenate([fold(attn_part), fold(ffn_part), heads], axis=1).astype(BF)
    partial = partial.reshape(4, 2, 32, 1024)
    send[...] = partial[:, 1].astype(BF)
    keep[...] = partial[:, 0]


def attend_weights(x_own, x_other, attn_gain, d_qkv, d_attn, o, gains, dw):
    x = jnp.concatenate([x_own[...], x_other[...]]).astype(F32)
    normed = (x * row_scale(x) * attn_gain[...]).astype(BF)
    first = left_product(normed, d_qkv[...]).astype(BF)
    second = left_product(d_attn[...], o[...].astype(BF)).astype(BF)
    dw[:, :32, :256] = first.reshape(32, 32, 256)
    dw[:, :32, 256:] = second.reshape(32, 32, 128)
    dw[:, 32:] = jnp.broadcast_to(gains[...][None], (32, 16, 384))


def token_rows(own, one, two, three, dh, x, gain, block, out):
    d_xn = total_of(own, one, two, three)
    rows = x[:32].astype(F32)
    scale = row_scale(rows)
    grad = row_norm_grad(d_xn * gain[...], rows * scale, scale)
    out[:32] = (dh[...] + grad).astype(BF)
    out[32:] = block[...]


def finish_attend(parts, wq, wk, wv, wo, gains):
    sums = [jnp.sum(parts[z].astype(F32), axis=0) for z in range(2)]
    gains[...] = sums[0][32:] + sums[1][32:]
    low, high = sums[0][:32], sums[1][:32]
    wq[...] = jnp.concatenate([low[:, :128], high[:, :128]], axis=1)
    wk[...] = jnp.concatenate([low[:, 128:192], high[:, 128:192]], axis=1)
    wv[...] = jnp.concatenate([low[:, 192:256], high[:, 192:256]], axis=1)
    wo[...] = jnp.concatenate([low[:, 256:], high[:, 256:]], axis=1)


def finish_feed(parts, wg, wu, wd):
    low = jnp.sum(parts[0].astype(F32), axis=0)
    high = jnp.sum(parts[1].astype(F32), axis=0)
    for i, out in enumerate((wg, wu, wd)):
        wide, tail = slice(i * 512, (i + 1) * 512), slice(1536 + i * 64, 1600 + i * 64)
        out[...] = jnp.concatenate(
            [low[:, wide], low[:, tail], high[:, wide], high[:, tail]], axis=1
        )


def add_two(own, one, out):
    out[...] = own[...] + one[...]


def finish_gains(one, two, attn, ffn, query, key):
    total = one[...] + two[...]
    attn[...] = total[:8, :128]
    ffn[...] = total[:8, 128:256]
    query[...] = total[0:1, 256:320] + total[0:1, 320:384]
    key[...] = total[1:2, 256:320]


def prepare(zl, head, wq, wk, wv, wo, wg, wu, wd, tokens, blocks, send_f, keep_f, x_own):
    for z in range(2):
        at = 0
        for w in (wq, wk, wv, wo):
            width = w.shape[1] // 2
            part = w[:, z * width : (z + 1) * width]
            blocks[z, :, :, at : at + width] = jnp.broadcast_to(part[None], (16, 32, width))
            at += width
    pad = jnp.zeros((32, 64), BF)
    sides = []
    for z in range(2):
        parts = [w[:, z * 576 : (z + 1) * 576] for w in (wg, wu, wd)]
        sides.append(
            jnp.concatenate([p[:, :512] for p in parts] + [p[:, 512:] for p in parts] + [pad], axis=1)
        )
    first = zl[0] == 0
    keep_f[...] = jnp.where(first, sides[0], sides[1])
    send_f[...] = jnp.where(first, sides[1], sides[0])
    relative_rows(head, tokens, x_own)


def relative_rows(head, rows, out):
    for k in range(4):
        out[k * 32 : (k + 1) * 32] = rows[0, pl.ds((head[0] ^ k) * 32, 32)]


def order_rows(zl, own, got, out):
    out[zl[0]] = own[...]
    out[1 - zl[0]] = got[...]


def swap(value, axes, size, mask):
    return lax.ppermute(value, axes, [(i, i ^ mask) for i in range(size)])


def fan(pieces, axes):
    return [swap(pieces[k], axes, 4, k) for k in (1, 2, 3)]


def sum_pair(send, keep):
    got = swap(send, "c", 2, 1)
    shape = send.shape[1:]
    return call(pair_add, [(shape, F32)] + [(shape, BF)] * 3, keep, got)


def sum_scatter(send, keep):
    own, *rest = sum_pair(send, keep)
    return [own] + fan([None] + rest, Z)


def gather_rows(rows):
    column = [rows] + fan([rows] * 4, Z)
    pieces = []
    for piece in column:
        pieces += [piece, swap(piece, "c", 2, 1)]
    return pieces


def place_rows(head, p0, p1, p2, p3, tokens_grad, block_out):
    for k, piece in enumerate((p0, p1, p2, p3)):
        at = pl.ds((head[0] ^ k) * 32, 32)
        tokens_grad[at] = piece[:32]
        block_out[at] = piece[32:]


def gather_head(rows, head):
    other = swap(rows, "c", 2, 1)
    pieces = [rows, other, swap(rows, "zh", 2, 1), swap(other, "zh", 2, 1)]
    return call(place_rows, [Far(((128, 1024), BF))] * 2, *pieces, scalars=(head.reshape(1),))


def after(values, *first):
    out = lax.optimization_barrier(tuple(values) + tuple(first))
    return list(out[: len(values)])


def local(
    tokens, positions, attn_gain, ffn_gain, query_gain, key_gain,
    w_query, w_key, w_value, w_out, w_gate, w_up, w_down, cotangent,
):
    zl, y, head = lax.axis_index("zl"), lax.axis_index("y"), lax.axis_index(("zh", "c"))
    attn_gain_row, ffn_gain_row = attn_gain[None], ffn_gain[None]

    zl_ref, head_ref = zl.reshape(1), head.reshape(1)
    blocks, send_f, keep_f, x_own = call(
        prepare,
        [((2, 16, 32, 384), BF), ((32, 1792), BF), ((32, 1792), BF), ((128, 1024), BF)],
        *[Far(w) for w in (w_query, w_key, w_value, w_out, w_gate, w_up, w_down, tokens)],
        scalars=(zl_ref, head_ref), room=None,
    )
    got_f = swap(send_f, "zl", 2, 1)
    x_other = swap(x_own, "zl", 2, 1)
    w_a = lax.all_to_all(blocks.reshape(1024, 384), PLANE, 0, 0, tiled=True)
    (rows_f,) = call(order_rows, [Far(((2, 32, 1792), BF))], keep_f, got_f, scalars=(zl_ref,))
    w_f = lax.all_gather(rows_f, ("y", "x"), axis=0)

    (late_positions,) = after([positions], blocks)
    steps = jnp.array([dl * 16 + ky * 4 + d for ky in range(4) for dl in range(2) for d in range(4)])
    places = late_positions[0].reshape(32, 32)[steps ^ (zl * 16 + y * 4 + head)].reshape(1024)
    own_places = places[:256]
    frequency = ROPE_BASE ** (-(jnp.arange(32).astype(F32) * 2.0 / 64))
    angles = own_places.astype(F32)[:, None] * frequency
    cosine, sine = jnp.cos(angles), jnp.sin(angles)
    cosine = jnp.concatenate([cosine] * 4, axis=1)
    sine = jnp.concatenate([-sine, sine] * 2, axis=1)
    own_places, places = own_places[:, None], places[None]
    qk_gain = jnp.stack([jnp.tile(query_gain, 2), jnp.tile(key_gain, 2)])

    halves = [((4, 32, 1024), BF), ((4, 32, 1024), F32)]
    flat, wide_flat = ((256, 128), BF), ((256, 128), F32)
    rows_low, rows_high = ((32, 1024), BF), ((32, 1024), F32)
    qh, kv, qkv = call(
        project, [flat, flat, Far(((256, 256), F32))],
        x_own, x_other, Far(w_a), attn_gain_row, qk_gain, cosine, sine,
    )
    (late_dy,) = after([cotangent], kv)
    (dy_own,) = call(relative_rows, [((128, 1024), BF)], Far(late_dy), scalars=(head_ref,))
    dy_other = swap(dy_own, "zl", 2, 1)
    kvs = [kv] + fan([kv] * 4, "y")
    (qh,) = after([qh], dy_other)
    send, keep, o, l = call(
        attend, halves + [Far(wide_flat)] * 2, qh, *kvs, own_places, places, Far(w_a)
    )
    h, hn = call(
        hidden, [Far(rows_high), rows_low], *sum_scatter(send, keep), x_own, ffn_gain_row
    )
    send, keep, hn_all, act, dgu = call(
        feed,
        [((4, 64, 1024), BF), ((4, 64, 1024), F32)]
        + [((256, 1024), BF), ((256, 640), BF), ((256, 1152), BF)],
        *gather_rows(hn), dy_own, dy_other, w_f,
    )
    pair = sum_pair(send, keep)
    act, dgu = after([act, dgu], *pair)
    d_hn = [pair[0]] + fan([None] + pair[1:], Z)
    (dw_f,) = call(
        feed_weights, [Far(((4, 2, 4, 32, 1792), BF))], hn_all, dy_own, dy_other, act, dgu
    )
    dw_f = lax.psum_scatter(dw_f.reshape(1024, 1792), "x", scatter_dimension=0, tiled=True)
    dh, d_low, ffn_part, block = call(
        hidden_grad, [Far(rows_high), rows_low, Far(((1, 1024), F32)), Far(rows_low)],
        *d_hn, Far(h), dy_own, ffn_gain_row,
    )
    d_attn, d_qh, *d_kvs = call(
        attend_grad, [Far(((256, 1024), BF)), wide_flat, wide_flat, flat, flat, flat],
        *gather_rows(d_low), Far(qh), *[Far(t) for t in kvs], own_places, places, Far(w_a), Far(o), Far(l),
    )
    d_qkv, send, keep, gains = call(
        project_grad, [((256, 256), BF)] + halves + [((16, 384), BF)],
        d_qh, d_kvs[0], *fan(d_kvs, "y"), Far(qkv), cosine, sine, qk_gain, Far(w_a),
        Far(x_own), Far(x_other), Far(ffn_part),
    )
    (dw_a,) = call(
        attend_weights, [((32, 48, 384), BF)],
        Far(x_own), Far(x_other), attn_gain_row, d_qkv, Far(d_attn), Far(o), gains,
    )
    own, *rest = sum_pair(send, keep)
    (dw_a,) = after([dw_a], own)
    dw_a = lax.all_to_all(dw_a, PLANE, 0, 0, tiled=True)
    d_xn = [own] + fan([None] + rest, Z)
    (rows,) = call(
        token_rows, [((64, 1024), BF)], *d_xn, Far(dh), x_own, attn_gain_row, Far(block)
    )
    tokens_grad, block_out = gather_head(rows, head)
    tokens_grad, block_out = tokens_grad[None], block_out[None]

    (dw_a,) = after([dw_a], rows)
    grad_wq, grad_wk, grad_wv, grad_wo, gains = call(
        finish_attend,
        [Far(((32, n), F32)) for n in (256, 128, 128, 256)] + [((16, 384), F32)],
        dw_a.reshape(2, 16, 48, 384),
    )
    (gains,) = call(add_two, [((16, 384), F32)], gains, swap(gains, "c", 2, 1))
    (dw_f,) = after([dw_f], gains)
    dw_f = lax.all_to_all(dw_f, ("zl", "y"), 0, 0, tiled=True)
    attn_sum, ffn_sum, query_sum, key_sum = call(
        finish_gains, [((8, 128), F32)] * 2 + [((1, 64), F32)] * 2,
        gains, swap(gains, "zh", 2, 1),
    )
    grad_wg, grad_wu, grad_wd = call(
        finish_feed, [Far(((32, 1152), F32))] * 3, dw_f.reshape(2, 4, 32, 1792)
    )
    return (
        block_out, tokens_grad, attn_sum.reshape(1024), ffn_sum.reshape(1024),
        query_sum.reshape(64), key_sum.reshape(64),
        grad_wq, grad_wk, grad_wv, grad_wo, grad_wg, grad_wu, grad_wd,
    )


def solution(mesh):
    cube = Mesh(mesh.devices.reshape(2, 4, 4, 2, 2), AXES)
    rows = P("x", ("zl", "y"), None)
    weight = P(("zl", "y", "x"), ("zh", "c"))
    return jax.shard_map(
        local,
        mesh=cube,
        in_specs=(rows, P("x", None)) + (P(),) * 4 + (weight,) * 7 + (rows,),
        out_specs=(rows, rows) + (P(),) * 4 + (weight,) * 7,
        check_vma=False,
    )
```

```python
import functools

import jax
import jax.numpy as jnp
from jax import lax
from jax.experimental import pallas as pl
from jax.experimental.pallas import tpu as pltpu
from jax.sharding import Mesh, PartitionSpec as P

EPSILON = 1e-05
ROPE_BASE = 1000000.0
AXES = ("zl", "y", "x", "zh", "c")
Z = ("zl", "zh")
PLANE = ("zl", "y", "x")
BF = jnp.bfloat16
F32 = jnp.float32
SCALE = 64 ** (-0.5)
WHOLE = pl.BlockSpec(memory_space=pltpu.VMEM)


class Far:
    def __init__(self, value):
        self.value = value


def spec(item):
    return pl.BlockSpec() if isinstance(item, Far) else WHOLE


def bare(item):
    return item.value if isinstance(item, Far) else item


def call(body, outs, *operands, room=8, scalars=(), scratch=()):
    scalar = pl.BlockSpec(memory_space=pltpu.SMEM)
    return list(
        pl.pallas_call(
            body,
            out_shape=[jax.ShapeDtypeStruct(*bare(out)) for out in outs],
            in_specs=[scalar] * len(scalars) + [spec(item) for item in operands],
            out_specs=[spec(out) for out in outs],
            scratch_shapes=list(scratch),
            compiler_params=pltpu.CompilerParams(vmem_limit_bytes=room * 2**20 if room else None),
        )(*scalars, *[bare(item) for item in operands])
    )


def dot(left, right):
    return jnp.dot(left, right, preferred_element_type=F32)


def left_product(left, right):
    return lax.dot_general(left, right, (((0,), (0,)), ((), ())), preferred_element_type=F32)


def right_product(left, right):
    return lax.dot_general(left, right, (((1,), (1,)), ((), ())), preferred_element_type=F32)


def row_scale(values):
    return lax.rsqrt(jnp.mean(values * values, axis=-1, keepdims=True) + EPSILON)


def row_norm_grad(grad, normal, scale):
    return scale * (grad - normal * jnp.mean(grad * normal, axis=-1, keepdims=True))


def lanes(values):
    return lax.broadcasted_iota(jnp.int32, values.shape, 1)


def head_sum(values):
    low = lanes(values) < 64
    first = jnp.sum(jnp.where(low, values, 0.0), axis=-1, keepdims=True)
    second = jnp.sum(jnp.where(low, 0.0, values), axis=-1, keepdims=True)
    return jnp.where(low, first, second)


def head_scale(values):
    return lax.rsqrt(head_sum(values * values) * (1.0 / 64) + EPSILON)


def head_norm_grad(grad, normal, scale):
    return scale * (grad - normal * (head_sum(grad * normal) * (1.0 / 64)))


def other_half(values):
    low = (lanes(values) & 63) < 32
    return jnp.where(low, pltpu.roll(values, 96, 1), pltpu.roll(values, 32, 1))


def project(own, other, w, attn_gain, qk_gain, cosine, sine, qh, kv, qkv):
    x = jnp.concatenate([own[...], other[...]]).astype(F32)
    low = (x * row_scale(x) * attn_gain[...]).astype(BF)
    out = dot(low, w[:, :256])
    qkv[...] = out
    q, k = out[:, :128], out[:, 128:]
    cos, sin = cosine[...], sine[...]
    qn = q * head_scale(q) * qk_gain[0:1]
    qh[...] = (qn * cos + other_half(qn) * sin).astype(BF)
    kn = k * head_scale(k) * qk_gain[1:2]
    kr = kn * cos + other_half(kn) * sin
    kv[...] = jnp.where(lanes(k) < 64, kr, k).astype(BF)


def weights_of(q, k, visible):
    scores = right_product(q, k) * SCALE
    return jnp.where(visible, jnp.exp(scores), 0.0)


def attend(qh, kv0, kv1, kv2, kv3, own_places, places, w, send, keep, o_out, l_out):
    sums, totals = [0.0, 0.0], [0.0, 0.0]
    mine = own_places[...]
    for i, kv in enumerate((kv0, kv1, kv2, kv3)):
        visible = places[:, i * 256 : (i + 1) * 256] <= mine
        k, v = kv[:, :64], kv[:, 64:]
        for g in range(2):
            u = weights_of(qh[:, g * 64 : (g + 1) * 64], k, visible)
            totals[g] = totals[g] + jnp.sum(u, axis=-1, keepdims=True)
            sums[g] = sums[g] + dot(u.astype(BF), v)
    o = jnp.concatenate([sums[g] / totals[g] for g in range(2)], axis=1)
    o_out[...] = o
    l_out[...] = jnp.where(lanes(o) < 64, totals[0], totals[1])
    partial = right_product(o.astype(BF), w[:, 256:]).reshape(4, 2, 32, 1024)
    send[...] = partial[:, 1].astype(BF)
    keep[...] = partial[:, 0]


def pair_add(keep, got, own, one, two, three):
    own[...] = keep[0] + got[0].astype(F32)
    for k, out in ((1, one), (2, two), (3, three)):
        out[...] = (keep[k] + got[k].astype(F32)).astype(BF)


def total_of(own, one, two, three):
    return (own[...] + one[...].astype(F32)) + (two[...].astype(F32) + three[...].astype(F32))


def hidden(own, one, two, three, x, gain, h, hn):
    rows = x[:32].astype(F32) + total_of(own, one, two, three)
    h[...] = rows
    hn[...] = (rows * row_scale(rows) * gain[...]).astype(BF)


def feed_parts(gate, up, d_act):
    sig = jax.nn.sigmoid(gate)
    silu = gate * sig
    active = silu * up
    d_gate = d_act * up * sig * (1.0 + gate * (1.0 - sig))
    return active.astype(BF), d_gate, d_act * silu


def feed(
    p0, p1, p2, p3, p4, p5, p6, p7, dy_own, dy_other, w,
    send, keep, hn, act, dgu,
):
    rows = jnp.concatenate([p[...] for p in (p0, p1, p2, p3, p4, p5, p6, p7)])
    hn[...] = rows
    dy = jnp.concatenate([dy_own[...], dy_other[...]])
    def both(left, at, width):
        first, second = left[:, :512], left[:, 512:]
        return dot(first, w[:, 0, :, at : at + width].reshape(512, width)) + dot(
            second, w[:, 1, :, at : at + width].reshape(512, width)
        )
    gate, up, d_act = both(rows, 0, 512), both(rows, 512, 512), both(dy, 1024, 512)
    active, d_gate, d_up = feed_parts(gate, up, d_act)
    act[:, :512] = active
    d_gate, d_up = d_gate.astype(BF), d_up.astype(BF)
    dgu[:, :512] = d_gate
    dgu[:, 512:1024] = d_up
    tail, d_tail = both(rows, 1536, 128), both(dy, 1664, 128)
    low = lanes(tail) < 64
    gate = jnp.where(low, tail, 0.0)
    up = jnp.where(low, pltpu.roll(tail, 64, 1), 0.0)
    active, dg_tail, du_tail = feed_parts(gate, up, d_tail)
    act[:, 512:] = active
    dgu_tail = jnp.where(low, dg_tail, pltpu.roll(du_tail, 64, 1)).astype(BF)
    dgu[:, 1024:] = dgu_tail
    halves = []
    for z in range(2):
        part = right_product(d_gate, w[:, z, :, :512].reshape(512, 512))
        part = part + right_product(d_up, w[:, z, :, 512:1024].reshape(512, 512))
        part = part + right_product(dgu_tail, w[:, z, :, 1536:1664].reshape(512, 128))
        halves.append(part)
    partial = jnp.concatenate(halves, axis=1).reshape(4, 2, 32, 1024)
    send[:, :32] = partial[:, 1].astype(BF)
    keep[:, :32] = partial[:, 0]
    low_act = act[...]
    halves = []
    for z in range(2):
        part = right_product(low_act[:, :512], w[:, z, :, 1024:1536].reshape(512, 512))
        halves.append(part + right_product(low_act[:, 512:], w[:, z, :, 1664:].reshape(512, 128)))
    partial = jnp.concatenate(halves, axis=1).reshape(4, 2, 32, 1024)
    send[:, 32:] = partial[:, 1].astype(BF)
    keep[:, 32:] = partial[:, 0]


def feed_weights(y, hn, dy_own, dy_other, act, dgu, dw):
    dy = jnp.concatenate([dy_own[...], dy_other[...]])
    rows, active = hn[...], act[...]
    def put(left, right, at, width):
        for z in range(2):
            value = left_product(left[:, z * 512 : (z + 1) * 512], right)
            blocks = value.astype(BF).reshape(4, 4, 32, width)
            for i in range(4):
                dw[:, i ^ y[0], z, :, at : at + width] = blocks[i]
    put(rows, dgu[:, :512], 0, 512)
    put(rows, dgu[:, 512:1024], 512, 512)
    put(dy, active[:, :512], 1024, 512)
    put(rows, dgu[:, 1024:], 1536, 128)
    put(dy, active[:, 512:], 1664, 128)


def split_sides(dw, own, one, two, three):
    for k, piece in enumerate((own, one, two, three)):
        piece[...] = dw[k * 64 : (k + 1) * 64].reshape(2, 32, 1792)


def add_sides(zl, own, one, two, three, mine, send):
    def total(z):
        first = own[z].astype(F32) + one[z].astype(F32)
        return first + (two[z].astype(F32) + three[z].astype(F32))
    mine[...] = total(zl[0])
    send[...] = total(1 - zl[0]).astype(BF)


def hidden_grad(own, one, two, three, h, dy, gain, dh, low, gain_part, block):
    total = total_of(own, one, two, three)
    d_hn, branch = total[:32], total[32:]
    rows = h[...]
    block[...] = (rows + branch).astype(BF)
    scale = row_scale(rows)
    hat = rows * scale
    gain_part[...] = jnp.sum(d_hn * hat, axis=0, keepdims=True)
    grad = dy[:32].astype(F32) + row_norm_grad(d_hn * gain[...], hat, scale)
    dh[...] = grad
    low[...] = grad.astype(BF)


def attend_grad(
    p0, p1, p2, p3, p4, p5, p6, p7, qh, kv0, kv1, kv2, kv3, own_places, places, w, o, l,
    d_attn, d_qh, d_kv0, d_kv1, d_kv2, d_kv3,
):
    rows = jnp.concatenate([p[...] for p in (p0, p1, p2, p3, p4, p5, p6, p7)])
    d_attn[...] = rows
    d_o = dot(rows, w[:, 256:])
    denom = l[...]
    d_inner = (d_o / denom).astype(BF)
    delta = head_sum(d_o * o[...]) / denom
    mine = own_places[...]
    d_q = [0.0, 0.0]
    for i, (kv, d_kv) in enumerate(((kv0, d_kv0), (kv1, d_kv1), (kv2, d_kv2), (kv3, d_kv3))):
        visible = places[:, i * 256 : (i + 1) * 256] <= mine
        k, v = kv[:, :64], kv[:, 64:]
        d_k, d_v = 0.0, 0.0
        for g in range(2):
            at = slice(g * 64, (g + 1) * 64)
            q, di = qh[:, at], d_inner[:, at]
            u = weights_of(q, k, visible)
            ds = (u * (right_product(di, v) - delta[:, g * 64 : g * 64 + 1])).astype(BF)
            d_q[g] = d_q[g] + dot(ds, k)
            d_k = d_k + left_product(ds, q)
            d_v = d_v + left_product(u.astype(BF), di)
        d_kv[...] = jnp.concatenate([d_k * SCALE, d_v], axis=1).astype(d_kv.dtype)
    d_qh[...] = jnp.concatenate(d_q, axis=1) * SCALE


def project_grad(
    d_qh, own, one, two, three, qkv, cosine, sine, qk_gain, w, x_own, x_other, ffn_part,
    d_qkv, send, keep, gains,
):
    d_kv = total_of(own, one, two, three)
    cos, sin = cosine[...], sine[...]
    q, k = qkv[:, :128], qkv[:, 128:]
    q_scale, k_scale = head_scale(q), head_scale(k)
    q_hat, k_hat = q * q_scale, k * k_scale
    d_q = d_qh[...]
    d_qn = d_q * cos - other_half(d_q) * sin
    d_kn = d_kv * cos - other_half(d_kv) * sin
    heads = jnp.concatenate(
        [jnp.sum(d_qn * q_hat, axis=0, keepdims=True), jnp.sum(d_kn * k_hat, axis=0, keepdims=True)]
    )
    d_q = head_norm_grad(d_qn * qk_gain[0:1], q_hat, q_scale)
    d_k = head_norm_grad(d_kn * qk_gain[1:2], k_hat, k_scale)
    d_k = jnp.where(lanes(d_k) < 64, d_k, d_kv)
    low = jnp.concatenate([d_q, d_k], axis=1).astype(BF)
    d_qkv[...] = low
    partial = right_product(low, w[:, :256])
    x = jnp.concatenate([x_own[...], x_other[...]]).astype(F32)
    attn_part = jnp.sum(partial * (x * row_scale(x)), axis=0, keepdims=True)
    def fold(part):
        return jnp.concatenate([part[:, i * 128 : (i + 1) * 128] for i in range(8)])
    heads = jnp.concatenate([heads, jnp.zeros((6, 128), F32)])
    gains[...] = jnp.concatenate([fold(attn_part), fold(ffn_part), heads], axis=1).astype(BF)
    partial = partial.reshape(4, 2, 32, 1024)
    send[...] = partial[:, 1].astype(BF)
    keep[...] = partial[:, 0]


def attend_weights(x_own, x_other, attn_gain, d_qkv, d_attn, o, gains, dw):
    x = jnp.concatenate([x_own[...], x_other[...]]).astype(F32)
    normed = (x * row_scale(x) * attn_gain[...]).astype(BF)
    first = left_product(normed, d_qkv[...]).astype(BF)
    second = left_product(d_attn[...], o[...].astype(BF)).astype(BF)
    dw[:, :32, :256] = first.reshape(32, 32, 256)
    dw[:, :32, 256:] = second.reshape(32, 32, 128)
    dw[:, 32:] = jnp.broadcast_to(gains[...][None], (32, 8, 384))


def token_rows(own, one, two, three, dh, x, gain, block, out):
    d_xn = total_of(own, one, two, three)
    rows = x[:32].astype(F32)
    scale = row_scale(rows)
    grad = row_norm_grad(d_xn * gain[...], rows * scale, scale)
    out[:32] = (dh[...] + grad).astype(BF)
    out[32:] = block[...]


def finish_attend(parts, wq, wk, wv, wo, gains):
    sums = [jnp.sum(parts[z].astype(F32), axis=0) for z in range(2)]
    gains[...] = sums[0][32:] + sums[1][32:]
    low, high = sums[0][:32], sums[1][:32]
    wq[...] = jnp.concatenate([low[:, :128], high[:, :128]], axis=1)
    wk[...] = jnp.concatenate([low[:, 128:192], high[:, 128:192]], axis=1)
    wv[...] = jnp.concatenate([low[:, 192:256], high[:, 192:256]], axis=1)
    wo[...] = jnp.concatenate([low[:, 256:], high[:, 256:]], axis=1)


def finish_feed(zl, own, got, wg, wu, wd):
    mine, its = own[...], got[...].astype(F32)
    first = zl[0] == 0
    low, high = jnp.where(first, mine, its), jnp.where(first, its, mine)
    for i, out in enumerate((wg, wu, wd)):
        wide, tail = slice(i * 512, (i + 1) * 512), slice(1536 + i * 64, 1600 + i * 64)
        out[...] = jnp.concatenate(
            [low[:, wide], low[:, tail], high[:, wide], high[:, tail]], axis=1
        )


def add_two(own, one, out):
    out[...] = own[...] + one[...]


def finish_gains(one, two, attn, ffn, query, key):
    total = one[...] + two[...]
    attn[...] = total[:8, :128]
    ffn[...] = total[:8, 128:256]
    query[...] = total[0:1, 256:320] + total[0:1, 320:384]
    key[...] = total[1:2, 256:320]


def prepare(zl, head, wq, wk, wv, wo, wg, wu, wd, tokens, blocks, send_f, keep_f, x_own):
    for z in range(2):
        at = 0
        for w in (wq, wk, wv, wo):
            width = w.shape[1] // 2
            part = w[:, z * width : (z + 1) * width]
            blocks[z, :, :, at : at + width] = jnp.broadcast_to(part[None], (16, 32, width))
            at += width
    pad = jnp.zeros((32, 64), BF)
    sides = []
    for z in range(2):
        parts = [w[:, z * 576 : (z + 1) * 576] for w in (wg, wu, wd)]
        sides.append(
            jnp.concatenate([p[:, :512] for p in parts] + [p[:, 512:] for p in parts] + [pad], axis=1)
        )
    first = zl[0] == 0
    keep_f[...] = jnp.where(first, sides[0], sides[1])
    send_f[...] = jnp.where(first, sides[1], sides[0])
    relative_rows(head, tokens, x_own)


def relative_rows(head, rows, out):
    for k in range(4):
        out[k * 32 : (k + 1) * 32] = rows[0, pl.ds((head[0] ^ k) * 32, 32)]


def order_rows(zl, own, got, out):
    out[zl[0]] = own[...]
    out[1 - zl[0]] = got[...]


def swap(value, axes, size, mask):
    return lax.ppermute(value, axes, [(i, i ^ mask) for i in range(size)])


def fan(pieces, axes):
    return [swap(pieces[k], axes, 4, k) for k in (1, 2, 3)]


def sum_pair(send, keep):
    got = swap(send, "c", 2, 1)
    shape = send.shape[1:]
    return call(pair_add, [(shape, F32)] + [(shape, BF)] * 3, keep, got)


def sum_scatter(send, keep):
    own, *rest = sum_pair(send, keep)
    return [own] + fan([None] + rest, Z)


def gather_rows(rows):
    column = [rows] + fan([rows] * 4, Z)
    pieces = []
    for piece in column:
        pieces += [piece, swap(piece, "c", 2, 1)]
    return pieces


def place_rows(head, p0, p1, p2, p3, tokens_grad, block_out):
    for k, piece in enumerate((p0, p1, p2, p3)):
        at = pl.ds((head[0] ^ k) * 32, 32)
        tokens_grad[at] = piece[:32]
        block_out[at] = piece[32:]


def gather_head(rows, head):
    other = swap(rows, "c", 2, 1)
    pieces = [rows, other, swap(rows, "zh", 2, 1), swap(other, "zh", 2, 1)]
    return call(place_rows, [Far(((128, 1024), BF))] * 2, *pieces, scalars=(head.reshape(1),))


def after(values, *first):
    out = lax.optimization_barrier(tuple(values) + tuple(first))
    return list(out[: len(values)])


def local(
    tokens, positions, attn_gain, ffn_gain, query_gain, key_gain,
    w_query, w_key, w_value, w_out, w_gate, w_up, w_down, cotangent,
):
    zl, y, head = lax.axis_index("zl"), lax.axis_index("y"), lax.axis_index(("zh", "c"))
    attn_gain_row, ffn_gain_row = attn_gain[None], ffn_gain[None]

    zl_ref, head_ref = zl.reshape(1), head.reshape(1)
    blocks, send_f, keep_f, x_own = call(
        prepare,
        [((2, 16, 32, 384), BF), ((32, 1792), BF), ((32, 1792), BF), ((128, 1024), BF)],
        *[Far(w) for w in (w_query, w_key, w_value, w_out, w_gate, w_up, w_down, tokens)],
        scalars=(zl_ref, head_ref), room=None,
    )
    got_f = swap(send_f, "zl", 2, 1)
    x_other = swap(x_own, "zl", 2, 1)
    w_a = lax.all_to_all(blocks.reshape(1024, 384), PLANE, 0, 0, tiled=True)
    (rows_f,) = call(order_rows, [Far(((2, 32, 1792), BF))], keep_f, got_f, scalars=(zl_ref,))
    w_f = lax.all_gather(rows_f, ("y", "x"), axis=0)

    (late_positions,) = after([positions], blocks)
    steps = jnp.array([dl * 16 + ky * 4 + d for ky in range(4) for dl in range(2) for d in range(4)])
    places = late_positions[0].reshape(32, 32)[steps ^ (zl * 16 + y * 4 + head)].reshape(1024)
    own_places = places[:256]
    frequency = ROPE_BASE ** (-(jnp.arange(32).astype(F32) * 2.0 / 64))
    angles = own_places.astype(F32)[:, None] * frequency
    cosine, sine = jnp.cos(angles), jnp.sin(angles)
    cosine = jnp.concatenate([cosine] * 4, axis=1)
    sine = jnp.concatenate([-sine, sine] * 2, axis=1)
    own_places, places = own_places[:, None], places[None]
    qk_gain = jnp.stack([jnp.tile(query_gain, 2), jnp.tile(key_gain, 2)])

    halves = [((4, 32, 1024), BF), ((4, 32, 1024), F32)]
    flat, wide_flat = ((256, 128), BF), ((256, 128), F32)
    rows_low, rows_high = ((32, 1024), BF), ((32, 1024), F32)
    qh, kv, qkv = call(
        project, [flat, flat, Far(((256, 256), F32))],
        x_own, x_other, Far(w_a), attn_gain_row, qk_gain, cosine, sine,
    )
    (late_dy,) = after([cotangent], kv)
    (dy_own,) = call(relative_rows, [((128, 1024), BF)], Far(late_dy), scalars=(head_ref,))
    dy_other = swap(dy_own, "zl", 2, 1)
    kvs = [kv] + fan([kv] * 4, "y")
    (qh,) = after([qh], dy_other)
    send, keep, o, l = call(
        attend, halves + [Far(wide_flat)] * 2, qh, *kvs, own_places, places, Far(w_a)
    )
    h, hn = call(
        hidden, [Far(rows_high), rows_low], *sum_scatter(send, keep), x_own, ffn_gain_row
    )
    send, keep, hn_all, act, dgu = call(
        feed,
        [((4, 64, 1024), BF), ((4, 64, 1024), F32)]
        + [((256, 1024), BF), ((256, 640), BF), ((256, 1152), BF)],
        *gather_rows(hn), dy_own, dy_other, w_f,
    )
    pair = sum_pair(send, keep)
    pair = sum_pair(send, keep)
    act, dgu = after([act, dgu], *pair)
    d_hn = [pair[0]] + fan([None] + pair[1:], Z)
    (dw_f,) = call(
        feed_weights, [Far(((4, 4, 2, 32, 1792), BF))], hn_all, dy_own, dy_other, act, dgu,
        scalars=(y.reshape(1),),
    )
    dw_f = lax.psum_scatter(dw_f.reshape(1024, 1792), "x", scatter_dimension=0, tiled=True)
    dh, d_low, ffn_part, block = call(
        hidden_grad, [Far(rows_high), rows_low, Far(((1, 1024), F32)), Far(rows_low)],
        *d_hn, Far(h), dy_own, ffn_gain_row,
    )
    d_attn, d_qh, *d_kvs = call(
        attend_grad, [Far(((256, 1024), BF)), wide_flat, wide_flat, flat, flat, flat],
        *gather_rows(d_low), Far(qh), *[Far(t) for t in kvs], own_places, places, Far(w_a), Far(o), Far(l),
    )
    d_qkv, send, keep, gains = call(
        project_grad, [((256, 256), BF)] + halves + [((8, 384), BF)],
        d_qh, d_kvs[0], *fan(d_kvs, "y"), Far(qkv), cosine, sine, qk_gain, Far(w_a),
        Far(x_own), Far(x_other), Far(ffn_part),
    )
    (dw_a,) = call(
        attend_weights, [((32, 40, 384), BF)],
        Far(x_own), Far(x_other), attn_gain_row, d_qkv, Far(d_attn), Far(o), gains,
    )
    own, *rest = sum_pair(send, keep)
    d_xn = [own] + fan([None] + rest, Z)
    (dw_a,) = after([dw_a], *d_xn)
    dw_a = lax.all_to_all(dw_a, PLANE, 0, 0, tiled=True)
    (rows,) = call(
        token_rows, [((64, 1024), BF)], *d_xn, Far(dh), x_own, attn_gain_row, Far(block)
    )
    tokens_grad, block_out = gather_head(rows, head)
    tokens_grad, block_out = tokens_grad[None], block_out[None]

    (dw_a,) = after([dw_a], tokens_grad)
    grad_wq, grad_wk, grad_wv, grad_wo, gains = call(
        finish_attend,
        [Far(((32, n), F32)) for n in (256, 128, 128, 256)] + [((8, 384), F32)],
        dw_a.reshape(2, 16, 40, 384),
    )
    (gains,) = call(add_two, [((8, 384), F32)], gains, swap(gains, "c", 2, 1))
    attn_sum, ffn_sum, query_sum, key_sum = call(
        finish_gains, [((8, 128), F32)] * 2 + [((1, 64), F32)] * 2,
        gains, swap(gains, "zh", 2, 1),
    )
    sides = call(split_sides, [((2, 32, 1792), BF)] * 4, Far(dw_f))
    others = after(fan(sides, "y"), gains)
    own_f, send_f = call(
        add_sides, [((32, 1792), F32), ((32, 1792), BF)], sides[0], *others,
        scalars=(zl_ref,),
    )
    grad_wg, grad_wu, grad_wd = call(
        finish_feed, [Far(((32, 1152), F32))] * 3, own_f, swap(send_f, "zl", 2, 1),
        scalars=(zl_ref,),
    )
    return (
        block_out, tokens_grad, attn_sum.reshape(1024), ffn_sum.reshape(1024),
        query_sum.reshape(64), key_sum.reshape(64),
        grad_wq, grad_wk, grad_wv, grad_wo, grad_wg, grad_wu, grad_wd,
    )


def solution(mesh):
    cube = Mesh(mesh.devices.reshape(2, 4, 4, 2, 2), AXES)
    rows = P("x", ("zl", "y"), None)
    weight = P(("zl", "y", "x"), ("zh", "c"))
    return jax.shard_map(
        local,
        mesh=cube,
        in_specs=(rows, P("x", None)) + (P(),) * 4 + (weight,) * 7 + (rows,),
        out_specs=(rows, rows) + (P(),) * 4 + (weight,) * 7,
        check_vma=False,
    )
```

```python
import functools

import jax
import jax.numpy as jnp
from jax import lax
from jax.experimental import pallas as pl
from jax.experimental.pallas import tpu as pltpu
from jax.sharding import Mesh, PartitionSpec as P

EPSILON = 1e-05
ROPE_BASE = 1000000.0
AXES = ("zl", "y", "x", "zh", "c")
Z = ("zl", "zh")
PLANE = ("zl", "y", "x")
BF = jnp.bfloat16
F32 = jnp.float32
SCALE = 64 ** (-0.5)
WHOLE = pl.BlockSpec(memory_space=pltpu.VMEM)


class Far:
    def __init__(self, value):
        self.value = value


def spec(item):
    return pl.BlockSpec() if isinstance(item, Far) else WHOLE


def bare(item):
    return item.value if isinstance(item, Far) else item


def call(body, outs, *operands, room=8, scalars=(), scratch=()):
    scalar = pl.BlockSpec(memory_space=pltpu.SMEM)
    return list(
        pl.pallas_call(
            body,
            out_shape=[jax.ShapeDtypeStruct(*bare(out)) for out in outs],
            in_specs=[scalar] * len(scalars) + [spec(item) for item in operands],
            out_specs=[spec(out) for out in outs],
            scratch_shapes=list(scratch),
            compiler_params=pltpu.CompilerParams(vmem_limit_bytes=room * 2**20 if room else None),
        )(*scalars, *[bare(item) for item in operands])
    )


def dot(left, right):
    return jnp.dot(left, right, preferred_element_type=F32)


def left_product(left, right):
    return lax.dot_general(left, right, (((0,), (0,)), ((), ())), preferred_element_type=F32)


def right_product(left, right):
    return lax.dot_general(left, right, (((1,), (1,)), ((), ())), preferred_element_type=F32)


def row_scale(values):
    return lax.rsqrt(jnp.mean(values * values, axis=-1, keepdims=True) + EPSILON)


def row_norm_grad(grad, normal, scale):
    return scale * (grad - normal * jnp.mean(grad * normal, axis=-1, keepdims=True))


def lanes(values):
    return lax.broadcasted_iota(jnp.int32, values.shape, 1)


def head_sum(values):
    low = lanes(values) < 64
    first = jnp.sum(jnp.where(low, values, 0.0), axis=-1, keepdims=True)
    second = jnp.sum(jnp.where(low, 0.0, values), axis=-1, keepdims=True)
    return jnp.where(low, first, second)


def head_scale(values):
    return lax.rsqrt(head_sum(values * values) * (1.0 / 64) + EPSILON)


def head_norm_grad(grad, normal, scale):
    return scale * (grad - normal * (head_sum(grad * normal) * (1.0 / 64)))


def other_half(values):
    low = (lanes(values) & 63) < 32
    return jnp.where(low, pltpu.roll(values, 96, 1), pltpu.roll(values, 32, 1))


def project(own, other, w, attn_gain, qk_gain, cosine, sine, qh, kv, qkv):
    x = jnp.concatenate([own[...], other[...]]).astype(F32)
    low = (x * row_scale(x) * attn_gain[...]).astype(BF)
    out = dot(low, w[:, :256])
    qkv[...] = out
    q, k = out[:, :128], out[:, 128:]
    cos, sin = cosine[...], sine[...]
    qn = q * head_scale(q) * qk_gain[0:1]
    qh[...] = (qn * cos + other_half(qn) * sin).astype(BF)
    kn = k * head_scale(k) * qk_gain[1:2]
    kr = kn * cos + other_half(kn) * sin
    kv[...] = jnp.where(lanes(k) < 64, kr, k).astype(BF)


def weights_of(q, k, visible):
    scores = right_product(q, k) * SCALE
    return jnp.where(visible, jnp.exp(scores), 0.0)


def attend(qh, kv0, kv1, kv2, kv3, own_places, places, w, send, keep, o_out, l_out):
    sums, totals = [0.0, 0.0], [0.0, 0.0]
    mine = own_places[...]
    for i, kv in enumerate((kv0, kv1, kv2, kv3)):
        visible = places[:, i * 256 : (i + 1) * 256] <= mine
        k, v = kv[:, :64], kv[:, 64:]
        for g in range(2):
            u = weights_of(qh[:, g * 64 : (g + 1) * 64], k, visible)
            totals[g] = totals[g] + jnp.sum(u, axis=-1, keepdims=True)
            sums[g] = sums[g] + dot(u.astype(BF), v)
    o = jnp.concatenate([sums[g] / totals[g] for g in range(2)], axis=1)
    o_out[...] = o
    l_out[...] = jnp.where(lanes(o) < 64, totals[0], totals[1])
    partial = right_product(o.astype(BF), w[:, 256:]).reshape(4, 2, 32, 1024)
    send[...] = partial[:, 1].astype(BF)
    keep[...] = partial[:, 0]


def pair_add(keep, got, own, one, two, three):
    own[...] = keep[0] + got[0].astype(F32)
    for k, out in ((1, one), (2, two), (3, three)):
        out[...] = (keep[k] + got[k].astype(F32)).astype(BF)


def total_of(own, one, two, three):
    return (own[...] + one[...].astype(F32)) + (two[...].astype(F32) + three[...].astype(F32))


def hidden(own, one, two, three, x, gain, h, hn):
    rows = x[:32].astype(F32) + total_of(own, one, two, three)
    h[...] = rows
    hn[...] = (rows * row_scale(rows) * gain[...]).astype(BF)


def feed_parts(gate, up, d_act):
    sig = jax.nn.sigmoid(gate)
    silu = gate * sig
    active = silu * up
    d_gate = d_act * up * sig * (1.0 + gate * (1.0 - sig))
    return active.astype(BF), d_gate, d_act * silu


def feed(
    p0, p1, p2, p3, p4, p5, p6, p7, dy_own, dy_other, w,
    send, keep, hn, act, dgu,
):
    rows = jnp.concatenate([p[...] for p in (p0, p1, p2, p3, p4, p5, p6, p7)])
    hn[...] = rows
    dy = jnp.concatenate([dy_own[...], dy_other[...]])
    def both(left, at, width):
        first, second = left[:, :512], left[:, 512:]
        return dot(first, w[:, 0, :, at : at + width].reshape(512, width)) + dot(
            second, w[:, 1, :, at : at + width].reshape(512, width)
        )
    gate, up, d_act = both(rows, 0, 512), both(rows, 512, 512), both(dy, 1024, 512)
    active, d_gate, d_up = feed_parts(gate, up, d_act)
    act[:, :512] = active
    d_gate, d_up = d_gate.astype(BF), d_up.astype(BF)
    dgu[:, :512] = d_gate
    dgu[:, 512:1024] = d_up
    tail, d_tail = both(rows, 1536, 128), both(dy, 1664, 128)
    low = lanes(tail) < 64
    gate = jnp.where(low, tail, 0.0)
    up = jnp.where(low, pltpu.roll(tail, 64, 1), 0.0)
    active, dg_tail, du_tail = feed_parts(gate, up, d_tail)
    act[:, 512:] = active
    dgu_tail = jnp.where(low, dg_tail, pltpu.roll(du_tail, 64, 1)).astype(BF)
    dgu[:, 1024:] = dgu_tail
    halves = []
    for z in range(2):
        part = right_product(d_gate, w[:, z, :, :512].reshape(512, 512))
        part = part + right_product(d_up, w[:, z, :, 512:1024].reshape(512, 512))
        part = part + right_product(dgu_tail, w[:, z, :, 1536:1664].reshape(512, 128))
        halves.append(part)
    partial = jnp.concatenate(halves, axis=1).reshape(4, 2, 32, 1024)
    send[:, :32] = partial[:, 1].astype(BF)
    keep[:, :32] = partial[:, 0]
    low_act = act[...]
    halves = []
    for z in range(2):
        part = right_product(low_act[:, :512], w[:, z, :, 1024:1536].reshape(512, 512))
        halves.append(part + right_product(low_act[:, 512:], w[:, z, :, 1664:].reshape(512, 128)))
    partial = jnp.concatenate(halves, axis=1).reshape(4, 2, 32, 1024)
    send[:, 32:] = partial[:, 1].astype(BF)
    keep[:, 32:] = partial[:, 0]


def feed_weights(y, hn, dy_own, dy_other, act, dgu, dw):
    dy = jnp.concatenate([dy_own[...], dy_other[...]])
    rows, active = hn[...], act[...]
    def put(left, right, at, width):
        for z in range(2):
            value = left_product(left[:, z * 512 : (z + 1) * 512], right)
            blocks = value.astype(BF).reshape(4, 4, 32, width)
            for i in range(4):
                dw[:, i ^ y[0], z, :, at : at + width] = blocks[i]
    put(rows, dgu[:, :512], 0, 512)
    put(rows, dgu[:, 512:1024], 512, 512)
    put(dy, active[:, :512], 1024, 512)
    put(rows, dgu[:, 1024:], 1536, 128)
    put(dy, active[:, 512:], 1664, 128)


def split_sides(dw, own, one, two, three):
    for k, piece in enumerate((own, one, two, three)):
        piece[...] = dw[k * 64 : (k + 1) * 64].reshape(2, 32, 1792)


def add_sides(zl, own, one, two, three, mine, send):
    def total(z):
        first = own[z].astype(F32) + one[z].astype(F32)
        return first + (two[z].astype(F32) + three[z].astype(F32))
    mine[...] = total(zl[0])
    send[...] = total(1 - zl[0]).astype(BF)


def hidden_grad(own, one, two, three, h, dy, gain, dh, low, gain_part, block):
    total = total_of(own, one, two, three)
    d_hn, branch = total[:32], total[32:]
    rows = h[...]
    block[...] = (rows + branch).astype(BF)
    scale = row_scale(rows)
    hat = rows * scale
    gain_part[...] = jnp.sum(d_hn * hat, axis=0, keepdims=True)
    grad = dy[:32].astype(F32) + row_norm_grad(d_hn * gain[...], hat, scale)
    dh[...] = grad
    low[...] = grad.astype(BF)


def attend_grad(
    p0, p1, p2, p3, p4, p5, p6, p7, qh, kv0, kv1, kv2, kv3, own_places, places, w, o, l,
    d_attn, d_qh, d_kv0, d_kv1, d_kv2, d_kv3,
):
    rows = jnp.concatenate([p[...] for p in (p0, p1, p2, p3, p4, p5, p6, p7)])
    d_attn[...] = rows
    d_o = dot(rows, w[:, 256:])
    denom = l[...]
    d_inner = (d_o / denom).astype(BF)
    delta = head_sum(d_o * o[...]) / denom
    mine = own_places[...]
    d_q = [0.0, 0.0]
    for i, (kv, d_kv) in enumerate(((kv0, d_kv0), (kv1, d_kv1), (kv2, d_kv2), (kv3, d_kv3))):
        visible = places[:, i * 256 : (i + 1) * 256] <= mine
        k, v = kv[:, :64], kv[:, 64:]
        d_k, d_v = 0.0, 0.0
        for g in range(2):
            at = slice(g * 64, (g + 1) * 64)
            q, di = qh[:, at], d_inner[:, at]
            u = weights_of(q, k, visible)
            ds = (u * (right_product(di, v) - delta[:, g * 64 : g * 64 + 1])).astype(BF)
            d_q[g] = d_q[g] + dot(ds, k)
            d_k = d_k + left_product(ds, q)
            d_v = d_v + left_product(u.astype(BF), di)
        d_kv[...] = jnp.concatenate([d_k * SCALE, d_v], axis=1).astype(d_kv.dtype)
    d_qh[...] = jnp.concatenate(d_q, axis=1) * SCALE


def project_grad(
    d_qh, own, one, two, three, qkv, cosine, sine, qk_gain, w, x_own, x_other, ffn_part,
    d_qkv, send, keep, gains,
):
    d_kv = total_of(own, one, two, three)
    cos, sin = cosine[...], sine[...]
    q, k = qkv[:, :128], qkv[:, 128:]
    q_scale, k_scale = head_scale(q), head_scale(k)
    q_hat, k_hat = q * q_scale, k * k_scale
    d_q = d_qh[...]
    d_qn = d_q * cos - other_half(d_q) * sin
    d_kn = d_kv * cos - other_half(d_kv) * sin
    heads = jnp.concatenate(
        [jnp.sum(d_qn * q_hat, axis=0, keepdims=True), jnp.sum(d_kn * k_hat, axis=0, keepdims=True)]
    )
    d_q = head_norm_grad(d_qn * qk_gain[0:1], q_hat, q_scale)
    d_k = head_norm_grad(d_kn * qk_gain[1:2], k_hat, k_scale)
    d_k = jnp.where(lanes(d_k) < 64, d_k, d_kv)
    low = jnp.concatenate([d_q, d_k], axis=1).astype(BF)
    d_qkv[...] = low
    partial = right_product(low, w[:, :256])
    x = jnp.concatenate([x_own[...], x_other[...]]).astype(F32)
    attn_part = jnp.sum(partial * (x * row_scale(x)), axis=0, keepdims=True)
    def fold(part):
        return jnp.concatenate([part[:, i * 128 : (i + 1) * 128] for i in range(8)])
    heads = jnp.concatenate([heads, jnp.zeros((6, 128), F32)])
    gains[...] = jnp.concatenate([fold(attn_part), fold(ffn_part), heads], axis=1).astype(BF)
    partial = partial.reshape(4, 2, 32, 1024)
    send[...] = partial[:, 1].astype(BF)
    keep[...] = partial[:, 0]


def attend_weights(x_own, x_other, attn_gain, d_qkv, d_attn, o, gains, dw):
    x = jnp.concatenate([x_own[...], x_other[...]]).astype(F32)
    normed = (x * row_scale(x) * attn_gain[...]).astype(BF)
    first = left_product(normed, d_qkv[...]).astype(BF)
    second = left_product(d_attn[...], o[...].astype(BF)).astype(BF)
    dw[:, :32, :256] = first.reshape(32, 32, 256)
    dw[:, :32, 256:] = second.reshape(32, 32, 128)
    dw[:, 32:] = jnp.broadcast_to(gains[...][None], (32, 8, 384))


def token_rows(own, one, two, three, dh, x, gain, block, out):
    d_xn = total_of(own, one, two, three)
    rows = x[:32].astype(F32)
    scale = row_scale(rows)
    grad = row_norm_grad(d_xn * gain[...], rows * scale, scale)
    out[:32] = (dh[...] + grad).astype(BF)
    out[32:] = block[...]


def finish_attend(parts, wq, wk, wv, wo, gains):
    sums = [jnp.sum(parts[z].astype(F32), axis=0) for z in range(2)]
    gains[...] = sums[0][32:] + sums[1][32:]
    low, high = sums[0][:32], sums[1][:32]
    wq[...] = jnp.concatenate([low[:, :128], high[:, :128]], axis=1)
    wk[...] = jnp.concatenate([low[:, 128:192], high[:, 128:192]], axis=1)
    wv[...] = jnp.concatenate([low[:, 192:256], high[:, 192:256]], axis=1)
    wo[...] = jnp.concatenate([low[:, 256:], high[:, 256:]], axis=1)


def finish_feed(zl, own, got, wg, wu, wd):
    mine, its = own[...], got[...].astype(F32)
    first = zl[0] == 0
    low, high = jnp.where(first, mine, its), jnp.where(first, its, mine)
    for i, out in enumerate((wg, wu, wd)):
        wide, tail = slice(i * 512, (i + 1) * 512), slice(1536 + i * 64, 1600 + i * 64)
        out[...] = jnp.concatenate(
            [low[:, wide], low[:, tail], high[:, wide], high[:, tail]], axis=1
        )


def add_two(own, one, out):
    out[...] = own[...] + one[...]


def finish_gains(one, two, attn, ffn, query, key):
    total = one[...] + two[...]
    attn[...] = total[:8, :128]
    ffn[...] = total[:8, 128:256]
    query[...] = total[0:1, 256:320] + total[0:1, 320:384]
    key[...] = total[1:2, 256:320]


def prepare(zl, head, wq, wk, wv, wo, wg, wu, wd, tokens, blocks, send_f, keep_f, x_own):
    for z in range(2):
        at = 0
        for w in (wq, wk, wv, wo):
            width = w.shape[1] // 2
            part = w[:, z * width : (z + 1) * width]
            blocks[z, :, :, at : at + width] = jnp.broadcast_to(part[None], (16, 32, width))
            at += width
    pad = jnp.zeros((32, 64), BF)
    sides = []
    for z in range(2):
        parts = [w[:, z * 576 : (z + 1) * 576] for w in (wg, wu, wd)]
        sides.append(
            jnp.concatenate([p[:, :512] for p in parts] + [p[:, 512:] for p in parts] + [pad], axis=1)
        )
    first = zl[0] == 0
    keep_f[...] = jnp.where(first, sides[0], sides[1])
    send_f[...] = jnp.where(first, sides[1], sides[0])
    relative_rows(head, tokens, x_own)


def relative_rows(head, rows, out):
    for k in range(4):
        out[k * 32 : (k + 1) * 32] = rows[0, pl.ds((head[0] ^ k) * 32, 32)]


def order_rows(zl, own, got, out):
    out[zl[0]] = own[...]
    out[1 - zl[0]] = got[...]


def swap(value, axes, size, mask):
    return lax.ppermute(value, axes, [(i, i ^ mask) for i in range(size)])


def fan(pieces, axes):
    return [swap(pieces[k], axes, 4, k) for k in (1, 2, 3)]


def sum_pair(send, keep):
    got = swap(send, "c", 2, 1)
    shape = send.shape[1:]
    return call(pair_add, [(shape, F32)] + [(shape, BF)] * 3, keep, got)


def sum_scatter(send, keep):
    own, *rest = sum_pair(send, keep)
    return [own] + fan([None] + rest, Z)


def gather_rows(rows, *first):
    column = [rows] + after(fan([rows] * 4, Z), *first)
    pieces = []
    for piece in column:
        pieces += [piece, swap(piece, "c", 2, 1)]
    return pieces


def place_rows(head, p0, p1, p2, p3, tokens_grad, block_out):
    for k, piece in enumerate((p0, p1, p2, p3)):
        at = pl.ds((head[0] ^ k) * 32, 32)
        tokens_grad[at] = piece[:32]
        block_out[at] = piece[32:]


def gather_head(rows, head):
    other = swap(rows, "c", 2, 1)
    pieces = [rows, other, swap(rows, "zh", 2, 1), swap(other, "zh", 2, 1)]
    return call(place_rows, [Far(((128, 1024), BF))] * 2, *pieces, scalars=(head.reshape(1),))


def after(values, *first):
    out = lax.optimization_barrier(tuple(values) + tuple(first))
    return list(out[: len(values)])


def local(
    tokens, positions, attn_gain, ffn_gain, query_gain, key_gain,
    w_query, w_key, w_value, w_out, w_gate, w_up, w_down, cotangent,
):
    zl, y, head = lax.axis_index("zl"), lax.axis_index("y"), lax.axis_index(("zh", "c"))
    attn_gain_row, ffn_gain_row = attn_gain[None], ffn_gain[None]

    zl_ref, head_ref = zl.reshape(1), head.reshape(1)
    blocks, send_f, keep_f, x_own = call(
        prepare,
        [((2, 16, 32, 384), BF), ((32, 1792), BF), ((32, 1792), BF), ((128, 1024), BF)],
        *[Far(w) for w in (w_query, w_key, w_value, w_out, w_gate, w_up, w_down, tokens)],
        scalars=(zl_ref, head_ref), room=None,
    )
    got_f = swap(send_f, "zl", 2, 1)
    x_other = swap(x_own, "zl", 2, 1)
    w_a = lax.all_to_all(blocks.reshape(1024, 384), PLANE, 0, 0, tiled=True)
    (rows_f,) = call(order_rows, [Far(((2, 32, 1792), BF))], keep_f, got_f, scalars=(zl_ref,))
    w_f = lax.all_gather(rows_f, ("y", "x"), axis=0)

    (late_positions,) = after([positions], blocks)
    steps = jnp.array([dl * 16 + ky * 4 + d for ky in range(4) for dl in range(2) for d in range(4)])
    places = late_positions[0].reshape(32, 32)[steps ^ (zl * 16 + y * 4 + head)].reshape(1024)
    own_places = places[:256]
    frequency = ROPE_BASE ** (-(jnp.arange(32).astype(F32) * 2.0 / 64))
    angles = own_places.astype(F32)[:, None] * frequency
    cosine, sine = jnp.cos(angles), jnp.sin(angles)
    cosine = jnp.concatenate([cosine] * 4, axis=1)
    sine = jnp.concatenate([-sine, sine] * 2, axis=1)
    own_places, places = own_places[:, None], places[None]
    qk_gain = jnp.stack([jnp.tile(query_gain, 2), jnp.tile(key_gain, 2)])

    halves = [((4, 32, 1024), BF), ((4, 32, 1024), F32)]
    flat, wide_flat = ((256, 128), BF), ((256, 128), F32)
    rows_low, rows_high = ((32, 1024), BF), ((32, 1024), F32)
    qh, kv, qkv = call(
        project, [flat, flat, Far(((256, 256), F32))],
        x_own, x_other, Far(w_a), attn_gain_row, qk_gain, cosine, sine,
    )
    (late_dy,) = after([cotangent], kv)
    (dy_own,) = call(relative_rows, [((128, 1024), BF)], Far(late_dy), scalars=(head_ref,))
    dy_other = swap(dy_own, "zl", 2, 1)
    kvs = [kv] + fan([kv] * 4, "y")
    (qh,) = after([qh], dy_other)
    send, keep, o, l = call(
        attend, halves + [Far(wide_flat)] * 2, qh, *kvs, own_places, places, Far(w_a)
    )
    h, hn = call(
        hidden, [Far(rows_high), rows_low], *sum_scatter(send, keep), x_own, ffn_gain_row
    )
    send, keep, hn_all, act, dgu = call(
        feed,
        [((4, 64, 1024), BF), ((4, 64, 1024), F32)]
        + [((256, 1024), BF), ((256, 640), BF), ((256, 1152), BF)],
        *gather_rows(hn, w_f), dy_own, dy_other, w_f,
    )
    pair = sum_pair(send, keep)
    pair = sum_pair(send, keep)
    act, dgu = after([act, dgu], *pair)
    d_hn = [pair[0]] + fan([None] + pair[1:], Z)
    (dw_f,) = call(
        feed_weights, [Far(((4, 4, 2, 32, 1792), BF))], hn_all, dy_own, dy_other, act, dgu,
        scalars=(y.reshape(1),),
    )
    dh, d_low, ffn_part, block = call(
        hidden_grad, [Far(rows_high), rows_low, Far(((1, 1024), F32)), Far(rows_low)],
        *d_hn, Far(h), dy_own, ffn_gain_row,
    )
    (dw_f,) = after([dw_f], d_low)
    dw_f = lax.psum_scatter(dw_f.reshape(1024, 1792), "x", scatter_dimension=0, tiled=True)
    d_attn, d_qh, *d_kvs = call(
        attend_grad, [Far(((256, 1024), BF)), wide_flat, wide_flat, flat, flat, flat],
        *gather_rows(d_low), Far(qh), *[Far(t) for t in kvs], own_places, places, Far(w_a), Far(o), Far(l),
    )
    d_qkv, send, keep, gains = call(
        project_grad, [((256, 256), BF)] + halves + [((8, 384), BF)],
        d_qh, d_kvs[0], *fan(d_kvs, "y"), Far(qkv), cosine, sine, qk_gain, Far(w_a),
        Far(x_own), Far(x_other), Far(ffn_part),
    )
    (dw_a,) = call(
        attend_weights, [((32, 40, 384), BF)],
        Far(x_own), Far(x_other), attn_gain_row, d_qkv, Far(d_attn), Far(o), gains,
    )
    own, *rest = sum_pair(send, keep)
    d_xn = [own] + fan([None] + rest, Z)
    (dw_a,) = after([dw_a], *d_xn)
    dw_a = lax.all_to_all(dw_a, PLANE, 0, 0, tiled=True)
    (rows,) = call(
        token_rows, [((64, 1024), BF)], *d_xn, Far(dh), x_own, attn_gain_row, Far(block)
    )
    tokens_grad, block_out = gather_head(rows, head)
    tokens_grad, block_out = tokens_grad[None], block_out[None]

    (dw_a,) = after([dw_a], tokens_grad)
    grad_wq, grad_wk, grad_wv, grad_wo, gains = call(
        finish_attend,
        [Far(((32, n), F32)) for n in (256, 128, 128, 256)] + [((8, 384), F32)],
        dw_a.reshape(2, 16, 40, 384),
    )
    (gains,) = call(add_two, [((8, 384), F32)], gains, swap(gains, "c", 2, 1))
    attn_sum, ffn_sum, query_sum, key_sum = call(
        finish_gains, [((8, 128), F32)] * 2 + [((1, 64), F32)] * 2,
        gains, swap(gains, "zh", 2, 1),
    )
    (dw_f,) = after([dw_f], rows)
    sides = call(split_sides, [((2, 32, 1792), BF)] * 4, Far(dw_f))
    others = after(fan(sides, "y"), gains)
    own_f, send_f = call(
        add_sides, [((32, 1792), F32), ((32, 1792), BF)], sides[0], *others,
        scalars=(zl_ref,),
    )
    grad_wg, grad_wu, grad_wd = call(
        finish_feed, [Far(((32, 1152), F32))] * 3, own_f, swap(send_f, "zl", 2, 1),
        scalars=(zl_ref,),
    )
    return (
        block_out, tokens_grad, attn_sum.reshape(1024), ffn_sum.reshape(1024),
        query_sum.reshape(64), key_sum.reshape(64),
        grad_wq, grad_wk, grad_wv, grad_wo, grad_wg, grad_wu, grad_wd,
    )


def solution(mesh):
    cube = Mesh(mesh.devices.reshape(2, 4, 4, 2, 2), AXES)
    rows = P("x", ("zl", "y"), None)
    weight = P(("zl", "y", "x"), ("zh", "c"))
    return jax.shard_map(
        local,
        mesh=cube,
        in_specs=(rows, P("x", None)) + (P(),) * 4 + (weight,) * 7 + (rows,),
        out_specs=(rows, rows) + (P(),) * 4 + (weight,) * 7,
        check_vma=False,
    )
```

```python
import functools

import jax
import jax.numpy as jnp
from jax import lax
from jax.experimental import pallas as pl
from jax.experimental.pallas import tpu as pltpu
from jax.sharding import Mesh, PartitionSpec as P

EPSILON = 1e-05
ROPE_BASE = 1000000.0
AXES = ("zl", "y", "x", "zh", "c")
Z = ("zl", "zh")
PLANE = ("zl", "y", "x")
BF = jnp.bfloat16
F32 = jnp.float32
SCALE = 64 ** (-0.5)
WHOLE = pl.BlockSpec(memory_space=pltpu.VMEM)


class Far:
    def __init__(self, value):
        self.value = value


def spec(item):
    return pl.BlockSpec() if isinstance(item, Far) else WHOLE


def bare(item):
    return item.value if isinstance(item, Far) else item


def call(body, outs, *operands, room=8, scalars=(), scratch=()):
    scalar = pl.BlockSpec(memory_space=pltpu.SMEM)
    return list(
        pl.pallas_call(
            body,
            out_shape=[jax.ShapeDtypeStruct(*bare(out)) for out in outs],
            in_specs=[scalar] * len(scalars) + [spec(item) for item in operands],
            out_specs=[spec(out) for out in outs],
            scratch_shapes=list(scratch),
            compiler_params=pltpu.CompilerParams(vmem_limit_bytes=room * 2**20 if room else None),
        )(*scalars, *[bare(item) for item in operands])
    )


def dot(left, right):
    return jnp.dot(left, right, preferred_element_type=F32)


def left_product(left, right):
    return lax.dot_general(left, right, (((0,), (0,)), ((), ())), preferred_element_type=F32)


def right_product(left, right):
    return lax.dot_general(left, right, (((1,), (1,)), ((), ())), preferred_element_type=F32)


def row_scale(values):
    return lax.rsqrt(jnp.mean(values * values, axis=-1, keepdims=True) + EPSILON)


def row_norm_grad(grad, normal, scale):
    return scale * (grad - normal * jnp.mean(grad * normal, axis=-1, keepdims=True))


def lanes(values):
    return lax.broadcasted_iota(jnp.int32, values.shape, 1)


def head_sum(values):
    low = lanes(values) < 64
    first = jnp.sum(jnp.where(low, values, 0.0), axis=-1, keepdims=True)
    second = jnp.sum(jnp.where(low, 0.0, values), axis=-1, keepdims=True)
    return jnp.where(low, first, second)


def head_scale(values):
    return lax.rsqrt(head_sum(values * values) * (1.0 / 64) + EPSILON)


def head_norm_grad(grad, normal, scale):
    return scale * (grad - normal * (head_sum(grad * normal) * (1.0 / 64)))


def other_half(values):
    low = (lanes(values) & 63) < 32
    return jnp.where(low, pltpu.roll(values, 96, 1), pltpu.roll(values, 32, 1))


def project(own, other, w, attn_gain, qk_gain, cosine, sine, qh, kv, qkv):
    x = jnp.concatenate([own[...], other[...]]).astype(F32)
    low = (x * row_scale(x) * attn_gain[...]).astype(BF)
    out = dot(low, w[:, :256])
    qkv[...] = out
    q, k = out[:, :128], out[:, 128:]
    cos, sin = cosine[...], sine[...]
    qn = q * head_scale(q) * qk_gain[0:1]
    qh[...] = (qn * cos + other_half(qn) * sin).astype(BF)
    kn = k * head_scale(k) * qk_gain[1:2]
    kr = kn * cos + other_half(kn) * sin
    kv[...] = jnp.where(lanes(k) < 64, kr, k).astype(BF)


def weights_of(q, k, visible):
    scores = right_product(q, k) * SCALE
    return jnp.where(visible, jnp.exp(scores), 0.0)


def attend(qh, kv0, kv1, kv2, kv3, own_places, places, w, send, keep, o_out, l_out):
    sums, totals = [0.0, 0.0], [0.0, 0.0]
    mine = own_places[...]
    for i, kv in enumerate((kv0, kv1, kv2, kv3)):
        visible = places[:, i * 256 : (i + 1) * 256] <= mine
        k, v = kv[:, :64], kv[:, 64:]
        for g in range(2):
            u = weights_of(qh[:, g * 64 : (g + 1) * 64], k, visible)
            totals[g] = totals[g] + jnp.sum(u, axis=-1, keepdims=True)
            sums[g] = sums[g] + dot(u.astype(BF), v)
    o = jnp.concatenate([sums[g] / totals[g] for g in range(2)], axis=1)
    o_out[...] = o
    l_out[...] = jnp.where(lanes(o) < 64, totals[0], totals[1])
    partial = right_product(o.astype(BF), w[:, 256:]).reshape(4, 2, 32, 1024)
    send[...] = partial[:, 1].astype(BF)
    keep[...] = partial[:, 0]


def pair_add(keep, got, own, one, two, three):
    own[...] = keep[0] + got[0].astype(F32)
    for k, out in ((1, one), (2, two), (3, three)):
        out[...] = (keep[k] + got[k].astype(F32)).astype(BF)


def total_of(own, one, two, three):
    return (own[...] + one[...].astype(F32)) + (two[...].astype(F32) + three[...].astype(F32))


def hidden(own, one, two, three, x, gain, h, hn):
    rows = x[:32].astype(F32) + total_of(own, one, two, three)
    h[...] = rows
    hn[...] = (rows * row_scale(rows) * gain[...]).astype(BF)


def feed_parts(gate, up, d_act):
    sig = jax.nn.sigmoid(gate)
    silu = gate * sig
    active = silu * up
    d_gate = d_act * up * sig * (1.0 + gate * (1.0 - sig))
    return active.astype(BF), d_gate, d_act * silu


def feed(
    p0, p1, p2, p3, p4, p5, p6, p7, dy_own, dy_other, w,
    send, keep, hn, act, dgu,
):
    rows = jnp.concatenate([p[...] for p in (p0, p1, p2, p3, p4, p5, p6, p7)])
    hn[...] = rows
    dy = jnp.concatenate([dy_own[...], dy_other[...]])
    def both(left, at, width):
        first, second = left[:, :512], left[:, 512:]
        return dot(first, w[:, 0, :, at : at + width].reshape(512, width)) + dot(
            second, w[:, 1, :, at : at + width].reshape(512, width)
        )
    gate, up, d_act = both(rows, 0, 512), both(rows, 512, 512), both(dy, 1024, 512)
    active, d_gate, d_up = feed_parts(gate, up, d_act)
    act[:, :512] = active
    d_gate, d_up = d_gate.astype(BF), d_up.astype(BF)
    dgu[:, :512] = d_gate
    dgu[:, 512:1024] = d_up
    tail, d_tail = both(rows, 1536, 128), both(dy, 1664, 128)
    low = lanes(tail) < 64
    gate = jnp.where(low, tail, 0.0)
    up = jnp.where(low, pltpu.roll(tail, 64, 1), 0.0)
    active, dg_tail, du_tail = feed_parts(gate, up, d_tail)
    act[:, 512:] = active
    dgu_tail = jnp.where(low, dg_tail, pltpu.roll(du_tail, 64, 1)).astype(BF)
    dgu[:, 1024:] = dgu_tail
    halves = []
    for z in range(2):
        part = right_product(d_gate, w[:, z, :, :512].reshape(512, 512))
        part = part + right_product(d_up, w[:, z, :, 512:1024].reshape(512, 512))
        part = part + right_product(dgu_tail, w[:, z, :, 1536:1664].reshape(512, 128))
        halves.append(part)
    partial = jnp.concatenate(halves, axis=1).reshape(4, 2, 32, 1024)
    send[:, :32] = partial[:, 1].astype(BF)
    keep[:, :32] = partial[:, 0]
    low_act = act[...]
    halves = []
    for z in range(2):
        part = right_product(low_act[:, :512], w[:, z, :, 1024:1536].reshape(512, 512))
        halves.append(part + right_product(low_act[:, 512:], w[:, z, :, 1664:].reshape(512, 128)))
    partial = jnp.concatenate(halves, axis=1).reshape(4, 2, 32, 1024)
    send[:, 32:] = partial[:, 1].astype(BF)
    keep[:, 32:] = partial[:, 0]


def feed_weights(y, hn, dy_own, dy_other, act, dgu, dw):
    dy = jnp.concatenate([dy_own[...], dy_other[...]])
    rows, active = hn[...], act[...]
    def put(left, right, at, width):
        for z in range(2):
            value = left_product(left[:, z * 512 : (z + 1) * 512], right)
            blocks = value.astype(BF).reshape(4, 4, 32, width)
            for i in range(4):
                dw[:, i ^ y[0], z, :, at : at + width] = blocks[i]
    put(rows, dgu[:, :512], 0, 512)
    put(rows, dgu[:, 512:1024], 512, 512)
    put(dy, active[:, :512], 1024, 512)
    put(rows, dgu[:, 1024:], 1536, 128)
    put(dy, active[:, 512:], 1664, 128)


def split_sides(dw, own, one, two, three):
    for k, piece in enumerate((own, one, two, three)):
        piece[...] = dw[k * 64 : (k + 1) * 64].reshape(2, 32, 1792)


def add_sides(zl, own, one, two, three, mine, send):
    def total(z):
        first = own[z].astype(F32) + one[z].astype(F32)
        return first + (two[z].astype(F32) + three[z].astype(F32))
    mine[...] = total(zl[0])
    send[...] = total(1 - zl[0]).astype(BF)


def hidden_grad(own, one, two, three, h, dy, gain, dh, low, gain_part, block):
    total = total_of(own, one, two, three)
    d_hn, branch = total[:32], total[32:]
    rows = h[...]
    block[...] = (rows + branch).astype(BF)
    scale = row_scale(rows)
    hat = rows * scale
    gain_part[...] = jnp.sum(d_hn * hat, axis=0, keepdims=True)
    grad = dy[:32].astype(F32) + row_norm_grad(d_hn * gain[...], hat, scale)
    dh[...] = grad
    low[...] = grad.astype(BF)


def attend_grad(
    p0, p1, p2, p3, p4, p5, p6, p7, qh, kv0, kv1, kv2, kv3, own_places, places, w, o, l,
    d_attn, d_qh, d_kv0, d_kv1, d_kv2, d_kv3,
):
    rows = jnp.concatenate([p[...] for p in (p0, p1, p2, p3, p4, p5, p6, p7)])
    d_attn[...] = rows
    d_o = dot(rows, w[:, 256:])
    denom = l[...]
    d_inner = (d_o / denom).astype(BF)
    delta = head_sum(d_o * o[...]) / denom
    mine = own_places[...]
    d_q = [0.0, 0.0]
    for i, (kv, d_kv) in enumerate(((kv0, d_kv0), (kv1, d_kv1), (kv2, d_kv2), (kv3, d_kv3))):
        visible = places[:, i * 256 : (i + 1) * 256] <= mine
        k, v = kv[:, :64], kv[:, 64:]
        d_k, d_v = 0.0, 0.0
        for g in range(2):
            at = slice(g * 64, (g + 1) * 64)
            q, di = qh[:, at], d_inner[:, at]
            u = weights_of(q, k, visible)
            ds = (u * (right_product(di, v) - delta[:, g * 64 : g * 64 + 1])).astype(BF)
            d_q[g] = d_q[g] + dot(ds, k)
            d_k = d_k + left_product(ds, q)
            d_v = d_v + left_product(u.astype(BF), di)
        d_kv[...] = jnp.concatenate([d_k * SCALE, d_v], axis=1).astype(d_kv.dtype)
    d_qh[...] = jnp.concatenate(d_q, axis=1) * SCALE


def project_grad(
    d_qh, own, one, two, three, qkv, cosine, sine, qk_gain, w, x_own, x_other, ffn_part,
    d_qkv, send, keep, gains,
):
    d_kv = total_of(own, one, two, three)
    cos, sin = cosine[...], sine[...]
    q, k = qkv[:, :128], qkv[:, 128:]
    q_scale, k_scale = head_scale(q), head_scale(k)
    q_hat, k_hat = q * q_scale, k * k_scale
    d_q = d_qh[...]
    d_qn = d_q * cos - other_half(d_q) * sin
    d_kn = d_kv * cos - other_half(d_kv) * sin
    heads = jnp.concatenate(
        [jnp.sum(d_qn * q_hat, axis=0, keepdims=True), jnp.sum(d_kn * k_hat, axis=0, keepdims=True)]
    )
    d_q = head_norm_grad(d_qn * qk_gain[0:1], q_hat, q_scale)
    d_k = head_norm_grad(d_kn * qk_gain[1:2], k_hat, k_scale)
    d_k = jnp.where(lanes(d_k) < 64, d_k, d_kv)
    low = jnp.concatenate([d_q, d_k], axis=1).astype(BF)
    d_qkv[...] = low
    partial = right_product(low, w[:, :256])
    x = jnp.concatenate([x_own[...], x_other[...]]).astype(F32)
    attn_part = jnp.sum(partial * (x * row_scale(x)), axis=0, keepdims=True)
    def fold(part):
        return jnp.concatenate([part[:, i * 128 : (i + 1) * 128] for i in range(8)])
    heads = jnp.concatenate([heads, jnp.zeros((6, 128), F32)])
    gains[...] = jnp.concatenate([fold(attn_part), fold(ffn_part), heads], axis=1)
    partial = partial.reshape(4, 2, 32, 1024)
    send[...] = partial[:, 1].astype(BF)
    keep[...] = partial[:, 0]


def attend_weights(x_own, x_other, attn_gain, d_qkv, d_attn, o, gains, dw):
    x = jnp.concatenate([x_own[...], x_other[...]]).astype(F32)
    normed = (x * row_scale(x) * attn_gain[...]).astype(BF)
    first = left_product(normed, d_qkv[...]).astype(BF)
    second = left_product(d_attn[...], o[...].astype(BF)).astype(BF)
    dw[:, :32, :256] = first.reshape(32, 32, 256)
    dw[:, :32, 256:] = second.reshape(32, 32, 128)
    dw[:, 32:] = jnp.broadcast_to(gains[...].astype(BF)[None], (32, 8, 384))


def token_rows(own, one, two, three, dh, x, gain, block, out):
    d_xn = total_of(own, one, two, three)
    rows = x[:32].astype(F32)
    scale = row_scale(rows)
    grad = row_norm_grad(d_xn * gain[...], rows * scale, scale)
    out[:32] = (dh[...] + grad).astype(BF)
    out[32:] = block[...]


def finish_attend(parts, wq, wk, wv, wo, attn, ffn, query, key):
    sums = [jnp.sum(parts[z].astype(F32), axis=0) for z in range(2)]
    gains = sums[0][32:] + sums[1][32:]
    attn[...] = gains[:, :128]
    ffn[...] = gains[:, 128:256]
    query[...] = gains[0:1, 256:320] + gains[0:1, 320:384]
    key[...] = gains[1:2, 256:320]
    low, high = sums[0][:32], sums[1][:32]
    wq[...] = jnp.concatenate([low[:, :128], high[:, :128]], axis=1)
    wk[...] = jnp.concatenate([low[:, 128:192], high[:, 128:192]], axis=1)
    wv[...] = jnp.concatenate([low[:, 192:256], high[:, 192:256]], axis=1)
    wo[...] = jnp.concatenate([low[:, 256:], high[:, 256:]], axis=1)


def finish_feed(zl, own, got, wg, wu, wd):
    mine, its = own[...], got[...].astype(F32)
    first = zl[0] == 0
    low, high = jnp.where(first, mine, its), jnp.where(first, its, mine)
    for i, out in enumerate((wg, wu, wd)):
        wide, tail = slice(i * 512, (i + 1) * 512), slice(1536 + i * 64, 1600 + i * 64)
        out[...] = jnp.concatenate(
            [low[:, wide], low[:, tail], high[:, wide], high[:, tail]], axis=1
        )


def add_two(own, one, out):
    out[...] = own[...] + one[...]


def prepare(zl, head, wq, wk, wv, wo, wg, wu, wd, tokens, blocks, send_f, keep_f, x_own):
    for z in range(2):
        at = 0
        for w in (wq, wk, wv, wo):
            width = w.shape[1] // 2
            part = w[:, z * width : (z + 1) * width]
            blocks[z, :, :, at : at + width] = jnp.broadcast_to(part[None], (16, 32, width))
            at += width
    pad = jnp.zeros((32, 64), BF)
    sides = []
    for z in range(2):
        parts = [w[:, z * 576 : (z + 1) * 576] for w in (wg, wu, wd)]
        sides.append(
            jnp.concatenate([p[:, :512] for p in parts] + [p[:, 512:] for p in parts] + [pad], axis=1)
        )
    first = zl[0] == 0
    keep_f[...] = jnp.where(first, sides[0], sides[1])
    send_f[...] = jnp.where(first, sides[1], sides[0])
    relative_rows(head, tokens, x_own)


def relative_rows(head, rows, out):
    for k in range(4):
        out[k * 32 : (k + 1) * 32] = rows[0, pl.ds((head[0] ^ k) * 32, 32)]


def order_rows(zl, own, got, out):
    out[zl[0]] = own[...]
    out[1 - zl[0]] = got[...]


def swap(value, axes, size, mask):
    return lax.ppermute(value, axes, [(i, i ^ mask) for i in range(size)])


def fan(pieces, axes):
    return [swap(pieces[k], axes, 4, k) for k in (1, 2, 3)]


def sum_pair(send, keep):
    got = swap(send, "c", 2, 1)
    shape = send.shape[1:]
    return call(pair_add, [(shape, F32)] + [(shape, BF)] * 3, keep, got)


def sum_scatter(send, keep):
    own, *rest = sum_pair(send, keep)
    return [own] + fan([None] + rest, Z)


def gather_rows(rows, *first):
    column = [rows] + after(fan([rows] * 4, Z), *first)
    pieces = []
    for piece in column:
        pieces += [piece, swap(piece, "c", 2, 1)]
    return pieces


def place_rows(head, p0, p1, p2, p3, tokens_grad, block_out):
    for k, piece in enumerate((p0, p1, p2, p3)):
        at = pl.ds((head[0] ^ k) * 32, 32)
        tokens_grad[at] = piece[:32]
        block_out[at] = piece[32:]


def gather_head(rows, head):
    other = swap(rows, "c", 2, 1)
    pieces = [rows, other, swap(rows, "zh", 2, 1), swap(other, "zh", 2, 1)]
    return call(place_rows, [Far(((128, 1024), BF))] * 2, *pieces, scalars=(head.reshape(1),))


def after(values, *first):
    out = lax.optimization_barrier(tuple(values) + tuple(first))
    return list(out[: len(values)])


def local(
    tokens, positions, attn_gain, ffn_gain, query_gain, key_gain,
    w_query, w_key, w_value, w_out, w_gate, w_up, w_down, cotangent,
):
    zl, y, head = lax.axis_index("zl"), lax.axis_index("y"), lax.axis_index(("zh", "c"))
    attn_gain_row, ffn_gain_row = attn_gain[None], ffn_gain[None]

    zl_ref, head_ref = zl.reshape(1), head.reshape(1)
    blocks, send_f, keep_f, x_own = call(
        prepare,
        [((2, 16, 32, 384), BF), ((32, 1792), BF), ((32, 1792), BF), ((128, 1024), BF)],
        *[Far(w) for w in (w_query, w_key, w_value, w_out, w_gate, w_up, w_down, tokens)],
        scalars=(zl_ref, head_ref), room=None,
    )
    got_f = swap(send_f, "zl", 2, 1)
    x_other = swap(x_own, "zl", 2, 1)
    w_a = lax.all_to_all(blocks.reshape(1024, 384), PLANE, 0, 0, tiled=True)
    (rows_f,) = call(order_rows, [Far(((2, 32, 1792), BF))], keep_f, got_f, scalars=(zl_ref,))
    w_f = lax.all_gather(rows_f, ("y", "x"), axis=0)

    (late_positions,) = after([positions], blocks)
    steps = jnp.array([dl * 16 + ky * 4 + d for ky in range(4) for dl in range(2) for d in range(4)])
    places = late_positions[0].reshape(32, 32)[steps ^ (zl * 16 + y * 4 + head)].reshape(1024)
    own_places = places[:256]
    frequency = ROPE_BASE ** (-(jnp.arange(32).astype(F32) * 2.0 / 64))
    angles = own_places.astype(F32)[:, None] * frequency
    cosine, sine = jnp.cos(angles), jnp.sin(angles)
    cosine = jnp.concatenate([cosine] * 4, axis=1)
    sine = jnp.concatenate([-sine, sine] * 2, axis=1)
    own_places, places = own_places[:, None], places[None]
    qk_gain = jnp.stack([jnp.tile(query_gain, 2), jnp.tile(key_gain, 2)])

    halves = [((4, 32, 1024), BF), ((4, 32, 1024), F32)]
    flat, wide_flat = ((256, 128), BF), ((256, 128), F32)
    rows_low, rows_high = ((32, 1024), BF), ((32, 1024), F32)
    qh, kv, qkv = call(
        project, [flat, flat, Far(((256, 256), F32))],
        x_own, x_other, Far(w_a), attn_gain_row, qk_gain, cosine, sine,
    )
    (late_dy,) = after([cotangent], kv)
    (dy_own,) = call(relative_rows, [((128, 1024), BF)], Far(late_dy), scalars=(head_ref,))
    dy_other = swap(dy_own, "zl", 2, 1)
    kvs = [kv] + fan([kv] * 4, "y")
    (qh,) = after([qh], dy_other)
    send, keep, o, l = call(
        attend, halves + [Far(wide_flat)] * 2, qh, *kvs, own_places, places, Far(w_a)
    )
    h, hn = call(
        hidden, [Far(rows_high), rows_low], *sum_scatter(send, keep), x_own, ffn_gain_row
    )
    send, keep, hn_all, act, dgu = call(
        feed,
        [((4, 64, 1024), BF), ((4, 64, 1024), F32)]
        + [((256, 1024), BF), ((256, 640), BF), ((256, 1152), BF)],
        *gather_rows(hn, w_f), dy_own, dy_other, w_f,
    )
    pair = sum_pair(send, keep)
    pair = sum_pair(send, keep)
    act, dgu = after([act, dgu], *pair)
    d_hn = [pair[0]] + fan([None] + pair[1:], Z)
    (dw_f,) = call(
        feed_weights, [Far(((4, 4, 2, 32, 1792), BF))], hn_all, dy_own, dy_other, act, dgu,
        scalars=(y.reshape(1),),
    )
    dh, d_low, ffn_part, block = call(
        hidden_grad, [Far(rows_high), rows_low, Far(((1, 1024), F32)), Far(rows_low)],
        *d_hn, Far(h), dy_own, ffn_gain_row,
    )
    (dw_f,) = after([dw_f], d_low)
    dw_f = lax.psum_scatter(dw_f.reshape(1024, 1792), "x", scatter_dimension=0, tiled=True)
    d_attn, d_qh, *d_kvs = call(
        attend_grad, [Far(((256, 1024), BF)), wide_flat, wide_flat, flat, flat, flat],
        *gather_rows(d_low), Far(qh), *[Far(t) for t in kvs], own_places, places, Far(w_a), Far(o), Far(l),
    )
    d_qkv, send, keep, gains = call(
        project_grad, [((256, 256), BF)] + halves + [((8, 384), F32)],
        d_qh, d_kvs[0], *fan(d_kvs, "y"), Far(qkv), cosine, sine, qk_gain, Far(w_a),
        Far(x_own), Far(x_other), Far(ffn_part),
    )
    for axis in ("c", "zh"):
        (gains,) = call(add_two, [((8, 384), F32)], gains, swap(gains, axis, 2, 1))
    (dw_a,) = call(
        attend_weights, [((32, 40, 384), BF)],
        Far(x_own), Far(x_other), attn_gain_row, d_qkv, Far(d_attn), Far(o), gains,
    )
    own, *rest = sum_pair(send, keep)
    d_xn = [own] + fan([None] + rest, Z)
    (dw_a,) = after([dw_a], *d_xn)
    dw_a = lax.all_to_all(dw_a, PLANE, 0, 0, tiled=True)
    (rows,) = call(
        token_rows, [((64, 1024), BF)], *d_xn, Far(dh), x_own, attn_gain_row, Far(block)
    )
    tokens_grad, block_out = gather_head(rows, head)
    tokens_grad, block_out = tokens_grad[None], block_out[None]

    (dw_a,) = after([dw_a], tokens_grad)
    grad_wq, grad_wk, grad_wv, grad_wo, attn_sum, ffn_sum, query_sum, key_sum = call(
        finish_attend,
        [Far(((32, n), F32)) for n in (256, 128, 128, 256)]
        + [((8, 128), F32)] * 2 + [((1, 64), F32)] * 2,
        dw_a.reshape(2, 16, 40, 384),
    )
    (dw_f,) = after([dw_f], rows)
    sides = call(split_sides, [((2, 32, 1792), BF)] * 4, Far(dw_f))
    others = after(fan(sides, "y"), attn_sum)
    own_f, send_f = call(
        add_sides, [((32, 1792), F32), ((32, 1792), BF)], sides[0], *others,
        scalars=(zl_ref,),
    )
    grad_wg, grad_wu, grad_wd = call(
        finish_feed, [Far(((32, 1152), F32))] * 3, own_f, swap(send_f, "zl", 2, 1),
        scalars=(zl_ref,),
    )
    return (
        block_out, tokens_grad, attn_sum.reshape(1024), ffn_sum.reshape(1024),
        query_sum.reshape(64), key_sum.reshape(64),
        grad_wq, grad_wk, grad_wv, grad_wo, grad_wg, grad_wu, grad_wd,
    )


def solution(mesh):
    cube = Mesh(mesh.devices.reshape(2, 4, 4, 2, 2), AXES)
    rows = P("x", ("zl", "y"), None)
    weight = P(("zl", "y", "x"), ("zh", "c"))
    return jax.shard_map(
        local,
        mesh=cube,
        in_specs=(rows, P("x", None)) + (P(),) * 4 + (weight,) * 7 + (rows,),
        out_specs=(rows, rows) + (P(),) * 4 + (weight,) * 7,
        check_vma=False,
    )
```
